256 devices in a mesh: wide: 16 (over x, y), narrow: 16 (over z, core).
Axes of the slice: x: 4, y: 4, z: 8, core: 2. Of those that a mesh axis runs over, the one named last changes fastest.
Arguments:
- amplitudes: bfloat16 [4096, 32768], P('narrow', 'wide'), may hold values from -12 to 12
- integrals: bfloat16 [32768, 4096], P('wide'), may hold values from -0.046875 to 0.046875
- pair_integrals: bfloat16 [4096, 4096], P('narrow'), may hold values from -0.09375 to 0.09375
- slab_index: int32 [4096], replicated, may hold values from 0 to 32767, as said below
- occupied_energy: float32 [4096], P('narrow'), may hold values from -3 to -0.5
- virtual_energy: float32 [4096], P('wide'), may hold values from 1.5 to 6
Outputs:
- updated: float32 [4096, 4096], P('narrow', 'wide')
The draws below stay inside these ranges and needn't reach their ends.
Inputs may be any that keep to these rules, and one draw needn't show every extreme that they name: `slab_index`: distinct indices of cd pairs; at most 512 of them lie in any one aligned block of 2048 cd pairs, and one such block holds exactly that many.
All inputs are finite; a program needn't handle non-finite values.
Results may differ from the reference program's by a relative error of at most 0.0003.
Values may be sent and summed in bfloat16 or wider, within the bound.
No kernel may reach another device: no remote copies, remote signals or barrier semaphores. Data moves between devices by JAX's collectives and lax.ppermute only.
A program may use at most 128 MiB of HBM per device.

```python
import math
import jax
import jax.numpy as jnp
from jax import lax

CD_DEV = 2048
AB_DEV = 256
OP = 4096
CD = 32768
AB = 4096


def draw_slab_index(key, part):
    key = jax.random.fold_in(key, 11)
    shards = CD // CD_DEV
    key_heavy, key_perm, key_shuffle = jax.random.split(key, 3)
    heavy = jax.random.randint(key_heavy, (), 0, shards)
    order = jnp.arange(AB, dtype=jnp.int32)
    rest = order - 2 * AB_DEV
    others = jnp.maximum(rest, 0) % (shards - 1)
    others = others + (others >= heavy).astype(jnp.int32)
    owners = jnp.where(order < 2 * AB_DEV, heavy, others)
    ranking = jnp.where(order < 2 * AB_DEV, order, jnp.maximum(rest, 0) // (shards - 1))
    perm_keys = jax.random.split(key_perm, shards)
    tables = jax.vmap(lambda single: jax.random.permutation(single, CD_DEV))(perm_keys)
    offsets = tables[owners, ranking]
    values = owners * CD_DEV + offsets
    shuffle = jax.random.permutation(key_shuffle, AB)
    return values[shuffle].astype(jnp.int32)


def with_spikes(values, rng, source, target, blocks, factor):
    owner, partner = [(jnp.arange(values.shape[dim]) // (values.shape[dim] // blocks)).reshape([-1 if axis == dim else 1 for axis in range(values.ndim)]) for dim in (source, target)]
    chosen = jax.random.permutation(rng, blocks)[partner]
    strong = (owner == chosen) | (owner == (partner + blocks // 2) % blocks)
    return jnp.where(strong, factor * values, values)


def block_scale(rng, extent, cuts, smallest, high):
    def one(dim, shards_of):
        heights = jax.random.uniform(jax.random.fold_in(jax.random.fold_in(rng, 6), dim), (shards_of,), jnp.float32, smallest / len(cuts), high / len(cuts))
        return jnp.repeat(jnp.exp(heights), extent[dim] // shards_of).reshape((-1,) + (1,) * (len(extent) - dim - 1))

    loudness = one(*cuts[0])
    for cut in cuts[1:]:
        loudness = loudness * one(*cut)
    return loudness


def scatter_about(own_key, shape, spread, limit, cuts=(), kind=jnp.bfloat16):
    array = jax.random.normal(own_key, shape, jnp.float32) * spread
    if len(cuts) > 0:
        array = block_scale(own_key, shape, cuts, -0.22, 0.18) * array
    return jnp.clip(array, min=-limit, max=limit).astype(kind)


def heavy_noise(key, dims, spread, limit, cuts, heavy, kind=jnp.bfloat16):
    entries = spread * jax.random.normal(key, dims, jnp.float32)
    if cuts:
        entries = entries * block_scale(key, dims, cuts, -0.22, 0.18)
    return jnp.clip(with_spikes(entries, jax.random.fold_in(key, 3), *heavy), -limit, limit).astype(kind)


def setup_inputs(seed: int = 0) -> dict:
    keys = jax.random.split(jax.random.key(seed), 7)
    amplitudes = scatter_about(keys[0], (OP, CD), 2.0, 12.0, ((0, 16), (1, 16)))
    integrals = heavy_noise(keys[1], (CD, AB), CD ** -0.5, 0.046875, ((0, 16),), (0, 1, 16, 2.0))
    pair_integrals = scatter_about(keys[2], (OP, OP), OP ** -0.5, 0.09375, ((0, 16),))
    slab_index = draw_slab_index(jax.random.fold_in(keys[6], 71), 0)
    occupied_energy = jnp.clip(-3.0 + 2.5 * jax.random.uniform(keys[4], (OP,), jnp.float32) ** block_scale(keys[4], (OP,), ((0, 16),), -0.2, 0.2), -3.0, -0.5)
    virtual_energy = jnp.clip(1.5 + 4.5 * jax.random.uniform(keys[5], (AB,), jnp.float32) ** block_scale(keys[5], (AB,), ((0, 16),), -0.2, 0.2), 1.5, 6.0)
    return {"amplitudes": amplitudes, "integrals": integrals, "pair_integrals": pair_integrals, "slab_index": slab_index, "occupied_energy": occupied_energy, "virtual_energy": virtual_energy}


def reference(amplitudes, integrals, pair_integrals, slab_index, occupied_energy, virtual_energy):
    height = math.gcd(OP, 512)
    pieces = amplitudes.reshape(OP // height, height, CD)

    def product(rowset):
        return jnp.dot(rowset, integrals, preferred_element_type=jnp.float32)

    ladder = lax.map(product, pieces).reshape(OP, AB)
    selected = jnp.take(amplitudes, slab_index.astype(jnp.int32), axis=1)
    hole_term = jnp.dot(pair_integrals, selected, preferred_element_type=jnp.float32)
    denominator = virtual_energy[None, :] - occupied_energy[:, None]
    return (ladder + hole_term) / denominator
```

```python
import jax
import jax.numpy as jnp
from jax import lax
from jax.experimental import pallas as pl
from jax.experimental.pallas import tpu as pltpu
from jax.sharding import PartitionSpec as P

CHUNKS = 16
DEPTH = 32
LANES = 256
CODE_ROWS = 16
STEPS = 256.0
TOP = 32760.0
VMEM = pl.BlockSpec(memory_space=pltpu.VMEM)
SMEM = pl.BlockSpec(memory_space=pltpu.SMEM)


def iota(shape, dim):
    return lax.broadcasted_iota(jnp.int32, shape, dim)


def ones_where(mask):
    return jnp.where(mask, 1.0, 0.0)


def bdot(left, right, dims=((1,), (0,))):
    return lax.dot_general(
        left.astype(jnp.bfloat16),
        right.astype(jnp.bfloat16),
        (dims, ((), ())),
        preferred_element_type=jnp.float32,
    )


def count_before(classes):
    member = jnp.concatenate(
        [ones_where(classes[c : c + 1, :] == iota((CHUNKS, LANES), 0)) for c in range(CHUNKS)], 0
    )
    earlier = ones_where(iota((LANES, LANES), 0) < iota((LANES, LANES), 1))
    return member, bdot(member, earlier)


def pick(member, table):
    return jnp.sum((member * table).reshape(CHUNKS, CHUNKS, LANES), axis=1).astype(jnp.int32)


def select_kernel(shift, here_ref, index_ref, amp_ref, sent_ref, rank_ref):
    index = index_ref[...]
    here = here_ref[0]
    owner = jnp.right_shift(index, shift)
    member, within = count_before(owner)
    r, c = iota((LANES, LANES), 0), iota((LANES, LANES), 1)
    ahead = ones_where(((r & 15) == (c & 15)) & (jnp.right_shift(c, 4) < jnp.right_shift(r, 4)))
    base = jnp.sum(bdot(ahead, member), axis=1, keepdims=True)
    rank = pick(member, within + base)
    rank_ref[...] = rank
    middle, depth = rank & 15, jnp.right_shift(rank, 4)
    column = index & ((1 << shift) - 1)
    high, low = jnp.right_shift(column, 6).astype(jnp.float32), (column & 63).astype(jnp.float32)
    lefts, rights = [], []
    for k in range(CHUNKS):
        one = slice(k, k + 1)
        hit = ones_where((depth[one] == iota((DEPTH, LANES), 0)) & (owner[one] == here))
        lefts.append(jnp.concatenate([hit * high[one], hit * low[one]], 0))
        rights.append(ones_where(middle[one] == iota((CHUNKS, LANES), 0)))
    found = bdot(jnp.concatenate(lefts, 1), jnp.concatenate(rights, 1), ((1,), (1,)))
    columns = (found[:DEPTH] * 64.0 + found[DEPTH:]).astype(jnp.int32)
    span = amp_ref.shape[1]
    lane = iota((DEPTH, span), 1)
    for k in range(0, CHUNKS, 4):
        chosen = jnp.concatenate(
            [
                ones_where(lane == columns[:, j : j + 1]).astype(jnp.bfloat16)
                for j in range(k, k + 4)
            ],
            0,
        )
        got = bdot(chosen, amp_ref[...], ((1,), (1,))).astype(jnp.bfloat16)
        sent_ref[k : k + 4] = got.reshape(4, DEPTH, got.shape[1])


def route_kernel(shift, here_ref, index_ref, rank_ref, forward_ref, settle_ref):
    index, rank, here = index_ref[...], rank_ref[...], here_ref[0]
    owner = jnp.right_shift(index, shift)
    middle, depth = rank & 15, jnp.right_shift(rank, 4)
    member, within = count_before(middle)
    place = pick(member, within)
    source = (owner * DEPTH + depth).astype(jnp.float32)
    lane = iota((DEPTH, CHUNKS * DEPTH), 1)
    for k in range(CHUNKS):
        one = slice(k, k + 1)
        hit = (place[one] == iota((DEPTH, LANES), 0)) & (middle[one] == here)
        row = jnp.sum(jnp.where(hit, source[one], 0.0), axis=1, keepdims=True).astype(jnp.int32)
        forward_ref[k * DEPTH : (k + 1) * DEPTH, :] = ones_where(lane == row).astype(jnp.bfloat16)
    arrived = (middle * DEPTH + place).astype(jnp.float32)
    own = iota((CHUNKS, LANES), 0) == here
    wanted = jnp.sum(jnp.where(own, arrived, 0.0), axis=0, keepdims=True).astype(jnp.int32)
    settle_ref[...] = ones_where(iota((CHUNKS * DEPTH, LANES), 0) == wanted).astype(jnp.bfloat16)


def ladder_kernel(amp_ref, int_ref, coded_ref):
    height = amp_ref.shape[0]
    for k in range(coded_ref.shape[0]):
        part = jnp.dot(
            amp_ref[...],
            int_ref[:, k * LANES : (k + 1) * LANES],
            preferred_element_type=jnp.float32,
        )
        largest = jnp.max(jnp.abs(part), axis=0, keepdims=True)
        code = jnp.ceil(jnp.log2(jnp.maximum(largest, 2.0**-120)) * STEPS) + 1.0
        shrunk = part * jnp.exp2(code * (-1.0 / STEPS)) * TOP
        coded_ref[k, :height, :] = jnp.round(shrunk).astype(jnp.int32).astype(jnp.int16)
        coded_ref[k, height:, :] = jnp.broadcast_to(
            code.astype(jnp.int32), (CODE_ROWS, LANES)
        ).astype(jnp.int16)


def decode_kernel(coded_ref, sum_ref):
    height = sum_ref.shape[0]
    total = jnp.zeros(sum_ref.shape, jnp.float32)
    for k in range(CHUNKS):
        code = coded_ref[k, height:, :].astype(jnp.int32).astype(jnp.float32)[:1, :]
        values = coded_ref[k, :height, :].astype(jnp.int32).astype(jnp.float32)
        total = total + values * jnp.exp2(code * (1.0 / STEPS))
    sum_ref[...] = total * (1.0 / TOP)


def finish_kernel(place_ref, pair_ref, ladder_ref, occ_ref, virt_ref, own_ref, far_ref, sib_ref, sibfar_ref, out_ref):
    z, core = place_ref[0], place_ref[1]
    rows = out_ref.shape[0]
    half = rows // 2
    total = ladder_ref[...]

    def add(total, away, which, start, block):
        n = jnp.bitwise_and(z - away + 8, 7) * 2 + which
        columns = pl.ds(pl.multiple_of(n * rows + start, 128), block.shape[0])
        return total + jnp.dot(pair_ref[:, columns], block, preferred_element_type=jnp.float32)

    for near, far, which in ((own_ref, far_ref, core), (sib_ref, sibfar_ref, 1 - core)):
        for k, away in enumerate((0, 1, -1, 2, -2)):
            total = add(total, away, which, 0, near[k * rows : (k + 1) * rows])
        total = add(total, 3, which, 0, far[:rows])
        total = add(total, -3, which, 0, far[rows : 2 * rows])
        total = add(total, 4, which, 0, far[2 * rows : 2 * rows + half])
        total = add(total, 4, which, half, far[2 * rows + half :])
    out_ref[...] = total / (virt_ref[...] - occ_ref[...])


def on_device(amplitudes, integrals, pair_integrals, slab_index, occupied_energy, virtual_energy):
    wide_index = lax.axis_index("wide")
    narrow_index = lax.axis_index("narrow")
    height, span = amplitudes.shape
    shift = span.bit_length() - 1
    here = wide_index.astype(jnp.int32).reshape(1)
    index = slab_index.reshape(CHUNKS, LANES)
    half = height // 2

    def step(value, dz, dc=0):
        ring = [
            (z * 2 + c, (z + dz) % 8 * 2 + (c + dc) % 2) for z in range(8) for c in range(2)
        ]
        return lax.ppermute(value, "narrow", ring)

    sent, rank = pl.pallas_call(
        lambda *refs: select_kernel(shift, *refs),
        out_shape=(
            jax.ShapeDtypeStruct((CHUNKS, DEPTH, height), jnp.bfloat16),
            jax.ShapeDtypeStruct((CHUNKS, LANES), jnp.int32),
        ),
        in_specs=[SMEM, VMEM, VMEM],
        out_specs=(VMEM, VMEM),
        compiler_params=pltpu.CompilerParams(vmem_limit_bytes=24 << 20),
        cost_estimate=pl.CostEstimate(flops=2**30, bytes_accessed=2**21, transcendentals=0),
        name="select",
    )(here, index, amplitudes)
    first = lax.all_to_all(sent, "wide", 0, 0, tiled=True)

    forward, settle = pl.pallas_call(
        lambda *refs: route_kernel(shift, *refs),
        out_shape=(
            jax.ShapeDtypeStruct((CHUNKS * DEPTH, CHUNKS * DEPTH), jnp.bfloat16),
            jax.ShapeDtypeStruct((CHUNKS * DEPTH, LANES), jnp.bfloat16),
        ),
        in_specs=[SMEM, VMEM, VMEM],
        out_specs=(VMEM, VMEM),
        compiler_params=pltpu.CompilerParams(vmem_limit_bytes=16 << 20),
        cost_estimate=pl.CostEstimate(flops=2**28, bytes_accessed=2**20, transcendentals=0),
        name="route",
    )(here, index, rank)

    per = 2
    coded = pl.pallas_call(
        ladder_kernel,
        grid=(CHUNKS // per,),
        out_shape=jax.ShapeDtypeStruct((CHUNKS, height + CODE_ROWS, LANES), jnp.int16),
        in_specs=[
            pl.BlockSpec((height, span), lambda i: (0, 0)),
            pl.BlockSpec((span, per * LANES), lambda i: (0, i)),
        ],
        out_specs=pl.BlockSpec((per, height + CODE_ROWS, LANES), lambda i: (i, 0, 0)),
        compiler_params=pltpu.CompilerParams(vmem_limit_bytes=24 << 20),
        cost_estimate=pl.CostEstimate(
            flops=2 * height * span * CHUNKS * LANES, bytes_accessed=20 * 2**20, transcendentals=0
        ),
        name="ladder",
    )(amplitudes, integrals)
    shares = lax.all_to_all(coded, "wide", 0, 0, tiled=True)

    moved = bdot(forward, first.reshape(CHUNKS * DEPTH, height)).astype(jnp.bfloat16)
    second = lax.all_to_all(moved.reshape(CHUNKS, DEPTH, height), "wide", 0, 0, tiled=True)
    own = bdot(second.reshape(CHUNKS * DEPTH, height), settle, ((0,), (0,))).astype(jnp.bfloat16)

    up, down, up2, down2 = step(own, 1), step(own, -1), step(own, 2), step(own, -2)
    near = jnp.concatenate([own, up, down, up2, down2], 0)
    up3, down3 = step(up2, 1), step(down2, -1)
    up4, down4 = step(up2[:half], 2), step(down2[half:], -2)
    near_sibling = step(near, 0, 1)
    far = jnp.concatenate([up3, down3, up4, down4], 0)
    far_sibling = step(far, 0, 1)

    ladder = pl.pallas_call(
        decode_kernel,
        out_shape=jax.ShapeDtypeStruct((height, LANES), jnp.float32),
        in_specs=[VMEM],
        out_specs=VMEM,
        compiler_params=pltpu.CompilerParams(vmem_limit_bytes=16 << 20),
        cost_estimate=pl.CostEstimate(flops=2**22, bytes_accessed=5 * 2**19, transcendentals=0),
        name="decode",
    )(shares)

    where = jnp.stack([narrow_index // 2, narrow_index % 2]).astype(jnp.int32)
    return pl.pallas_call(
        finish_kernel,
        out_shape=jax.ShapeDtypeStruct((height, LANES), jnp.float32),
        in_specs=[SMEM] + [VMEM] * 8,
        out_specs=VMEM,
        compiler_params=pltpu.CompilerParams(vmem_limit_bytes=24 << 20),
        cost_estimate=pl.CostEstimate(flops=2**29, bytes_accessed=2**22, transcendentals=0),
        name="finish",
    )(
        where,
        pair_integrals,
        ladder,
        occupied_energy.reshape(height, 1),
        virtual_energy.reshape(1, LANES),
        near,
        far,
        near_sibling,
        far_sibling,
    )


def solution(mesh):
    placed = (P("narrow", "wide"), P("wide", None), P("narrow", None), P(), P("narrow"), P("wide"))
    return jax.shard_map(
        on_device, mesh=mesh, in_specs=placed, out_specs=P("narrow", "wide"), check_vma=False
    )
```

```python
import jax
import jax.numpy as jnp
from jax import lax
from jax.experimental import pallas as pl
from jax.experimental.pallas import tpu as pltpu
from jax.sharding import PartitionSpec as P

CHUNKS = 16
DEPTH = 32
LANES = 256
CODE_ROWS = 16
STEPS = 256.0
TOP = 32760.0
PER = 2
EARLY = 6
VMEM = pl.BlockSpec(memory_space=pltpu.VMEM)
HBM = pl.BlockSpec(memory_space=pltpu.HBM)
SMEM = pl.BlockSpec(memory_space=pltpu.SMEM)


def iota(shape, dim):
    return lax.broadcasted_iota(jnp.int32, shape, dim)


def ones_where(mask):
    return jnp.where(mask, 1.0, 0.0)


def bdot(left, right, dims=((1,), (0,))):
    return lax.dot_general(
        left.astype(jnp.bfloat16),
        right.astype(jnp.bfloat16),
        (dims, ((), ())),
        preferred_element_type=jnp.float32,
    )


def count_before(classes):
    member = jnp.concatenate(
        [ones_where(classes[c : c + 1, :] == iota((CHUNKS, LANES), 0)) for c in range(CHUNKS)], 0
    )
    earlier = ones_where(iota((LANES, LANES), 0) < iota((LANES, LANES), 1))
    return member, bdot(member, earlier)


def pick(member, table):
    return jnp.sum((member * table).reshape(CHUNKS, CHUNKS, LANES), axis=1).astype(jnp.int32)


def widen(ref):
    halves = [ref[pl.ds(k, CHUNKS, stride=2), :] for k in range(2)]
    return jnp.concatenate(halves, 1)


def select_kernel(shift, here_ref, index_ref, far_amp_ref, sent_ref, rank_ref, amp_ref, amp_sem):
    fetch = pltpu.make_async_copy(far_amp_ref, amp_ref, amp_sem)
    fetch.start()
    index = widen(index_ref)
    here = here_ref[0]
    owner = jnp.right_shift(index, shift)
    member, within = count_before(owner)
    r, c = iota((LANES, LANES), 0), iota((LANES, LANES), 1)
    ahead = ones_where(((r & 15) == (c & 15)) & (jnp.right_shift(c, 4) < jnp.right_shift(r, 4)))
    base = jnp.sum(bdot(ahead, member), axis=1, keepdims=True)
    rank = pick(member, within + base)
    rank_ref[...] = rank
    middle, depth = rank & 15, jnp.right_shift(rank, 4)
    column = index & ((1 << shift) - 1)
    high, low = jnp.right_shift(column, 6).astype(jnp.float32), (column & 63).astype(jnp.float32)
    lefts, rights = [], []
    for k in range(CHUNKS):
        one = slice(k, k + 1)
        hit = ones_where((depth[one] == iota((DEPTH, LANES), 0)) & (owner[one] == here))
        lefts.append(jnp.concatenate([hit * high[one], hit * low[one]], 0))
        rights.append(ones_where(middle[one] == iota((CHUNKS, LANES), 0)))
    found = bdot(jnp.concatenate(lefts, 1), jnp.concatenate(rights, 1), ((1,), (1,)))
    columns = (found[:DEPTH] * 64.0 + found[DEPTH:]).astype(jnp.int32)
    span = amp_ref.shape[1]
    lane = iota((DEPTH, span), 1)
    fetch.wait()
    for k in range(0, CHUNKS, 4):
        chosen = jnp.concatenate(
            [
                ones_where(lane == columns[:, j : j + 1]).astype(jnp.bfloat16)
                for j in range(k, k + 4)
            ],
            0,
        )
        got = bdot(chosen, amp_ref[...], ((1,), (1,))).astype(jnp.bfloat16)
        sent_ref[k : k + 4] = got.reshape(4, DEPTH, got.shape[1])


def route_kernel(shift, here_ref, index_ref, rank_ref, forward_ref, settle_ref):
    index, rank, here = widen(index_ref), rank_ref[...], here_ref[0]
    owner = jnp.right_shift(index, shift)
    middle, depth = rank & 15, jnp.right_shift(rank, 4)
    member, within = count_before(middle)
    place = pick(member, within)
    source = (owner * DEPTH + depth).astype(jnp.float32)
    lane = iota((DEPTH, CHUNKS * DEPTH), 1)
    for k in range(CHUNKS):
        one = slice(k, k + 1)
        hit = (place[one] == iota((DEPTH, LANES), 0)) & (middle[one] == here)
        row = jnp.sum(jnp.where(hit, source[one], 0.0), axis=1, keepdims=True).astype(jnp.int32)
        forward_ref[k * DEPTH : (k + 1) * DEPTH, :] = ones_where(lane == row).astype(jnp.bfloat16)
    arrived = (middle * DEPTH + place).astype(jnp.float32)
    own = iota((CHUNKS, LANES), 0) == here
    wanted = jnp.sum(jnp.where(own, arrived, 0.0), axis=0, keepdims=True).astype(jnp.int32)
    settle_ref[...] = ones_where(iota((CHUNKS * DEPTH, LANES), 0) == wanted).astype(jnp.bfloat16)


def forward_kernel(forward_ref, first_ref, after_ref, moved_ref):
    del after_ref
    arrived = first_ref[...].reshape(CHUNKS * DEPTH, first_ref.shape[2])
    moved = bdot(forward_ref[...], arrived).astype(jnp.bfloat16)
    moved_ref[...] = moved.reshape(moved_ref.shape)


def settle_kernel(second_ref, settle_ref, after_ref, own_ref):
    del after_ref
    arrived = second_ref[...].reshape(CHUNKS * DEPTH, second_ref.shape[2])
    own_ref[...] = bdot(arrived, settle_ref[...], ((0,), (0,))).astype(jnp.bfloat16)


def ladder_kernel(start, count, amp_ref, int_ref, *refs):
    coded_ref, held_ref, stage_ref, in_sems, out_sems = refs[-5:]
    height = amp_ref.shape[0]
    width = PER * LANES
    ins, outs = [], []
    for b in range(count):
        ins.append(
            pltpu.make_async_copy(
                int_ref.at[:, pl.ds((start + b) * width, width)], held_ref.at[b], in_sems.at[b]
            )
        )
        ins[b].start()
    for b in range(count):
        ins[b].wait()
        slab = jnp.dot(amp_ref[...], held_ref[b], preferred_element_type=jnp.float32)
        for j in range(PER):
            part = slab[:, j * LANES : (j + 1) * LANES]
            largest = jnp.max(jnp.abs(part), axis=0, keepdims=True)
            code = jnp.ceil(jnp.log2(jnp.maximum(largest, 2.0**-120)) * STEPS) + 1.0
            shrunk = part * jnp.exp2(code * (-1.0 / STEPS)) * TOP
            k = b * PER + j
            stage_ref[k, :height, :] = jnp.round(shrunk).astype(jnp.int32).astype(jnp.int16)
            stage_ref[k, height:, :] = jnp.broadcast_to(
                code.astype(jnp.int32), (CODE_ROWS, LANES)
            ).astype(jnp.int16)
        outs.append(
            pltpu.make_async_copy(
                stage_ref.at[pl.ds(b * PER, PER)],
                coded_ref.at[pl.ds((start + b) * PER, PER)],
                out_sems.at[b],
            )
        )
        outs[b].start()
    for out in outs:
        out.wait()


def decode_kernel(coded_ref, sum_ref):
    height = sum_ref.shape[0]
    total = jnp.zeros(sum_ref.shape, jnp.float32)
    for k in range(CHUNKS):
        code = coded_ref[k, height:, :].astype(jnp.int32).astype(jnp.float32)[:1, :]
        values = coded_ref[k, :height, :].astype(jnp.int32).astype(jnp.float32)
        total = total + values * jnp.exp2(code * (1.0 / STEPS))
    sum_ref[...] = total * (1.0 / TOP)


def hole(place_ref, pair_ref, total, blocks):
    z, core = place_ref[0], place_ref[1]
    rows = pair_ref.shape[0]
    for away, other, start, ref in blocks:
        which = 1 - core if other else core
        n = jnp.bitwise_and(z - away + 8, 7) * 2 + which
        columns = pl.ds(pl.multiple_of(n * rows + start, 128), ref.shape[0])
        total = total + jnp.dot(
            pair_ref[:, columns], ref[...], preferred_element_type=jnp.float32
        )
    return total


NEAR = (0, 1, -1, 2, -2)


def near_kernel(place_ref, pair_ref, *refs):
    blocks = [(NEAR[k % 5], k >= 5, 0, refs[k]) for k in range(10)]
    refs[-1][...] = hole(place_ref, pair_ref, jnp.zeros(refs[-1].shape, jnp.float32), blocks)


def finish_kernel(place_ref, pair_ref, ladder_ref, near_ref, occ_ref, virt_ref, *refs):
    half = pair_ref.shape[0] // 2
    kinds = ((3, 0), (-3, 0), (4, 0), (4, half))
    blocks = [kinds[k % 4][:1] + (k >= 4,) + kinds[k % 4][1:] + (refs[k],) for k in range(8)]
    total = hole(place_ref, pair_ref, ladder_ref[...] + near_ref[...], blocks)
    refs[-1][...] = total / (virt_ref[...] - occ_ref[...])


def on_device(amplitudes, integrals, pair_integrals, slab_index, occupied_energy, virtual_energy):
    wide_index = lax.axis_index("wide")
    narrow_index = lax.axis_index("narrow")
    height, span = amplitudes.shape
    shift = span.bit_length() - 1
    here = wide_index.astype(jnp.int32).reshape(1)
    index = slab_index.reshape(2 * CHUNKS, LANES // 2)
    half = height // 2

    def step(value, dz, dc=0):
        ring = [
            (z * 2 + c, (z + dz) % 8 * 2 + (c + dc) % 2) for z in range(8) for c in range(2)
        ]
        return lax.ppermute(value, "narrow", ring)

    sent, rank = pl.pallas_call(
        lambda *refs: select_kernel(shift, *refs),
        out_shape=(
            jax.ShapeDtypeStruct((CHUNKS, DEPTH, height), jnp.bfloat16),
            jax.ShapeDtypeStruct((CHUNKS, LANES), jnp.int32),
        ),
        in_specs=[SMEM, VMEM, HBM],
        out_specs=(VMEM, VMEM),
        scratch_shapes=[pltpu.VMEM((height, span), jnp.bfloat16), pltpu.SemaphoreType.DMA(())],
        compiler_params=pltpu.CompilerParams(vmem_limit_bytes=59 << 20),
        cost_estimate=pl.CostEstimate(flops=2**30, bytes_accessed=2**21, transcendentals=0),
        name="select",
    )(here, index, amplitudes)
    first = lax.all_to_all(sent, "wide", 0, 0, tiled=True)

    forward, settle = pl.pallas_call(
        lambda *refs: route_kernel(shift, *refs),
        out_shape=(
            jax.ShapeDtypeStruct((CHUNKS * DEPTH, CHUNKS * DEPTH), jnp.bfloat16),
            jax.ShapeDtypeStruct((CHUNKS * DEPTH, LANES), jnp.bfloat16),
        ),
        in_specs=[SMEM, VMEM, VMEM],
        out_specs=(VMEM, VMEM),
        compiler_params=pltpu.CompilerParams(vmem_limit_bytes=16 << 20),
        cost_estimate=pl.CostEstimate(flops=2**28, bytes_accessed=2**20, transcendentals=0),
        name="route",
    )(here, index, rank)

    def ladder_part(start, count, extra, **kw):
        return pl.pallas_call(
            lambda *refs: ladder_kernel(start, count, *refs),
            out_shape=jax.ShapeDtypeStruct((CHUNKS, height + CODE_ROWS, LANES), jnp.int16),
            in_specs=[VMEM] + [HBM] * (1 + len(extra)),
            out_specs=HBM,
            scratch_shapes=[
                pltpu.VMEM((count, span, PER * LANES), jnp.bfloat16),
                pltpu.VMEM((count * PER, height + CODE_ROWS, LANES), jnp.int16),
                pltpu.SemaphoreType.DMA((count,)),
                pltpu.SemaphoreType.DMA((count,)),
            ],
            compiler_params=pltpu.CompilerParams(vmem_limit_bytes=50 << 20),
            cost_estimate=pl.CostEstimate(
                flops=2 * height * span * count * PER * LANES,
                bytes_accessed=count * PER * 2**20,
                transcendentals=0,
            ),
            **kw,
        )(amplitudes, integrals, *extra)

    slabs = CHUNKS // PER
    early = ladder_part(0, EARLY, (rank,), name="ladder_early")

    moved = pl.pallas_call(
        forward_kernel,
        out_shape=jax.ShapeDtypeStruct((CHUNKS, DEPTH, height), jnp.bfloat16),
        in_specs=[VMEM, VMEM, HBM],
        out_specs=VMEM,
        compiler_params=pltpu.CompilerParams(vmem_limit_bytes=8 << 20),
        cost_estimate=pl.CostEstimate(flops=2**27, bytes_accessed=2**20, transcendentals=0),
        name="forward",
    )(forward, first, early)
    second = lax.all_to_all(moved, "wide", 0, 0, tiled=True)

    coded = ladder_part(
        EARLY, slabs - EARLY, (moved, early), input_output_aliases={3: 0}, name="ladder_late"
    )
    shares = lax.all_to_all(coded, "wide", 0, 0, tiled=True)

    own = pl.pallas_call(
        settle_kernel,
        out_shape=jax.ShapeDtypeStruct((height, LANES), jnp.bfloat16),
        in_specs=[VMEM, VMEM, HBM],
        out_specs=VMEM,
        compiler_params=pltpu.CompilerParams(vmem_limit_bytes=8 << 20),
        cost_estimate=pl.CostEstimate(flops=2**26, bytes_accessed=2**20, transcendentals=0),
        name="settle",
    )(second, settle, coded)

    up, down, up2, down2 = step(own, 1), step(own, -1), step(own, 2), step(own, -2)
    up3, down3 = step(up2, 1), step(down2, -1)
    up4, down4 = step(up2[:half], 2), step(down2[half:], -2)
    near = [own, up, down, up2, down2]
    far = [up3, down3, up4, down4]
    near += [step(block, 0, 1) for block in near]
    far += [step(block, 0, 1) for block in far]

    ladder = pl.pallas_call(
        decode_kernel,
        out_shape=jax.ShapeDtypeStruct((height, LANES), jnp.float32),
        in_specs=[VMEM],
        out_specs=VMEM,
        compiler_params=pltpu.CompilerParams(vmem_limit_bytes=16 << 20),
        cost_estimate=pl.CostEstimate(flops=2**22, bytes_accessed=5 * 2**19, transcendentals=0),
        name="decode",
    )(shares)

    where = jnp.stack([narrow_index >> 1, narrow_index & 1]).astype(jnp.int32)
    near_sum = pl.pallas_call(
        near_kernel,
        out_shape=jax.ShapeDtypeStruct((height, LANES), jnp.float32),
        in_specs=[SMEM] + [VMEM] * 11,
        out_specs=VMEM,
        compiler_params=pltpu.CompilerParams(vmem_limit_bytes=16 << 20),
        cost_estimate=pl.CostEstimate(flops=2**28, bytes_accessed=2**22, transcendentals=0),
        name="near",
    )(where, pair_integrals, *near)
    return pl.pallas_call(
        finish_kernel,
        out_shape=jax.ShapeDtypeStruct((height, LANES), jnp.float32),
        in_specs=[SMEM] + [VMEM] * 13,
        out_specs=VMEM,
        compiler_params=pltpu.CompilerParams(vmem_limit_bytes=16 << 20),
        cost_estimate=pl.CostEstimate(flops=2**28, bytes_accessed=2**22, transcendentals=0),
        name="finish",
    )(
        where,
        pair_integrals,
        ladder,
        near_sum,
        occupied_energy.reshape(height, 1),
        virtual_energy.reshape(1, LANES),
        *far,
    )


def solution(mesh):
    placed = (P("narrow", "wide"), P("wide", None), P("narrow", None), P(), P("narrow"), P("wide"))
    return jax.shard_map(
        on_device, mesh=mesh, in_specs=placed, out_specs=P("narrow", "wide"), check_vma=False
    )
```

```python
import jax
import jax.numpy as jnp
from jax import lax
from jax.experimental import pallas as pl
from jax.experimental.pallas import tpu as pltpu
from jax.sharding import PartitionSpec as P

CHUNKS = 16
DEPTH = 32
LANES = 256
CODE_ROWS = 16
STEPS = 256.0
TOP = 32760.0
PER = 2
EARLY = 5
VMEM = pl.BlockSpec(memory_space=pltpu.VMEM)
HBM = pl.BlockSpec(memory_space=pltpu.HBM)
SMEM = pl.BlockSpec(memory_space=pltpu.SMEM)


def iota(shape, dim):
    return lax.broadcasted_iota(jnp.int32, shape, dim)


def ones_where(mask):
    return jnp.where(mask, 1.0, 0.0)


def bdot(left, right, dims=((1,), (0,))):
    return lax.dot_general(
        left.astype(jnp.bfloat16),
        right.astype(jnp.bfloat16),
        (dims, ((), ())),
        preferred_element_type=jnp.float32,
    )


def count_before(classes):
    member = jnp.concatenate(
        [ones_where(classes[c : c + 1, :] == iota((CHUNKS, LANES), 0)) for c in range(CHUNKS)], 0
    )
    earlier = ones_where(iota((LANES, LANES), 0) < iota((LANES, LANES), 1))
    return member, bdot(member, earlier)


def pick(member, table):
    return jnp.sum((member * table).reshape(CHUNKS, CHUNKS, LANES), axis=1).astype(jnp.int32)


def widen(ref):
    halves = [ref[pl.ds(k, CHUNKS, stride=2), :] for k in range(2)]
    return jnp.concatenate(halves, 1)


def select_kernel(shift, here_ref, index_ref, far_amp_ref, sent_ref, rank_ref, amp_ref, amp_sem):
    fetch = pltpu.make_async_copy(far_amp_ref, amp_ref, amp_sem)
    fetch.start()
    index = widen(index_ref)
    here = here_ref[0]
    owner = jnp.right_shift(index, shift)
    member, within = count_before(owner)
    r, c = iota((LANES, LANES), 0), iota((LANES, LANES), 1)
    ahead = ones_where(((r & 15) == (c & 15)) & (jnp.right_shift(c, 4) < jnp.right_shift(r, 4)))
    base = jnp.sum(bdot(ahead, member), axis=1, keepdims=True)
    rank = pick(member, within + base)
    rank_ref[...] = rank
    middle, depth = rank & 15, jnp.right_shift(rank, 4)
    column = index & ((1 << shift) - 1)
    high, low = jnp.right_shift(column, 6).astype(jnp.float32), (column & 63).astype(jnp.float32)
    lefts, rights = [], []
    for k in range(CHUNKS):
        one = slice(k, k + 1)
        hit = ones_where((depth[one] == iota((DEPTH, LANES), 0)) & (owner[one] == here))
        lefts.append(jnp.concatenate([hit * high[one], hit * low[one]], 0))
        rights.append(ones_where(middle[one] == iota((CHUNKS, LANES), 0)))
    found = bdot(jnp.concatenate(lefts, 1), jnp.concatenate(rights, 1), ((1,), (1,)))
    columns = (found[:DEPTH] * 64.0 + found[DEPTH:]).astype(jnp.int32)
    span = amp_ref.shape[1]
    lane = iota((DEPTH, span), 1)
    fetch.wait()
    for k in range(0, CHUNKS, 4):
        chosen = jnp.concatenate(
            [
                ones_where(lane == columns[:, j : j + 1]).astype(jnp.bfloat16)
                for j in range(k, k + 4)
            ],
            0,
        )
        got = bdot(chosen, amp_ref[...], ((1,), (1,))).astype(jnp.bfloat16)
        sent_ref[k : k + 4] = got.reshape(4, DEPTH, got.shape[1])


def route_kernel(shift, here_ref, index_ref, rank_ref, forward_ref, settle_ref):
    index, rank, here = widen(index_ref), rank_ref[...], here_ref[0]
    owner = jnp.right_shift(index, shift)
    middle, depth = rank & 15, jnp.right_shift(rank, 4)
    member, within = count_before(middle)
    place = pick(member, within)
    source = (owner * DEPTH + depth).astype(jnp.float32)
    lane = iota((DEPTH, CHUNKS * DEPTH), 1)
    for k in range(CHUNKS):
        one = slice(k, k + 1)
        hit = (place[one] == iota((DEPTH, LANES), 0)) & (middle[one] == here)
        row = jnp.sum(jnp.where(hit, source[one], 0.0), axis=1, keepdims=True).astype(jnp.int32)
        forward_ref[k * DEPTH : (k + 1) * DEPTH, :] = ones_where(lane == row).astype(jnp.bfloat16)
    arrived = (middle * DEPTH + place).astype(jnp.float32)
    own = iota((CHUNKS, LANES), 0) == here
    wanted = jnp.sum(jnp.where(own, arrived, 0.0), axis=0, keepdims=True).astype(jnp.int32)
    settle_ref[...] = ones_where(iota((CHUNKS * DEPTH, LANES), 0) == wanted).astype(jnp.bfloat16)


def forward_kernel(forward_ref, first_ref, after_ref, moved_ref):
    del after_ref
    arrived = first_ref[...].reshape(CHUNKS * DEPTH, first_ref.shape[2])
    moved = bdot(forward_ref[...], arrived).astype(jnp.bfloat16)
    moved_ref[...] = moved.reshape(moved_ref.shape)


def settle_kernel(second_ref, settle_ref, after_ref, own_ref):
    del after_ref
    arrived = second_ref[...].reshape(CHUNKS * DEPTH, second_ref.shape[2])
    own_ref[...] = bdot(arrived, settle_ref[...], ((0,), (0,))).astype(jnp.bfloat16)


def ladder_kernel(start, count, amp_ref, int_ref, *refs):
    coded_ref, held_ref, stage_ref, in_sems, out_sems = refs[-5:]
    height = amp_ref.shape[0]
    width = PER * LANES
    ins, outs = [], []
    for b in range(count):
        ins.append(
            pltpu.make_async_copy(
                int_ref.at[:, pl.ds((start + b) * width, width)], held_ref.at[b], in_sems.at[b]
            )
        )
        ins[b].start()
    for b in range(count):
        ins[b].wait()
        slab = jnp.dot(amp_ref[...], held_ref[b], preferred_element_type=jnp.float32)
        for j in range(PER):
            part = slab[:, j * LANES : (j + 1) * LANES]
            largest = jnp.max(jnp.abs(part), axis=0, keepdims=True)
            code = jnp.ceil(jnp.log2(jnp.maximum(largest, 2.0**-120)) * STEPS) + 1.0
            shrunk = part * jnp.exp2(code * (-1.0 / STEPS)) * TOP
            k = b * PER + j
            stage_ref[k, :height, :] = jnp.round(shrunk).astype(jnp.int32).astype(jnp.int16)
            stage_ref[k, height:, :] = jnp.broadcast_to(
                code.astype(jnp.int32), (CODE_ROWS, LANES)
            ).astype(jnp.int16)
        outs.append(
            pltpu.make_async_copy(
                stage_ref.at[pl.ds(b * PER, PER)],
                coded_ref.at[pl.ds((start + b) * PER, PER)],
                out_sems.at[b],
            )
        )
        outs[b].start()
    for out in outs:
        out.wait()


def finish_kernel(
    place_ref, far_pair_ref, far_coded_ref, occ_ref, virt_ref, near_ref, far_ref, *refs
):
    near_sibling_ref, far_sibling_ref, out_ref, pair_ref, coded_ref, sems = refs
    fetches = [
        pltpu.make_async_copy(far_pair_ref, pair_ref, sems.at[0]),
        pltpu.make_async_copy(far_coded_ref, coded_ref, sems.at[1]),
    ]
    for fetch in fetches:
        fetch.start()
    z, core = place_ref[0], place_ref[1]
    rows = out_ref.shape[0]
    half = rows // 2
    fetches[0].wait()
    total = jnp.zeros(out_ref.shape, jnp.float32)

    def add(total, away, which, start, block):
        n = jnp.bitwise_and(z - away + 8, 7) * 2 + which
        columns = pl.ds(pl.multiple_of(n * rows + start, 128), block.shape[0])
        return total + jnp.dot(pair_ref[:, columns], block, preferred_element_type=jnp.float32)

    sides = ((near_ref, far_ref, core), (near_sibling_ref, far_sibling_ref, 1 - core))
    for near, far, which in sides:
        for k, away in enumerate((0, 1, -1, 2, -2)):
            total = add(total, away, which, 0, near[k * rows : (k + 1) * rows])
        total = add(total, 3, which, 0, far[:rows])
        total = add(total, -3, which, 0, far[rows : 2 * rows])
        total = add(total, 4, which, 0, far[2 * rows : 2 * rows + half])
        total = add(total, 4, which, half, far[2 * rows + half :])
    fetches[1].wait()
    ladder = jnp.zeros(out_ref.shape, jnp.float32)
    for k in range(CHUNKS):
        code = coded_ref[k, rows:, :].astype(jnp.int32).astype(jnp.float32)[:1, :]
        values = coded_ref[k, :rows, :].astype(jnp.int32).astype(jnp.float32)
        ladder = ladder + values * jnp.exp2(code * (1.0 / STEPS))
    out_ref[...] = (ladder * (1.0 / TOP) + total) / (virt_ref[...] - occ_ref[...])


def on_device(amplitudes, integrals, pair_integrals, slab_index, occupied_energy, virtual_energy):
    wide_index = lax.axis_index("wide")
    narrow_index = lax.axis_index("narrow")
    height, span = amplitudes.shape
    shift = span.bit_length() - 1
    here = wide_index.astype(jnp.int32).reshape(1)
    index = slab_index.reshape(2 * CHUNKS, LANES // 2)
    half = height // 2

    def step(value, dz, dc=0):
        ring = [
            (z * 2 + c, (z + dz) % 8 * 2 + (c + dc) % 2) for z in range(8) for c in range(2)
        ]
        return lax.ppermute(value, "narrow", ring)

    sent, rank = pl.pallas_call(
        lambda *refs: select_kernel(shift, *refs),
        out_shape=(
            jax.ShapeDtypeStruct((CHUNKS, DEPTH, height), jnp.bfloat16),
            jax.ShapeDtypeStruct((CHUNKS, LANES), jnp.int32),
        ),
        in_specs=[SMEM, VMEM, HBM],
        out_specs=(VMEM, VMEM),
        scratch_shapes=[pltpu.VMEM((height, span), jnp.bfloat16), pltpu.SemaphoreType.DMA(())],
        compiler_params=pltpu.CompilerParams(vmem_limit_bytes=59 << 20),
        cost_estimate=pl.CostEstimate(flops=2**30, bytes_accessed=2**21, transcendentals=0),
        name="select",
    )(here, index, amplitudes)
    first = lax.all_to_all(sent, "wide", 0, 0, tiled=True)

    forward, settle = pl.pallas_call(
        lambda *refs: route_kernel(shift, *refs),
        out_shape=(
            jax.ShapeDtypeStruct((CHUNKS * DEPTH, CHUNKS * DEPTH), jnp.bfloat16),
            jax.ShapeDtypeStruct((CHUNKS * DEPTH, LANES), jnp.bfloat16),
        ),
        in_specs=[SMEM, VMEM, VMEM],
        out_specs=(VMEM, VMEM),
        compiler_params=pltpu.CompilerParams(vmem_limit_bytes=16 << 20),
        cost_estimate=pl.CostEstimate(flops=2**28, bytes_accessed=2**20, transcendentals=0),
        name="route",
    )(here, index, rank)

    def ladder_part(start, count, extra, **kw):
        return pl.pallas_call(
            lambda *refs: ladder_kernel(start, count, *refs),
            out_shape=jax.ShapeDtypeStruct((CHUNKS, height + CODE_ROWS, LANES), jnp.int16),
            in_specs=[VMEM] + [HBM] * (1 + len(extra)),
            out_specs=HBM,
            scratch_shapes=[
                pltpu.VMEM((count, span, PER * LANES), jnp.bfloat16),
                pltpu.VMEM((count * PER, height + CODE_ROWS, LANES), jnp.int16),
                pltpu.SemaphoreType.DMA((count,)),
                pltpu.SemaphoreType.DMA((count,)),
            ],
            compiler_params=pltpu.CompilerParams(vmem_limit_bytes=50 << 20),
            cost_estimate=pl.CostEstimate(
                flops=2 * height * span * count * PER * LANES,
                bytes_accessed=count * PER * 2**20,
                transcendentals=0,
            ),
            **kw,
        )(amplitudes, integrals, *extra)

    slabs = CHUNKS // PER
    early = ladder_part(0, EARLY, (rank,), name="ladder_early")

    moved = pl.pallas_call(
        forward_kernel,
        out_shape=jax.ShapeDtypeStruct((CHUNKS, DEPTH, height), jnp.bfloat16),
        in_specs=[VMEM, VMEM, HBM],
        out_specs=VMEM,
        compiler_params=pltpu.CompilerParams(vmem_limit_bytes=8 << 20),
        cost_estimate=pl.CostEstimate(flops=2**27, bytes_accessed=2**20, transcendentals=0),
        name="forward",
    )(forward, first, early)
    second = lax.all_to_all(moved, "wide", 0, 0, tiled=True)

    coded = ladder_part(
        EARLY, slabs - EARLY, (moved, early), input_output_aliases={3: 0}, name="ladder_late"
    )
    shares = lax.all_to_all(coded, "wide", 0, 0, tiled=True)

    own = pl.pallas_call(
        settle_kernel,
        out_shape=jax.ShapeDtypeStruct((height, LANES), jnp.bfloat16),
        in_specs=[VMEM, VMEM, HBM],
        out_specs=VMEM,
        compiler_params=pltpu.CompilerParams(vmem_limit_bytes=8 << 20),
        cost_estimate=pl.CostEstimate(flops=2**26, bytes_accessed=2**20, transcendentals=0),
        name="settle",
    )(second, settle, coded)

    up, down, up2, down2 = step(own, 1), step(own, -1), step(own, 2), step(own, -2)
    up3, down3 = step(up2, 1), step(down2, -1)
    up4, down4 = step(up2[:half], 2), step(down2[half:], -2)
    near = jnp.concatenate([own, up, down, up2, down2], 0)
    near_sibling = step(near, 0, 1)
    far = jnp.concatenate([up3, down3, up4, down4], 0)
    far_sibling = step(far, 0, 1)

    where = jnp.stack([narrow_index >> 1, narrow_index & 1]).astype(jnp.int32)
    return pl.pallas_call(
        finish_kernel,
        out_shape=jax.ShapeDtypeStruct((height, LANES), jnp.float32),
        in_specs=[SMEM, HBM, HBM] + [VMEM] * 6,
        out_specs=VMEM,
        scratch_shapes=[
            pltpu.VMEM(pair_integrals.shape, jnp.bfloat16),
            pltpu.VMEM(shares.shape, jnp.int16),
            pltpu.SemaphoreType.DMA((2,)),
        ],
        compiler_params=pltpu.CompilerParams(vmem_limit_bytes=50 << 20),
        cost_estimate=pl.CostEstimate(flops=2**30, bytes_accessed=2**23, transcendentals=0),
        name="finish",
    )(
        where,
        pair_integrals,
        shares,
        occupied_energy.reshape(height, 1),
        virtual_energy.reshape(1, LANES),
        near,
        far,
        near_sibling,
        far_sibling,
    )


def solution(mesh):
    placed = (P("narrow", "wide"), P("wide", None), P("narrow", None), P(), P("narrow"), P("wide"))
    return jax.shard_map(
        on_device, mesh=mesh, in_specs=placed, out_specs=P("narrow", "wide"), check_vma=False
    )
```

```python
import jax
import jax.numpy as jnp
from jax import lax
from jax.experimental import pallas as pl
from jax.experimental.pallas import tpu as pltpu
from jax.sharding import PartitionSpec as P

CHUNKS = 16
DEPTH = 32
HOPS = ((0, 0), (1, 0), (3, 0), (0, 1))
ROOM = 80
LANES = 256
CODE_ROWS = 16
STEPS = 256.0
TOP = 32760.0
PER = 2
VMEM = pl.BlockSpec(memory_space=pltpu.VMEM)
HBM = pl.BlockSpec(memory_space=pltpu.HBM)
SMEM = pl.BlockSpec(memory_space=pltpu.SMEM)


def iota(shape, dim):
    return lax.broadcasted_iota(jnp.int32, shape, dim)


def ones_where(mask):
    return jnp.where(mask, 1.0, 0.0)


def bdot(left, right, dims=((1,), (0,))):
    return lax.dot_general(
        left.astype(jnp.bfloat16),
        right.astype(jnp.bfloat16),
        (dims, ((), ())),
        preferred_element_type=jnp.float32,
    )


def count_before(classes):
    member = jnp.concatenate(
        [ones_where(classes[c : c + 1, :] == iota((CHUNKS, LANES), 0)) for c in range(CHUNKS)], 0
    )
    earlier = ones_where(iota((LANES, LANES), 0) < iota((LANES, LANES), 1))
    return member, bdot(member, earlier)


def pick(member, table):
    return jnp.sum((member * table).reshape(CHUNKS, CHUNKS, LANES), axis=1).astype(jnp.int32)


def widen(ref):
    halves = [ref[pl.ds(k, CHUNKS, stride=2), :] for k in range(2)]
    return jnp.concatenate(halves, 1)


def select_kernel(shift, here_ref, index_ref, far_amp_ref, *refs):
    *sent_refs, rank_ref, amp_ref, amp_sem = refs
    fetch = pltpu.make_async_copy(far_amp_ref, amp_ref, amp_sem)
    fetch.start()
    index = widen(index_ref)
    here = here_ref[0]
    owner = jnp.right_shift(index, shift)
    member, within = count_before(owner)
    r, c = iota((LANES, LANES), 0), iota((LANES, LANES), 1)
    ahead = ones_where(((r & 15) == (c & 15)) & (jnp.right_shift(c, 4) < jnp.right_shift(r, 4)))
    base = jnp.sum(bdot(ahead, member), axis=1, keepdims=True)
    rank = pick(member, within + base)
    rank_ref[...] = rank
    middle, depth = rank & 15, jnp.right_shift(rank, 4)
    column = index & ((1 << shift) - 1)
    high, low = jnp.right_shift(column, 6).astype(jnp.float32), (column & 63).astype(jnp.float32)
    lefts, rights = [], []
    for k in range(CHUNKS):
        one = slice(k, k + 1)
        hit = ones_where((depth[one] == iota((DEPTH, LANES), 0)) & (owner[one] == here))
        lefts.append(jnp.concatenate([hit * high[one], hit * low[one]], 0))
        rights.append(ones_where(middle[one] == iota((CHUNKS, LANES), 0)))
    found = bdot(jnp.concatenate(lefts, 1), jnp.concatenate(rights, 1), ((1,), (1,)))
    columns = (found[:DEPTH] * 64.0 + found[DEPTH:]).astype(jnp.int32)
    span = amp_ref.shape[1]
    lane = iota((DEPTH, span), 1)
    fetch.wait()
    for hop, sent_ref in enumerate(sent_refs):
        chosen = jnp.concatenate(
            [
                ones_where(lane == columns[:, j : j + 1]).astype(jnp.bfloat16)
                for j in range(hop, CHUNKS, 4)
            ],
            0,
        )
        sent_ref[...] = bdot(chosen, amp_ref[...], ((1,), (1,))).astype(jnp.bfloat16)


def route_kernel(shift, here_ref, index_ref, rank_ref, forward_ref, settle_ref):
    index, rank, here = widen(index_ref), rank_ref[...], here_ref[0]
    owner = jnp.right_shift(index, shift)
    last, depth = rank & 15, jnp.right_shift(rank, 4)
    hop = rank & 3
    x, y = jnp.right_shift(owner, 2), owner & 3
    for k, (dx, dy) in enumerate(HOPS):
        x, y = jnp.where(hop == k, x + dx, x), jnp.where(hop == k, y + dy, y)
    middle = (x & 3) * 4 + (y & 3)
    member, within = count_before(middle)
    place = pick(member, within)
    source = (hop * (4 * DEPTH) + jnp.right_shift(last, 2) * DEPTH + depth).astype(jnp.float32)
    lane = iota((ROOM, CHUNKS * DEPTH), 1)
    for k in range(CHUNKS):
        one = slice(k, k + 1)
        hit = (place[one] == iota((ROOM, LANES), 0)) & (middle[one] == here)
        row = jnp.sum(jnp.where(hit, source[one], 0.0), axis=1, keepdims=True).astype(jnp.int32)
        forward_ref[k * ROOM : (k + 1) * ROOM, :] = ones_where(lane == row).astype(jnp.bfloat16)
    arrived = (middle * ROOM + place).astype(jnp.float32)
    own = iota((CHUNKS, LANES), 0) == here
    wanted = jnp.sum(jnp.where(own, arrived, 0.0), axis=0, keepdims=True).astype(jnp.int32)
    settle_ref[...] = ones_where(iota((CHUNKS * ROOM, LANES), 0) == wanted).astype(jnp.bfloat16)


def forward_kernel(forward_ref, *refs):
    *first_refs, moved_ref = refs
    arrived = jnp.concatenate([ref[...] for ref in first_refs], 0)
    moved = bdot(forward_ref[...], arrived).astype(jnp.bfloat16)
    moved_ref[...] = moved.reshape(moved_ref.shape)


def settle_kernel(second_ref, settle_ref, after_ref, own_ref):
    del after_ref
    arrived = second_ref[...].reshape(CHUNKS * ROOM, second_ref.shape[2])
    own_ref[...] = bdot(arrived, settle_ref[...], ((0,), (0,))).astype(jnp.bfloat16)


def ladder_kernel(amp_ref, int_ref, after_ref, coded_ref, held_ref, stage_ref, in_sems, out_sems):
    del after_ref
    count = CHUNKS // PER
    height = amp_ref.shape[0]
    width = PER * LANES
    ins, outs = [], []
    for b in range(count):
        ins.append(
            pltpu.make_async_copy(
                int_ref.at[:, pl.ds(b * width, width)], held_ref.at[b], in_sems.at[b]
            )
        )
        ins[b].start()
    for b in range(count):
        ins[b].wait()
        slab = jnp.dot(amp_ref[...], held_ref[b], preferred_element_type=jnp.float32)
        for j in range(PER):
            part = slab[:, j * LANES : (j + 1) * LANES]
            largest = jnp.max(jnp.abs(part), axis=0, keepdims=True)
            code = jnp.ceil(jnp.log2(jnp.maximum(largest, 2.0**-120)) * STEPS) + 1.0
            shrunk = part * jnp.exp2(code * (-1.0 / STEPS)) * TOP
            k = b * PER + j
            stage_ref[k, :height, :] = jnp.round(shrunk).astype(jnp.int32).astype(jnp.int16)
            stage_ref[k, height:, :] = jnp.broadcast_to(
                code.astype(jnp.int32), (CODE_ROWS, LANES)
            ).astype(jnp.int16)
        outs.append(
            pltpu.make_async_copy(
                stage_ref.at[pl.ds(b * PER, PER)],
                coded_ref.at[pl.ds(b * PER, PER)],
                out_sems.at[b],
            )
        )
        outs[b].start()
    for out in outs:
        out.wait()


def hole_kernel(place_ref, far_pair_ref, occ_ref, virt_ref, near_ref, far_ref, *refs):
    *away_refs, out_ref, pair_ref, near_sibling_ref, far_sibling_ref, sems = refs
    fetches = [
        pltpu.make_async_copy(source, target, sems.at[k])
        for k, (source, target) in enumerate(
            zip([far_pair_ref] + away_refs, [pair_ref, near_sibling_ref, far_sibling_ref])
        )
    ]
    for fetch in fetches:
        fetch.start()
    z, core = place_ref[0], place_ref[1]
    rows = near_ref.shape[0] // 5
    half = rows // 2
    total = jnp.zeros(out_ref.shape[1:], jnp.float32)

    def add(total, away, which, start, block):
        n = jnp.bitwise_and(z - away + 8, 7) * 2 + which
        columns = pl.ds(pl.multiple_of(n * rows + start, 128), block.shape[0])
        return total + jnp.dot(pair_ref[:, columns], block, preferred_element_type=jnp.float32)

    out_ref[1] = virt_ref[...] - occ_ref[...]
    fetches[0].wait()
    sides = ((near_ref, far_ref, core), (near_sibling_ref, far_sibling_ref, 1 - core))
    for near, far, which in sides:
        if near is near_sibling_ref:
            fetches[1].wait()
            fetches[2].wait()
        for k, away in enumerate((0, 1, -1, 2, -2)):
            total = add(total, away, which, 0, near[k * rows : (k + 1) * rows])
        total = add(total, 3, which, 0, far[:rows])
        total = add(total, -3, which, 0, far[rows : 2 * rows])
        total = add(total, 4, which, 0, far[2 * rows : 2 * rows + half])
        total = add(total, 4, which, half, far[2 * rows + half :])
    out_ref[0] = total


def finish_kernel(coded_ref, far_hole_ref, out_ref, hole_ref, hole_sem):
    fetch = pltpu.make_async_copy(far_hole_ref, hole_ref, hole_sem)
    fetch.start()
    rows = out_ref.shape[0]
    ladder = jnp.zeros(out_ref.shape, jnp.float32)
    for k in range(CHUNKS):
        code = coded_ref[k, rows:, :].astype(jnp.int32).astype(jnp.float32)[:1, :]
        values = coded_ref[k, :rows, :].astype(jnp.int32).astype(jnp.float32)
        ladder = ladder + values * jnp.exp2(code * (1.0 / STEPS))
    fetch.wait()
    out_ref[...] = (ladder * (1.0 / TOP) + hole_ref[0]) / hole_ref[1]


def on_device(amplitudes, integrals, pair_integrals, slab_index, occupied_energy, virtual_energy):
    wide_index = lax.axis_index("wide")
    narrow_index = lax.axis_index("narrow")
    height, span = amplitudes.shape
    shift = span.bit_length() - 1
    here = wide_index.astype(jnp.int32).reshape(1)
    index = slab_index.reshape(2 * CHUNKS, LANES // 2)
    half = height // 2

    def step(value, dz, dc=0):
        ring = [
            (z * 2 + c, (z + dz) % 8 * 2 + (c + dc) % 2) for z in range(8) for c in range(2)
        ]
        return lax.ppermute(value, "narrow", ring)

    *sent, rank = pl.pallas_call(
        lambda *refs: select_kernel(shift, *refs),
        out_shape=(
            *[jax.ShapeDtypeStruct((4 * DEPTH, height), jnp.bfloat16) for _ in HOPS],
            jax.ShapeDtypeStruct((CHUNKS, LANES), jnp.int32),
        ),
        in_specs=[SMEM, VMEM, HBM],
        out_specs=(VMEM,) * (len(HOPS) + 1),
        scratch_shapes=[pltpu.VMEM((height, span), jnp.bfloat16), pltpu.SemaphoreType.DMA(())],
        compiler_params=pltpu.CompilerParams(vmem_limit_bytes=59 << 20),
        cost_estimate=pl.CostEstimate(flops=2**30, bytes_accessed=2**21, transcendentals=0),
        name="select",
    )(here, index, amplitudes)
    first = sent[:1] + [
        lax.ppermute(
            sent[k],
            "wide",
            [(x * 4 + y, (x + dx) % 4 * 4 + (y + dy) % 4) for x in range(4) for y in range(4)],
        )
        for k, (dx, dy) in enumerate(HOPS)
        if k
    ]

    forward, settle = pl.pallas_call(
        lambda *refs: route_kernel(shift, *refs),
        out_shape=(
            jax.ShapeDtypeStruct((CHUNKS * ROOM, CHUNKS * DEPTH), jnp.bfloat16),
            jax.ShapeDtypeStruct((CHUNKS * ROOM, LANES), jnp.bfloat16),
        ),
        in_specs=[SMEM, VMEM, VMEM],
        out_specs=(VMEM, VMEM),
        compiler_params=pltpu.CompilerParams(vmem_limit_bytes=16 << 20),
        cost_estimate=pl.CostEstimate(flops=2**28, bytes_accessed=2**20, transcendentals=0),
        name="route",
    )(here, index, rank)

    moved = pl.pallas_call(
        forward_kernel,
        out_shape=jax.ShapeDtypeStruct((CHUNKS, ROOM, height), jnp.bfloat16),
        in_specs=[VMEM] * (len(HOPS) + 1),
        out_specs=VMEM,
        compiler_params=pltpu.CompilerParams(vmem_limit_bytes=8 << 20),
        cost_estimate=pl.CostEstimate(flops=2**28, bytes_accessed=2**20, transcendentals=0),
        name="forward",
    )(forward, *first)
    second = lax.all_to_all(moved, "wide", 0, 0, tiled=True)

    slabs = CHUNKS // PER
    coded = pl.pallas_call(
        ladder_kernel,
        out_shape=jax.ShapeDtypeStruct((CHUNKS, height + CODE_ROWS, LANES), jnp.int16),
        in_specs=[VMEM, HBM, HBM],
        out_specs=HBM,
        scratch_shapes=[
            pltpu.VMEM((slabs, span, PER * LANES), jnp.bfloat16),
            pltpu.VMEM((CHUNKS, height + CODE_ROWS, LANES), jnp.int16),
            pltpu.SemaphoreType.DMA((slabs,)),
            pltpu.SemaphoreType.DMA((slabs,)),
        ],
        compiler_params=pltpu.CompilerParams(vmem_limit_bytes=50 << 20),
        cost_estimate=pl.CostEstimate(
            flops=2 * height * span * CHUNKS * LANES, bytes_accessed=18 * 2**20, transcendentals=0
        ),
        name="ladder",
    )(amplitudes, integrals, moved)
    shares = lax.all_to_all(coded, "wide", 0, 0, tiled=True)

    own = pl.pallas_call(
        settle_kernel,
        out_shape=jax.ShapeDtypeStruct((height, LANES), jnp.bfloat16),
        in_specs=[VMEM, VMEM, HBM],
        out_specs=VMEM,
        compiler_params=pltpu.CompilerParams(vmem_limit_bytes=8 << 20),
        cost_estimate=pl.CostEstimate(flops=2**26, bytes_accessed=2**20, transcendentals=0),
        name="settle",
    )(second, settle, coded)

    up, down, up2, down2 = step(own, 1), step(own, -1), step(own, 2), step(own, -2)
    up3, down3 = step(up2, 1), step(down2, -1)
    up4, down4 = step(up2[:half], 2), step(down2[half:], -2)
    near = jnp.concatenate([own, up, down, up2, down2], 0)
    near_sibling = step(near, 0, 1)
    far = jnp.concatenate([up3, down3, up4, down4], 0)
    far_sibling = step(far, 0, 1)

    where = jnp.stack([narrow_index >> 1, narrow_index & 1]).astype(jnp.int32)
    hole = pl.pallas_call(
        hole_kernel,
        out_shape=jax.ShapeDtypeStruct((2, height, LANES), jnp.float32),
        in_specs=[SMEM, HBM] + [VMEM] * 4 + [HBM] * 2,
        out_specs=VMEM,
        scratch_shapes=[
            pltpu.VMEM(pair_integrals.shape, jnp.bfloat16),
            pltpu.VMEM(near.shape, jnp.bfloat16),
            pltpu.VMEM(far.shape, jnp.bfloat16),
            pltpu.SemaphoreType.DMA((3,)),
        ],
        compiler_params=pltpu.CompilerParams(vmem_limit_bytes=50 << 20),
        cost_estimate=pl.CostEstimate(flops=2**30, bytes_accessed=2**22, transcendentals=0),
        name="hole",
    )(
        where,
        pair_integrals,
        occupied_energy.reshape(height, 1),
        virtual_energy.reshape(1, LANES),
        near,
        far,
        near_sibling,
        far_sibling,
    )
    return pl.pallas_call(
        finish_kernel,
        out_shape=jax.ShapeDtypeStruct((height, LANES), jnp.float32),
        in_specs=[VMEM, HBM],
        out_specs=VMEM,
        scratch_shapes=[
            pltpu.VMEM((2, height, LANES), jnp.float32),
            pltpu.SemaphoreType.DMA(()),
        ],
        compiler_params=pltpu.CompilerParams(vmem_limit_bytes=20 << 20),
        cost_estimate=pl.CostEstimate(flops=2**23, bytes_accessed=2**22, transcendentals=0),
        name="finish",
    )(shares, hole)


def solution(mesh):
    placed = (P("narrow", "wide"), P("wide", None), P("narrow", None), P(), P("narrow"), P("wide"))
    return jax.shard_map(
        on_device, mesh=mesh, in_specs=placed, out_specs=P("narrow", "wide"), check_vma=False
    )
```

```python
import jax
import jax.numpy as jnp
from jax import lax
from jax.experimental import pallas as pl
from jax.experimental.pallas import tpu as pltpu
from jax.sharding import PartitionSpec as P

CHUNKS = 16
DEPTH = 32
HOPS = ((0, 0), (1, 0), (3, 0), (0, 1))
ROOM = 80
LANES = 256
CODE_ROWS = 16
STEPS = 256.0
TOP = 32760.0
PER = 2
VMEM = pl.BlockSpec(memory_space=pltpu.VMEM)
HBM = pl.BlockSpec(memory_space=pltpu.HBM)
SMEM = pl.BlockSpec(memory_space=pltpu.SMEM)


def iota(shape, dim):
    return lax.broadcasted_iota(jnp.int32, shape, dim)


def ones_where(mask):
    return jnp.where(mask, 1.0, 0.0)


def bdot(left, right, dims=((1,), (0,))):
    return lax.dot_general(
        left.astype(jnp.bfloat16),
        right.astype(jnp.bfloat16),
        (dims, ((), ())),
        preferred_element_type=jnp.float32,
    )


def count_before(classes):
    member = jnp.concatenate(
        [ones_where(classes[c : c + 1, :] == iota((CHUNKS, LANES), 0)) for c in range(CHUNKS)], 0
    )
    earlier = ones_where(iota((LANES, LANES), 0) < iota((LANES, LANES), 1))
    return member, bdot(member, earlier)


def pick(member, table):
    return jnp.sum((member * table).reshape(CHUNKS, CHUNKS, LANES), axis=1).astype(jnp.int32)


def widen(ref):
    halves = [ref[pl.ds(k, CHUNKS, stride=2), :] for k in range(2)]
    return jnp.concatenate(halves, 1)


def select_kernel(shift, here_ref, index_ref, far_amp_ref, *refs):
    *sent_refs, rank_ref, amp_ref, amp_sem = refs
    fetch = pltpu.make_async_copy(far_amp_ref, amp_ref, amp_sem)
    fetch.start()
    index = widen(index_ref)
    here = here_ref[0]
    owner = jnp.right_shift(index, shift)
    member, within = count_before(owner)
    r, c = iota((LANES, LANES), 0), iota((LANES, LANES), 1)
    ahead = ones_where(((r & 15) == (c & 15)) & (jnp.right_shift(c, 4) < jnp.right_shift(r, 4)))
    base = jnp.sum(bdot(ahead, member), axis=1, keepdims=True)
    rank = pick(member, within + base)
    rank_ref[...] = rank
    middle, depth = rank & 15, jnp.right_shift(rank, 4)
    column = index & ((1 << shift) - 1)
    high, low = jnp.right_shift(column, 6).astype(jnp.float32), (column & 63).astype(jnp.float32)
    lefts, rights = [], []
    for k in range(CHUNKS):
        one = slice(k, k + 1)
        hit = ones_where((depth[one] == iota((DEPTH, LANES), 0)) & (owner[one] == here))
        lefts.append(jnp.concatenate([hit * high[one], hit * low[one]], 0))
        rights.append(ones_where(middle[one] == iota((CHUNKS, LANES), 0)))
    found = bdot(jnp.concatenate(lefts, 1), jnp.concatenate(rights, 1), ((1,), (1,)))
    columns = (found[:DEPTH] * 64.0 + found[DEPTH:]).astype(jnp.int32)
    span = amp_ref.shape[1]
    lane = iota((DEPTH, span), 1)
    order = [j for hop in range(len(HOPS)) for j in range(hop, CHUNKS, len(HOPS))]
    chosen = jnp.concatenate(
        [ones_where(lane == columns[:, j : j + 1]).astype(jnp.bfloat16) for j in order], 0
    )
    fetch.wait()
    got = bdot(chosen, amp_ref[...], ((1,), (1,))).astype(jnp.bfloat16)
    for hop, sent_ref in enumerate(sent_refs):
        sent_ref[...] = got[hop * 4 * DEPTH : (hop + 1) * 4 * DEPTH]


def route_kernel(shift, here_ref, index_ref, rank_ref, kept_ref, *refs):
    forward_ref, settle_ref, stay_ref = refs
    stay_ref[...] = kept_ref[...]
    index, rank, here = widen(index_ref), rank_ref[...], here_ref[0]
    owner = jnp.right_shift(index, shift)
    last, depth = rank & 15, jnp.right_shift(rank, 4)
    hop = rank & 3
    x, y = jnp.right_shift(owner, 2), owner & 3
    for k, (dx, dy) in enumerate(HOPS):
        x, y = jnp.where(hop == k, x + dx, x), jnp.where(hop == k, y + dy, y)
    middle = (x & 3) * 4 + (y & 3)
    member, within = count_before(middle)
    place = pick(member, within)
    source = (hop * (4 * DEPTH) + jnp.right_shift(last, 2) * DEPTH + depth).astype(jnp.float32)
    lane = iota((ROOM, CHUNKS * DEPTH), 1)
    for k in range(CHUNKS):
        one = slice(k, k + 1)
        hit = (place[one] == iota((ROOM, LANES), 0)) & (middle[one] == here)
        row = jnp.sum(jnp.where(hit, source[one], 0.0), axis=1, keepdims=True).astype(jnp.int32)
        forward_ref[k * ROOM : (k + 1) * ROOM, :] = ones_where(lane == row).astype(jnp.bfloat16)
    arrived = (middle * ROOM + place).astype(jnp.float32)
    own = iota((CHUNKS, LANES), 0) == here
    wanted = jnp.sum(jnp.where(own, arrived, 0.0), axis=0, keepdims=True).astype(jnp.int32)
    settle_ref[...] = ones_where(iota((CHUNKS * ROOM, LANES), 0) == wanted).astype(jnp.bfloat16)


def forward_kernel(forward_ref, *refs):
    *come_refs, moved_ref = refs
    arrived = jnp.concatenate([ref[...] for ref in come_refs], 0)
    moved = bdot(forward_ref[...], arrived).astype(jnp.bfloat16)
    moved_ref[...] = moved.reshape(moved_ref.shape)


def settle_kernel(second_ref, settle_ref, after_ref, own_ref):
    del after_ref
    arrived = second_ref[...].reshape(CHUNKS * ROOM, second_ref.shape[2])
    own_ref[...] = bdot(arrived, settle_ref[...], ((0,), (0,))).astype(jnp.bfloat16)


def ladder_kernel(amp_ref, int_ref, after_ref, coded_ref, held_ref, stage_ref, in_sems, out_sems):
    del after_ref
    count = CHUNKS // PER
    height = amp_ref.shape[0]
    width = PER * LANES
    ins, outs = [], []
    for b in range(count):
        ins.append(
            pltpu.make_async_copy(
                int_ref.at[:, pl.ds(b * width, width)], held_ref.at[b], in_sems.at[b]
            )
        )
        ins[b].start()
    for b in range(count):
        ins[b].wait()
        slab = jnp.dot(amp_ref[...], held_ref[b], preferred_element_type=jnp.float32)
        for j in range(PER):
            part = slab[:, j * LANES : (j + 1) * LANES]
            largest = jnp.max(jnp.abs(part), axis=0, keepdims=True)
            code = jnp.ceil(jnp.log2(jnp.maximum(largest, 2.0**-120)) * STEPS) + 1.0
            shrunk = part * jnp.exp2(code * (-1.0 / STEPS)) * TOP
            k = b * PER + j
            stage_ref[k, :height, :] = jnp.round(shrunk).astype(jnp.int32).astype(jnp.int16)
            stage_ref[k, height:, :] = jnp.broadcast_to(
                code.astype(jnp.int32), (CODE_ROWS, LANES)
            ).astype(jnp.int16)
        outs.append(
            pltpu.make_async_copy(
                stage_ref.at[pl.ds(b * PER, PER)],
                coded_ref.at[pl.ds(b * PER, PER)],
                out_sems.at[b],
            )
        )
        outs[b].start()
    for out in outs:
        out.wait()


def either_kernel(core_ref, zero_ref, one_ref, out_ref):
    @pl.when(core_ref[0] == 0)
    def _():
        out_ref[...] = zero_ref[...]

    @pl.when(core_ref[0] != 0)
    def _():
        out_ref[...] = one_ref[...]


def hole_kernel(place_ref, far_pair_ref, occ_ref, virt_ref, near_ref, far_ref, *refs):
    near_sibling_ref, far_sibling_ref, out_ref, pair_ref, sems = refs
    z, core = place_ref[0], place_ref[1]
    rows = near_ref.shape[0] // 5
    blocks = [
        (group, k, chips, which)
        for near, far, which in (
            (near_ref, far_ref, core),
            (near_sibling_ref, far_sibling_ref, 1 - core),
        )
        for group, away in ((near, (0, 1, -1, 2, -2)), (far, (3, -3, 4)))
        for k, chips in enumerate(away)
    ]
    fetches = []
    for slot, (_, _, chips, which) in enumerate(blocks):
        n = jnp.bitwise_and(z - chips + 8, 7) * 2 + which
        columns = far_pair_ref.at[:, pl.ds(pl.multiple_of(n * rows, rows), rows)]
        fetches.append(pltpu.make_async_copy(columns, pair_ref.at[slot], sems.at[slot]))
        fetches[slot].start()
    out_ref[1] = virt_ref[...] - occ_ref[...]
    total = jnp.zeros(out_ref.shape[1:], jnp.float32)
    for slot, (group, k, _, _) in enumerate(blocks):
        fetches[slot].wait()
        block = group[k * rows : (k + 1) * rows]
        total = total + jnp.dot(pair_ref[slot], block, preferred_element_type=jnp.float32)
    out_ref[0] = total


def finish_kernel(far_coded_ref, far_hole_ref, out_ref, coded_ref, hole_ref, sems):
    rows = out_ref.shape[0]
    group = CHUNKS // 4
    fetches = [
        pltpu.make_async_copy(
            far_coded_ref.at[pl.ds(k * group, group)],
            coded_ref.at[pl.ds(k * group, group)],
            sems.at[k],
        )
        for k in range(4)
    ]
    fetches.append(pltpu.make_async_copy(far_hole_ref, hole_ref, sems.at[4]))
    for fetch in fetches:
        fetch.start()
    ladder = jnp.zeros(out_ref.shape, jnp.float32)
    for k in range(CHUNKS):
        if k % group == 0:
            fetches[k // group].wait()
        code = coded_ref[k, rows:, :].astype(jnp.int32).astype(jnp.float32)[:1, :]
        values = coded_ref[k, :rows, :].astype(jnp.int32).astype(jnp.float32)
        ladder = ladder + values * jnp.exp2(code * (1.0 / STEPS))
    fetches[4].wait()
    out_ref[...] = (ladder * (1.0 / TOP) + hole_ref[0]) / hole_ref[1]


def on_device(amplitudes, integrals, pair_integrals, slab_index, occupied_energy, virtual_energy):
    wide_index = lax.axis_index("wide")
    narrow_index = lax.axis_index("narrow")
    height, span = amplitudes.shape
    shift = span.bit_length() - 1
    here = wide_index.astype(jnp.int32).reshape(1)
    index = slab_index.reshape(2 * CHUNKS, LANES // 2)
    core = narrow_index & 1

    def step(value, dz, dc=0, turn=1):
        ring = [
            (z * 2 + c, (z + (turn if c else 1) * dz) % 8 * 2 + (c + dc) % 2)
            for z in range(8)
            for c in range(2)
        ]
        return lax.ppermute(value, "narrow", ring)

    *sent, rank = pl.pallas_call(
        lambda *refs: select_kernel(shift, *refs),
        out_shape=(
            *[jax.ShapeDtypeStruct((4 * DEPTH, height), jnp.bfloat16) for _ in HOPS],
            jax.ShapeDtypeStruct((CHUNKS, LANES), jnp.int32),
        ),
        in_specs=[SMEM, VMEM, HBM],
        out_specs=(VMEM,) * (len(HOPS) + 1),
        scratch_shapes=[pltpu.VMEM((height, span), jnp.bfloat16), pltpu.SemaphoreType.DMA(())],
        compiler_params=pltpu.CompilerParams(vmem_limit_bytes=59 << 20),
        cost_estimate=pl.CostEstimate(flops=2**30, bytes_accessed=2**21, transcendentals=0),
        name="select",
    )(here, index, amplitudes)
    came = [
        lax.ppermute(
            sent[k],
            "wide",
            [(x * 4 + y, (x + dx) % 4 * 4 + (y + dy) % 4) for x in range(4) for y in range(4)],
        )
        for k, (dx, dy) in enumerate(HOPS)
        if k
    ]

    forward, settle, stay = pl.pallas_call(
        lambda *refs: route_kernel(shift, *refs),
        out_shape=(
            jax.ShapeDtypeStruct((CHUNKS * ROOM, CHUNKS * DEPTH), jnp.bfloat16),
            jax.ShapeDtypeStruct((CHUNKS * ROOM, LANES), jnp.bfloat16),
            jax.ShapeDtypeStruct(sent[0].shape, jnp.bfloat16),
        ),
        in_specs=[SMEM, VMEM, VMEM, VMEM],
        out_specs=(VMEM, VMEM, VMEM),
        compiler_params=pltpu.CompilerParams(vmem_limit_bytes=16 << 20),
        cost_estimate=pl.CostEstimate(flops=2**28, bytes_accessed=2**20, transcendentals=0),
        name="route",
    )(here, index, rank, sent[0])

    moved = pl.pallas_call(
        forward_kernel,
        out_shape=jax.ShapeDtypeStruct((CHUNKS, ROOM, height), jnp.bfloat16),
        in_specs=[VMEM] * (len(HOPS) + 1),
        out_specs=VMEM,
        compiler_params=pltpu.CompilerParams(vmem_limit_bytes=8 << 20),
        cost_estimate=pl.CostEstimate(flops=2**28, bytes_accessed=2**20, transcendentals=0),
        name="forward",
    )(forward, stay, *came)
    second = lax.all_to_all(moved, "wide", 0, 0, tiled=True)

    slabs = CHUNKS // PER
    coded = pl.pallas_call(
        ladder_kernel,
        out_shape=jax.ShapeDtypeStruct((CHUNKS, height + CODE_ROWS, LANES), jnp.int16),
        in_specs=[VMEM, HBM, HBM],
        out_specs=HBM,
        scratch_shapes=[
            pltpu.VMEM((slabs, span, PER * LANES), jnp.bfloat16),
            pltpu.VMEM((CHUNKS, height + CODE_ROWS, LANES), jnp.int16),
            pltpu.SemaphoreType.DMA((slabs,)),
            pltpu.SemaphoreType.DMA((slabs,)),
        ],
        compiler_params=pltpu.CompilerParams(vmem_limit_bytes=50 << 20),
        cost_estimate=pl.CostEstimate(
            flops=2 * height * span * CHUNKS * LANES, bytes_accessed=18 * 2**20, transcendentals=0
        ),
        name="ladder",
    )(amplitudes, integrals, moved)
    shares = lax.all_to_all(coded, "wide", 0, 0, tiled=True)

    own = pl.pallas_call(
        settle_kernel,
        out_shape=jax.ShapeDtypeStruct((height, LANES), jnp.bfloat16),
        in_specs=[VMEM, VMEM, HBM],
        out_specs=VMEM,
        compiler_params=pltpu.CompilerParams(vmem_limit_bytes=8 << 20),
        cost_estimate=pl.CostEstimate(flops=2**26, bytes_accessed=2**20, transcendentals=0),
        name="settle",
    )(second, settle, coded)

    up, down, up2, down2 = step(own, 1), step(own, -1), step(own, 2), step(own, -2)
    up3, down3 = step(up2, 1), step(down2, -1)
    two = pl.pallas_call(
        either_kernel,
        out_shape=jax.ShapeDtypeStruct(up2.shape, jnp.bfloat16),
        in_specs=[SMEM, VMEM, VMEM],
        out_specs=VMEM,
        compiler_params=pltpu.CompilerParams(vmem_limit_bytes=4 << 20),
        cost_estimate=pl.CostEstimate(flops=0, bytes_accessed=2**18, transcendentals=0),
        name="either",
    )(core.astype(jnp.int32).reshape(1), up2, down2)
    four = step(two, 2, turn=-1)
    near = jnp.concatenate([own, up, down, up2, down2], 0)
    near_sibling = step(near, 0, 1)
    far = jnp.concatenate([up3, down3, four], 0)
    far_sibling = step(far, 0, 1)

    where = jnp.stack([narrow_index >> 1, core]).astype(jnp.int32)
    hole = pl.pallas_call(
        hole_kernel,
        out_shape=jax.ShapeDtypeStruct((2, height, LANES), jnp.float32),
        in_specs=[SMEM, HBM] + [VMEM] * 6,
        out_specs=VMEM,
        scratch_shapes=[
            pltpu.VMEM((CHUNKS, height, height), jnp.bfloat16),
            pltpu.SemaphoreType.DMA((CHUNKS,)),
        ],
        compiler_params=pltpu.CompilerParams(vmem_limit_bytes=50 << 20),
        cost_estimate=pl.CostEstimate(flops=2**30, bytes_accessed=2**22, transcendentals=0),
        name="hole",
    )(
        where,
        pair_integrals,
        occupied_energy.reshape(height, 1),
        virtual_energy.reshape(1, LANES),
        near,
        far,
        near_sibling,
        far_sibling,
    )
    return pl.pallas_call(
        finish_kernel,
        out_shape=jax.ShapeDtypeStruct((height, LANES), jnp.float32),
        in_specs=[HBM] * 2,
        out_specs=VMEM,
        scratch_shapes=[
            pltpu.VMEM(shares.shape, jnp.int16),
            pltpu.VMEM(hole.shape, jnp.float32),
            pltpu.SemaphoreType.DMA((5,)),
        ],
        compiler_params=pltpu.CompilerParams(vmem_limit_bytes=54 << 20),
        cost_estimate=pl.CostEstimate(flops=2**23, bytes_accessed=2**22, transcendentals=0),
        name="finish",
    )(shares, hole)


def solution(mesh):
    placed = (P("narrow", "wide"), P("wide", None), P("narrow", None), P(), P("narrow"), P("wide"))
    return jax.shard_map(
        on_device, mesh=mesh, in_specs=placed, out_specs=P("narrow", "wide"), check_vma=False
    )
```

```python
import jax
import jax.numpy as jnp
from jax import lax
from jax.experimental import pallas as pl
from jax.experimental.pallas import tpu as pltpu
from jax.sharding import PartitionSpec as P

CHUNKS = 16
DEPTH = 32
HOPS = ((0, 0), (1, 0), (3, 0), (0, 1))
ROOM = 80
LANES = 256
CODE_ROWS = 16
STEPS = 256.0
TOP = 32760.0
PER = 2
VMEM = pl.BlockSpec(memory_space=pltpu.VMEM)
HBM = pl.BlockSpec(memory_space=pltpu.HBM)
SMEM = pl.BlockSpec(memory_space=pltpu.SMEM)


def iota(shape, dim):
    return lax.broadcasted_iota(jnp.int32, shape, dim)


def ones_where(mask):
    return jnp.where(mask, 1.0, 0.0)


def bdot(left, right, dims=((1,), (0,))):
    return lax.dot_general(
        left.astype(jnp.bfloat16),
        right.astype(jnp.bfloat16),
        (dims, ((), ())),
        preferred_element_type=jnp.float32,
    )


def count_before(classes):
    member = jnp.concatenate(
        [ones_where(classes[c : c + 1, :] == iota((CHUNKS, LANES), 0)) for c in range(CHUNKS)], 0
    )
    earlier = ones_where(iota((LANES, LANES), 0) < iota((LANES, LANES), 1))
    return member, bdot(member, earlier)


def pick(member, table):
    return jnp.sum((member * table).reshape(CHUNKS, CHUNKS, LANES), axis=1).astype(jnp.int32)


def widen(ref):
    halves = [ref[pl.ds(k, CHUNKS, stride=2), :] for k in range(2)]
    return jnp.concatenate(halves, 1)


def select_kernel(shift, here_ref, index_ref, far_amp_ref, *refs):
    *sent_refs, rank_ref, amp_ref, amp_sem = refs
    fetch = pltpu.make_async_copy(far_amp_ref, amp_ref, amp_sem)
    fetch.start()
    index = widen(index_ref)
    here = here_ref[0]
    owner = jnp.right_shift(index, shift)
    member, within = count_before(owner)
    r, c = iota((LANES, LANES), 0), iota((LANES, LANES), 1)
    ahead = ones_where(((r & 15) == (c & 15)) & (jnp.right_shift(c, 4) < jnp.right_shift(r, 4)))
    base = jnp.sum(bdot(ahead, member), axis=1, keepdims=True)
    rank = pick(member, within + base)
    rank_ref[...] = rank
    middle, depth = rank & 15, jnp.right_shift(rank, 4)
    column = index & ((1 << shift) - 1)
    high, low = jnp.right_shift(column, 6).astype(jnp.float32), (column & 63).astype(jnp.float32)
    lefts, rights = [], []
    for k in range(CHUNKS):
        one = slice(k, k + 1)
        hit = ones_where((depth[one] == iota((DEPTH, LANES), 0)) & (owner[one] == here))
        lefts.append(jnp.concatenate([hit * high[one], hit * low[one]], 0))
        rights.append(ones_where(middle[one] == iota((CHUNKS, LANES), 0)))
    found = bdot(jnp.concatenate(lefts, 1), jnp.concatenate(rights, 1), ((1,), (1,)))
    columns = (found[:DEPTH] * 64.0 + found[DEPTH:]).astype(jnp.int32)
    span = amp_ref.shape[1]
    lane = iota((DEPTH, span), 1)
    order = [j for hop in range(len(HOPS)) for j in range(hop, CHUNKS, len(HOPS))]
    chosen = jnp.concatenate(
        [ones_where(lane == columns[:, j : j + 1]).astype(jnp.bfloat16) for j in order], 0
    )
    fetch.wait()
    got = bdot(chosen, amp_ref[...], ((1,), (1,))).astype(jnp.bfloat16)
    for hop, sent_ref in enumerate(sent_refs):
        sent_ref[...] = got[hop * 4 * DEPTH : (hop + 1) * 4 * DEPTH]


def route_kernel(shift, here_ref, index_ref, rank_ref, kept_ref, *refs):
    forward_ref, settle_ref, stay_ref = refs
    stay_ref[...] = kept_ref[...]
    index, rank, here = widen(index_ref), rank_ref[...], here_ref[0]
    owner = jnp.right_shift(index, shift)
    last, depth = rank & 15, jnp.right_shift(rank, 4)
    hop = rank & 3
    x, y = jnp.right_shift(owner, 2), owner & 3
    for k, (dx, dy) in enumerate(HOPS):
        x, y = jnp.where(hop == k, x + dx, x), jnp.where(hop == k, y + dy, y)
    middle = (x & 3) * 4 + (y & 3)
    member, within = count_before(middle)
    place = pick(member, within)
    source = (hop * (4 * DEPTH) + jnp.right_shift(last, 2) * DEPTH + depth).astype(jnp.float32)
    lane = iota((ROOM, CHUNKS * DEPTH), 1)
    for k in range(CHUNKS):
        one = slice(k, k + 1)
        hit = (place[one] == iota((ROOM, LANES), 0)) & (middle[one] == here)
        row = jnp.sum(jnp.where(hit, source[one], 0.0), axis=1, keepdims=True).astype(jnp.int32)
        forward_ref[k * ROOM : (k + 1) * ROOM, :] = ones_where(lane == row).astype(jnp.bfloat16)
    arrived = (middle * ROOM + place).astype(jnp.float32)
    own = iota((CHUNKS, LANES), 0) == here
    wanted = jnp.sum(jnp.where(own, arrived, 0.0), axis=0, keepdims=True).astype(jnp.int32)
    settle_ref[...] = ones_where(iota((CHUNKS * ROOM, LANES), 0) == wanted).astype(jnp.bfloat16)


def forward_kernel(forward_ref, *refs):
    *come_refs, moved_ref = refs
    arrived = jnp.concatenate([ref[...] for ref in come_refs], 0)
    moved = bdot(forward_ref[...], arrived).astype(jnp.bfloat16)
    moved_ref[...] = moved.reshape(moved_ref.shape)


def settle_kernel(second_ref, settle_ref, after_ref, own_ref):
    del after_ref
    arrived = second_ref[...].reshape(CHUNKS * ROOM, second_ref.shape[2])
    own_ref[...] = bdot(arrived, settle_ref[...], ((0,), (0,))).astype(jnp.bfloat16)


def ladder_kernel(amp_ref, int_ref, after_ref, coded_ref, held_ref, stage_ref, in_sems, out_sems):
    del after_ref
    count = CHUNKS // PER
    height = amp_ref.shape[0]
    width = PER * LANES
    ins, outs = [], []
    for b in range(count):
        ins.append(
            pltpu.make_async_copy(
                int_ref.at[:, pl.ds(b * width, width)], held_ref.at[b], in_sems.at[b]
            )
        )
        ins[b].start()
    for b in range(count):
        ins[b].wait()
        slab = jnp.dot(amp_ref[...], held_ref[b], preferred_element_type=jnp.float32)
        for j in range(PER):
            part = slab[:, j * LANES : (j + 1) * LANES]
            largest = jnp.max(jnp.abs(part), axis=0, keepdims=True)
            code = jnp.ceil(jnp.log2(jnp.maximum(largest, 2.0**-120)) * STEPS) + 1.0
            shrunk = part * jnp.exp2(code * (-1.0 / STEPS)) * TOP
            k = b * PER + j
            stage_ref[k, :height, :] = jnp.round(shrunk).astype(jnp.int32).astype(jnp.int16)
            stage_ref[k, height:, :] = jnp.broadcast_to(
                code.astype(jnp.int32), (CODE_ROWS, LANES)
            ).astype(jnp.int16)
        outs.append(
            pltpu.make_async_copy(
                stage_ref.at[pl.ds(b * PER, PER)],
                coded_ref.at[pl.ds(b * PER, PER)],
                out_sems.at[b],
            )
        )
        outs[b].start()
    for out in outs:
        out.wait()


def either_kernel(core_ref, zero_ref, one_ref, out_ref):
    @pl.when(core_ref[0] == 0)
    def _():
        out_ref[...] = zero_ref[...]

    @pl.when(core_ref[0] != 0)
    def _():
        out_ref[...] = one_ref[...]


def finish_kernel(place_ref, far_coded_ref, far_pair_ref, occ_ref, virt_ref, *refs):
    *groups, out_ref, coded_ref, pair_ref, coded_sems, pair_sems = refs
    z, core = place_ref[0], place_ref[1]
    rows = out_ref.shape[0]
    piece = CHUNKS // 4
    shares = [
        pltpu.make_async_copy(
            far_coded_ref.at[pl.ds(k * piece, piece)],
            coded_ref.at[pl.ds(k * piece, piece)],
            coded_sems.at[k],
        )
        for k in range(4)
    ]
    chips = (0, 1, -1, 2, -2, 3, -3, 4)
    pairs = []
    for slot in range(2 * len(chips)):
        which = core if slot < len(chips) else 1 - core
        n = jnp.bitwise_and(z - chips[slot % len(chips)] + 8, 7) * 2 + which
        pairs.append(
            pltpu.make_async_copy(
                far_pair_ref.at[:, pl.ds(pl.multiple_of(n * rows, rows), rows)],
                pair_ref.at[:, pl.ds(slot * rows, rows)],
                pair_sems.at[slot],
            )
        )
    for copy in shares + pairs:
        copy.start()
    total = jnp.zeros(out_ref.shape, jnp.float32)
    for k in range(CHUNKS):
        if k % piece == 0:
            shares[k // piece].wait()
        code = coded_ref[k, rows:, :].astype(jnp.int32).astype(jnp.float32)[:1, :]
        values = coded_ref[k, :rows, :].astype(jnp.int32).astype(jnp.float32)
        total = total + values * jnp.exp2(code * (1.0 / STEPS))
    total = total * (1.0 / TOP)
    start = 0
    for group_ref in groups:
        count = group_ref.shape[0] // rows
        for copy in pairs[start : start + count]:
            copy.wait()
        total = total + jnp.dot(
            pair_ref[:, start * rows : (start + count) * rows],
            group_ref[...],
            preferred_element_type=jnp.float32,
        )
        start += count
    out_ref[...] = total / (virt_ref[...] - occ_ref[...])


def on_device(amplitudes, integrals, pair_integrals, slab_index, occupied_energy, virtual_energy):
    wide_index = lax.axis_index("wide")
    narrow_index = lax.axis_index("narrow")
    height, span = amplitudes.shape
    shift = span.bit_length() - 1
    here = wide_index.astype(jnp.int32).reshape(1)
    index = slab_index.reshape(2 * CHUNKS, LANES // 2)
    core = narrow_index & 1

    def step(value, dz, dc=0, turn=1):
        ring = [
            (z * 2 + c, (z + (turn if c else 1) * dz) % 8 * 2 + (c + dc) % 2)
            for z in range(8)
            for c in range(2)
        ]
        return lax.ppermute(value, "narrow", ring)

    *sent, rank = pl.pallas_call(
        lambda *refs: select_kernel(shift, *refs),
        out_shape=(
            *[jax.ShapeDtypeStruct((4 * DEPTH, height), jnp.bfloat16) for _ in HOPS],
            jax.ShapeDtypeStruct((CHUNKS, LANES), jnp.int32),
        ),
        in_specs=[SMEM, VMEM, HBM],
        out_specs=(VMEM,) * (len(HOPS) + 1),
        scratch_shapes=[pltpu.VMEM((height, span), jnp.bfloat16), pltpu.SemaphoreType.DMA(())],
        compiler_params=pltpu.CompilerParams(vmem_limit_bytes=59 << 20),
        cost_estimate=pl.CostEstimate(flops=2**30, bytes_accessed=2**21, transcendentals=0),
        name="select",
    )(here, index, amplitudes)
    came = [
        lax.ppermute(
            sent[k],
            "wide",
            [(x * 4 + y, (x + dx) % 4 * 4 + (y + dy) % 4) for x in range(4) for y in range(4)],
        )
        for k, (dx, dy) in enumerate(HOPS)
        if k
    ]

    forward, settle, stay = pl.pallas_call(
        lambda *refs: route_kernel(shift, *refs),
        out_shape=(
            jax.ShapeDtypeStruct((CHUNKS * ROOM, CHUNKS * DEPTH), jnp.bfloat16),
            jax.ShapeDtypeStruct((CHUNKS * ROOM, LANES), jnp.bfloat16),
            jax.ShapeDtypeStruct(sent[0].shape, jnp.bfloat16),
        ),
        in_specs=[SMEM, VMEM, VMEM, VMEM],
        out_specs=(VMEM, VMEM, VMEM),
        compiler_params=pltpu.CompilerParams(vmem_limit_bytes=16 << 20),
        cost_estimate=pl.CostEstimate(flops=2**28, bytes_accessed=2**20, transcendentals=0),
        name="route",
    )(here, index, rank, sent[0])

    moved = pl.pallas_call(
        forward_kernel,
        out_shape=jax.ShapeDtypeStruct((CHUNKS, ROOM, height), jnp.bfloat16),
        in_specs=[VMEM] * (len(HOPS) + 1),
        out_specs=VMEM,
        compiler_params=pltpu.CompilerParams(vmem_limit_bytes=8 << 20),
        cost_estimate=pl.CostEstimate(flops=2**28, bytes_accessed=2**20, transcendentals=0),
        name="forward",
    )(forward, stay, *came)
    second = lax.all_to_all(moved, "wide", 0, 0, tiled=True)

    slabs = CHUNKS // PER
    coded = pl.pallas_call(
        ladder_kernel,
        out_shape=jax.ShapeDtypeStruct((CHUNKS, height + CODE_ROWS, LANES), jnp.int16),
        in_specs=[VMEM, HBM, HBM],
        out_specs=HBM,
        scratch_shapes=[
            pltpu.VMEM((slabs, span, PER * LANES), jnp.bfloat16),
            pltpu.VMEM((CHUNKS, height + CODE_ROWS, LANES), jnp.int16),
            pltpu.SemaphoreType.DMA((slabs,)),
            pltpu.SemaphoreType.DMA((slabs,)),
        ],
        compiler_params=pltpu.CompilerParams(vmem_limit_bytes=50 << 20),
        cost_estimate=pl.CostEstimate(
            flops=2 * height * span * CHUNKS * LANES, bytes_accessed=18 * 2**20, transcendentals=0
        ),
        name="ladder",
    )(amplitudes, integrals, moved)
    shares = lax.all_to_all(coded, "wide", 0, 0, tiled=True)

    own = pl.pallas_call(
        settle_kernel,
        out_shape=jax.ShapeDtypeStruct((height, LANES), jnp.bfloat16),
        in_specs=[VMEM, VMEM, HBM],
        out_specs=VMEM,
        compiler_params=pltpu.CompilerParams(vmem_limit_bytes=8 << 20),
        cost_estimate=pl.CostEstimate(flops=2**26, bytes_accessed=2**20, transcendentals=0),
        name="settle",
    )(second, settle, coded)

    up, down, up2, down2 = step(own, 1), step(own, -1), step(own, 2), step(own, -2)
    up3, down3 = step(up2, 1), step(down2, -1)
    two = pl.pallas_call(
        either_kernel,
        out_shape=jax.ShapeDtypeStruct(up2.shape, jnp.bfloat16),
        in_specs=[SMEM, VMEM, VMEM],
        out_specs=VMEM,
        compiler_params=pltpu.CompilerParams(vmem_limit_bytes=4 << 20),
        cost_estimate=pl.CostEstimate(flops=0, bytes_accessed=2**18, transcendentals=0),
        name="either",
    )(core.astype(jnp.int32).reshape(1), up2, down2)
    four = step(two, 2, turn=-1)
    near = jnp.concatenate([own, up, down, up2, down2], 0)
    near_sibling = step(near, 0, 1)
    far = jnp.concatenate([up3, down3, four], 0)
    far_sibling = step(far, 0, 1)

    where = jnp.stack([narrow_index >> 1, core]).astype(jnp.int32)
    return pl.pallas_call(
        finish_kernel,
        out_shape=jax.ShapeDtypeStruct((height, LANES), jnp.float32),
        in_specs=[SMEM, HBM, HBM] + [VMEM] * 6,
        out_specs=VMEM,
        scratch_shapes=[
            pltpu.VMEM(shares.shape, jnp.int16),
            pltpu.VMEM(pair_integrals.shape, jnp.bfloat16),
            pltpu.SemaphoreType.DMA((4,)),
            pltpu.SemaphoreType.DMA((CHUNKS,)),
        ],
        compiler_params=pltpu.CompilerParams(vmem_limit_bytes=51 << 20),
        cost_estimate=pl.CostEstimate(flops=2**30, bytes_accessed=2**23, transcendentals=0),
        name="finish",
    )(
        where,
        shares,
        pair_integrals,
        occupied_energy.reshape(height, 1),
        virtual_energy.reshape(1, LANES),
        near,
        far,
        near_sibling,
        far_sibling,
    )


def solution(mesh):
    placed = (P("narrow", "wide"), P("wide", None), P("narrow", None), P(), P("narrow"), P("wide"))
    return jax.shard_map(
        on_device, mesh=mesh, in_specs=placed, out_specs=P("narrow", "wide"), check_vma=False
    )
```

```python
import jax
import jax.numpy as jnp
from jax import lax
from jax.experimental import pallas as pl
from jax.experimental.pallas import tpu as pltpu
from jax.sharding import PartitionSpec as P

CHUNKS = 16
DEPTH = 32
HOPS = ((0, 0), (1, 0), (3, 0), (0, 1))
ROOM = 80
LANES = 256
CODE_ROWS = 16
STEPS = 256.0
TOP = 32760.0
PIECES = 4
PER = 2
VMEM = pl.BlockSpec(memory_space=pltpu.VMEM)
HBM = pl.BlockSpec(memory_space=pltpu.HBM)
SMEM = pl.BlockSpec(memory_space=pltpu.SMEM)


def iota(shape, dim):
    return lax.broadcasted_iota(jnp.int32, shape, dim)


def ones_where(mask):
    return jnp.where(mask, 1.0, 0.0)


def bdot(left, right, dims=((1,), (0,))):
    return lax.dot_general(
        left.astype(jnp.bfloat16),
        right.astype(jnp.bfloat16),
        (dims, ((), ())),
        preferred_element_type=jnp.float32,
    )


def count_before(classes):
    member = jnp.concatenate(
        [ones_where(classes[c : c + 1, :] == iota((CHUNKS, LANES), 0)) for c in range(CHUNKS)], 0
    )
    earlier = ones_where(iota((LANES, LANES), 0) < iota((LANES, LANES), 1))
    return member, bdot(member, earlier)


def pick(member, table):
    return jnp.sum((member * table).reshape(CHUNKS, CHUNKS, LANES), axis=1).astype(jnp.int32)


def widen(ref):
    halves = [ref[pl.ds(k, CHUNKS, stride=2), :] for k in range(2)]
    return jnp.concatenate(halves, 1)


def select_kernel(shift, here_ref, index_ref, far_amp_ref, *refs):
    *sent_refs, rank_ref, amp_ref, amp_sem = refs
    fetch = pltpu.make_async_copy(far_amp_ref, amp_ref, amp_sem)
    fetch.start()
    index = widen(index_ref)
    here = here_ref[0]
    owner = jnp.right_shift(index, shift)
    member, within = count_before(owner)
    r, c = iota((LANES, LANES), 0), iota((LANES, LANES), 1)
    ahead = ones_where(((r & 15) == (c & 15)) & (jnp.right_shift(c, 4) < jnp.right_shift(r, 4)))
    base = jnp.sum(bdot(ahead, member), axis=1, keepdims=True)
    rank = pick(member, within + base)
    rank_ref[...] = rank
    middle, depth = rank & 15, jnp.right_shift(rank, 4)
    column = index & ((1 << shift) - 1)
    high, low = jnp.right_shift(column, 6).astype(jnp.float32), (column & 63).astype(jnp.float32)
    lefts, rights = [], []
    for k in range(CHUNKS):
        one = slice(k, k + 1)
        hit = ones_where((depth[one] == iota((DEPTH, LANES), 0)) & (owner[one] == here))
        lefts.append(jnp.concatenate([hit * high[one], hit * low[one]], 0))
        rights.append(ones_where(middle[one] == iota((CHUNKS, LANES), 0)))
    found = bdot(jnp.concatenate(lefts, 1), jnp.concatenate(rights, 1), ((1,), (1,)))
    columns = (found[:DEPTH] * 64.0 + found[DEPTH:]).astype(jnp.int32)
    span = amp_ref.shape[1]
    lane = iota((DEPTH, span), 1)
    order = [j for hop in range(len(HOPS)) for j in range(hop, CHUNKS, len(HOPS))]
    chosen = jnp.concatenate(
        [ones_where(lane == columns[:, j : j + 1]).astype(jnp.bfloat16) for j in order], 0
    )
    fetch.wait()
    got = bdot(chosen, amp_ref[...], ((1,), (1,))).astype(jnp.bfloat16)
    for hop, sent_ref in enumerate(sent_refs):
        sent_ref[...] = got[hop * 4 * DEPTH : (hop + 1) * 4 * DEPTH]


def route_kernel(shift, here_ref, index_ref, rank_ref, kept_ref, *refs):
    forward_ref, settle_ref, stay_ref = refs
    stay_ref[...] = kept_ref[...]
    index, rank, here = widen(index_ref), rank_ref[...], here_ref[0]
    owner = jnp.right_shift(index, shift)
    last, depth = rank & 15, jnp.right_shift(rank, 4)
    hop = rank & 3
    x, y = jnp.right_shift(owner, 2), owner & 3
    for k, (dx, dy) in enumerate(HOPS):
        x, y = jnp.where(hop == k, x + dx, x), jnp.where(hop == k, y + dy, y)
    middle = (x & 3) * 4 + (y & 3)
    member, within = count_before(middle)
    place = pick(member, within)
    source = (hop * (4 * DEPTH) + jnp.right_shift(last, 2) * DEPTH + depth).astype(jnp.float32)
    lane = iota((ROOM, CHUNKS * DEPTH), 1)
    for k in range(CHUNKS):
        one = slice(k, k + 1)
        hit = (place[one] == iota((ROOM, LANES), 0)) & (middle[one] == here)
        row = jnp.sum(jnp.where(hit, source[one], 0.0), axis=1, keepdims=True).astype(jnp.int32)
        forward_ref[k * ROOM : (k + 1) * ROOM, :] = ones_where(lane == row).astype(jnp.bfloat16)
    arrived = (middle * ROOM + place).astype(jnp.float32)
    own = iota((CHUNKS, LANES), 0) == here
    wanted = jnp.sum(jnp.where(own, arrived, 0.0), axis=0, keepdims=True).astype(jnp.int32)
    settle_ref[...] = ones_where(iota((CHUNKS * ROOM, LANES), 0) == wanted).astype(jnp.bfloat16)


def forward_kernel(forward_ref, *refs):
    *come_refs, moved_ref = refs
    arrived = jnp.concatenate([ref[...] for ref in come_refs], 0)
    moved = bdot(forward_ref[...], arrived).astype(jnp.bfloat16)
    moved_ref[...] = moved.reshape(moved_ref.shape)


def settle_kernel(second_ref, settle_ref, after_ref, own_ref):
    del after_ref
    arrived = second_ref[...].reshape(CHUNKS * ROOM, second_ref.shape[2])
    own_ref[...] = bdot(arrived, settle_ref[...], ((0,), (0,))).astype(jnp.bfloat16)


def ladder_kernel(amp_ref, int_ref, after_ref, coded_ref, held_ref, stage_ref, in_sems, out_sems):
    del after_ref
    count = CHUNKS // PER
    height = amp_ref.shape[0]
    width = PER * LANES
    ins, outs = [], []
    for b in range(count):
        ins.append(
            pltpu.make_async_copy(
                int_ref.at[:, pl.ds(b * width, width)], held_ref.at[b], in_sems.at[b]
            )
        )
        ins[b].start()
    for b in range(count):
        ins[b].wait()
        slab = jnp.dot(amp_ref[...], held_ref[b], preferred_element_type=jnp.float32)
        for j in range(PER):
            part = slab[:, j * LANES : (j + 1) * LANES]
            largest = jnp.max(jnp.abs(part), axis=0, keepdims=True)
            code = jnp.ceil(jnp.log2(jnp.maximum(largest, 2.0**-120)) * STEPS) + 1.0
            shrunk = part * jnp.exp2(code * (-1.0 / STEPS)) * TOP
            k = b * PER + j
            stage_ref[k, :height, :] = jnp.round(shrunk).astype(jnp.int32).astype(jnp.int16)
            stage_ref[k, height:, :] = jnp.broadcast_to(
                code.astype(jnp.int32), (CODE_ROWS, LANES)
            ).astype(jnp.int16)
        outs.append(
            pltpu.make_async_copy(
                stage_ref.at[pl.ds(b * PER, PER)],
                coded_ref.at[pl.ds(b * PER, PER)],
                out_sems.at[b],
            )
        )
        outs[b].start()
    for out in outs:
        out.wait()


def either_kernel(core_ref, zero_ref, one_ref, out_ref):
    @pl.when(core_ref[0] == 0)
    def _():
        out_ref[...] = zero_ref[...]

    @pl.when(core_ref[0] != 0)
    def _():
        out_ref[...] = one_ref[...]


def finish_kernel(place_ref, far_pair_ref, far_coded_ref, occ_ref, virt_ref, *refs):
    *groups, out_ref, pair_ref, coded_ref, ordered_ref, sems = refs
    piece = CHUNKS // PIECES
    fetches = [pltpu.make_async_copy(far_pair_ref, pair_ref, sems.at[PIECES])]
    for k in range(PIECES):
        some = pl.ds(k * piece, piece)
        fetches.append(
            pltpu.make_async_copy(far_coded_ref.at[some], coded_ref.at[some], sems.at[k])
        )
    for fetch in fetches:
        fetch.start()
    z, core = place_ref[0], place_ref[1]
    rows = out_ref.shape[0]
    chips = (0, 1, -1, 2, -2, 3, -3, 4)
    slot = 0
    for group_ref in groups:
        for k in range(group_ref.shape[0] // rows):
            which = core if slot < len(chips) else 1 - core
            n = jnp.bitwise_and(z - chips[slot % len(chips)] + 8, 7) * 2 + which
            held = pl.ds(pl.multiple_of(n * rows, rows), rows)
            ordered_ref[held, :] = group_ref[k * rows : (k + 1) * rows, :]
            slot += 1
    fetches[0].wait()
    hole = jnp.dot(pair_ref[...], ordered_ref[...], preferred_element_type=jnp.float32)
    total = jnp.zeros(out_ref.shape, jnp.float32)
    for k in range(CHUNKS):
        if k % piece == 0:
            fetches[1 + k // piece].wait()
        code = coded_ref[k, rows:, :].astype(jnp.int32).astype(jnp.float32)[:1, :]
        values = coded_ref[k, :rows, :].astype(jnp.int32).astype(jnp.float32)
        total = total + values * jnp.exp2(code * (1.0 / STEPS))
    out_ref[...] = (total * (1.0 / TOP) + hole) / (virt_ref[...] - occ_ref[...])


def on_device(amplitudes, integrals, pair_integrals, slab_index, occupied_energy, virtual_energy):
    wide_index = lax.axis_index("wide")
    narrow_index = lax.axis_index("narrow")
    height, span = amplitudes.shape
    shift = span.bit_length() - 1
    here = wide_index.astype(jnp.int32).reshape(1)
    index = slab_index.reshape(2 * CHUNKS, LANES // 2)
    core = narrow_index & 1

    def step(value, dz, dc=0, turn=1):
        ring = [
            (z * 2 + c, (z + (turn if c else 1) * dz) % 8 * 2 + (c + dc) % 2)
            for z in range(8)
            for c in range(2)
        ]
        return lax.ppermute(value, "narrow", ring)

    *sent, rank = pl.pallas_call(
        lambda *refs: select_kernel(shift, *refs),
        out_shape=(
            *[jax.ShapeDtypeStruct((4 * DEPTH, height), jnp.bfloat16) for _ in HOPS],
            jax.ShapeDtypeStruct((CHUNKS, LANES), jnp.int32),
        ),
        in_specs=[SMEM, VMEM, HBM],
        out_specs=(VMEM,) * (len(HOPS) + 1),
        scratch_shapes=[pltpu.VMEM((height, span), jnp.bfloat16), pltpu.SemaphoreType.DMA(())],
        compiler_params=pltpu.CompilerParams(vmem_limit_bytes=59 << 20),
        cost_estimate=pl.CostEstimate(flops=2**30, bytes_accessed=2**21, transcendentals=0),
        name="select",
    )(here, index, amplitudes)
    came = [
        lax.ppermute(
            sent[k],
            "wide",
            [(x * 4 + y, (x + dx) % 4 * 4 + (y + dy) % 4) for x in range(4) for y in range(4)],
        )
        for k, (dx, dy) in enumerate(HOPS)
        if k
    ]

    forward, settle, stay = pl.pallas_call(
        lambda *refs: route_kernel(shift, *refs),
        out_shape=(
            jax.ShapeDtypeStruct((CHUNKS * ROOM, CHUNKS * DEPTH), jnp.bfloat16),
            jax.ShapeDtypeStruct((CHUNKS * ROOM, LANES), jnp.bfloat16),
            jax.ShapeDtypeStruct(sent[0].shape, jnp.bfloat16),
        ),
        in_specs=[SMEM, VMEM, VMEM, VMEM],
        out_specs=(VMEM, VMEM, VMEM),
        compiler_params=pltpu.CompilerParams(vmem_limit_bytes=16 << 20),
        cost_estimate=pl.CostEstimate(flops=2**28, bytes_accessed=2**20, transcendentals=0),
        name="route",
    )(here, index, rank, sent[0])

    moved = pl.pallas_call(
        forward_kernel,
        out_shape=jax.ShapeDtypeStruct((CHUNKS, ROOM, height), jnp.bfloat16),
        in_specs=[VMEM] * (len(HOPS) + 1),
        out_specs=VMEM,
        compiler_params=pltpu.CompilerParams(vmem_limit_bytes=8 << 20),
        cost_estimate=pl.CostEstimate(flops=2**28, bytes_accessed=2**20, transcendentals=0),
        name="forward",
    )(forward, stay, *came)
    second = lax.all_to_all(moved, "wide", 0, 0, tiled=True)

    slabs = CHUNKS // PER
    coded = pl.pallas_call(
        ladder_kernel,
        out_shape=jax.ShapeDtypeStruct((CHUNKS, height + CODE_ROWS, LANES), jnp.int16),
        in_specs=[VMEM, HBM, HBM],
        out_specs=HBM,
        scratch_shapes=[
            pltpu.VMEM((slabs, span, PER * LANES), jnp.bfloat16),
            pltpu.VMEM((CHUNKS, height + CODE_ROWS, LANES), jnp.int16),
            pltpu.SemaphoreType.DMA((slabs,)),
            pltpu.SemaphoreType.DMA((slabs,)),
        ],
        compiler_params=pltpu.CompilerParams(vmem_limit_bytes=50 << 20),
        cost_estimate=pl.CostEstimate(
            flops=2 * height * span * CHUNKS * LANES, bytes_accessed=18 * 2**20, transcendentals=0
        ),
        name="ladder",
    )(amplitudes, integrals, moved)
    shares = lax.all_to_all(coded, "wide", 0, 0, tiled=True)

    own = pl.pallas_call(
        settle_kernel,
        out_shape=jax.ShapeDtypeStruct((height, LANES), jnp.bfloat16),
        in_specs=[VMEM, VMEM, HBM],
        out_specs=VMEM,
        compiler_params=pltpu.CompilerParams(vmem_limit_bytes=8 << 20),
        cost_estimate=pl.CostEstimate(flops=2**26, bytes_accessed=2**20, transcendentals=0),
        name="settle",
    )(second, settle, coded)

    up, down, up2, down2 = step(own, 1), step(own, -1), step(own, 2), step(own, -2)
    up3, down3 = step(up2, 1), step(down2, -1)
    two = pl.pallas_call(
        either_kernel,
        out_shape=jax.ShapeDtypeStruct(up2.shape, jnp.bfloat16),
        in_specs=[SMEM, VMEM, VMEM],
        out_specs=VMEM,
        compiler_params=pltpu.CompilerParams(vmem_limit_bytes=4 << 20),
        cost_estimate=pl.CostEstimate(flops=0, bytes_accessed=2**18, transcendentals=0),
        name="either",
    )(core.astype(jnp.int32).reshape(1), up2, down2)
    four = step(two, 2, turn=-1)
    near = jnp.concatenate([own, up, down, up2, down2], 0)
    near_sibling = step(near, 0, 1)
    far = jnp.concatenate([up3, down3, four], 0)
    far_sibling = step(far, 0, 1)

    where = jnp.stack([narrow_index >> 1, core]).astype(jnp.int32)
    return pl.pallas_call(
        finish_kernel,
        out_shape=jax.ShapeDtypeStruct((height, LANES), jnp.float32),
        in_specs=[SMEM, HBM, HBM] + [VMEM] * 6,
        out_specs=VMEM,
        scratch_shapes=[
            pltpu.VMEM(pair_integrals.shape, jnp.bfloat16),
            pltpu.VMEM(shares.shape, jnp.int16),
            pltpu.VMEM((CHUNKS * height, LANES), jnp.bfloat16),
            pltpu.SemaphoreType.DMA((PIECES + 1,)),
        ],
        compiler_params=pltpu.CompilerParams(vmem_limit_bytes=51 << 20),
        cost_estimate=pl.CostEstimate(flops=2**30, bytes_accessed=2**23, transcendentals=0),
        name="finish",
    )(
        where,
        pair_integrals,
        shares,
        occupied_energy.reshape(height, 1),
        virtual_energy.reshape(1, LANES),
        near,
        far,
        near_sibling,
        far_sibling,
    )


def solution(mesh):
    placed = (P("narrow", "wide"), P("wide", None), P("narrow", None), P(), P("narrow"), P("wide"))
    return jax.shard_map(
        on_device, mesh=mesh, in_specs=placed, out_specs=P("narrow", "wide"), check_vma=False
    )
```

```python
import jax
import jax.numpy as jnp
from jax import lax
from jax.experimental import pallas as pl
from jax.experimental.pallas import tpu as pltpu
from jax.sharding import PartitionSpec as P

CHUNKS = 16
DEPTH = 32
HOPS = ((0, 0), (1, 0), (3, 0), (0, 1))
ROOM = 80
LANES = 256
CODE_ROWS = 16
STEPS = 256.0
TOP = 32760.0
PIECES = 4
PER = 2
VMEM = pl.BlockSpec(memory_space=pltpu.VMEM)
HBM = pl.BlockSpec(memory_space=pltpu.HBM)
SMEM = pl.BlockSpec(memory_space=pltpu.SMEM)


def iota(shape, dim):
    return lax.broadcasted_iota(jnp.int32, shape, dim)


def ones_where(mask):
    return jnp.where(mask, 1.0, 0.0)


def bdot(left, right, dims=((1,), (0,))):
    return lax.dot_general(
        left.astype(jnp.bfloat16),
        right.astype(jnp.bfloat16),
        (dims, ((), ())),
        preferred_element_type=jnp.float32,
    )


def count_before(classes):
    member = jnp.concatenate(
        [ones_where(classes[c : c + 1, :] == iota((CHUNKS, LANES), 0)) for c in range(CHUNKS)], 0
    )
    earlier = ones_where(iota((LANES, LANES), 0) < iota((LANES, LANES), 1))
    return member, bdot(member, earlier)


def pick(member, table):
    return jnp.sum((member * table).reshape(CHUNKS, CHUNKS, LANES), axis=1).astype(jnp.int32)


def widen(ref):
    halves = [ref[pl.ds(k, CHUNKS, stride=2), :] for k in range(2)]
    return jnp.concatenate(halves, 1)


def select_kernel(shift, here_ref, index_ref, far_amp_ref, *refs):
    *sent_refs, rank_ref, amp_ref, amp_sem = refs
    fetch = pltpu.make_async_copy(far_amp_ref, amp_ref, amp_sem)
    fetch.start()
    index = widen(index_ref)
    here = here_ref[0]
    owner = jnp.right_shift(index, shift)
    member, within = count_before(owner)
    r, c = iota((LANES, LANES), 0), iota((LANES, LANES), 1)
    ahead = ones_where(((r & 15) == (c & 15)) & (jnp.right_shift(c, 4) < jnp.right_shift(r, 4)))
    base = jnp.sum(bdot(ahead, member), axis=1, keepdims=True)
    rank = pick(member, within + base)
    rank_ref[...] = rank
    middle, depth = rank & 15, jnp.right_shift(rank, 4)
    column = index & ((1 << shift) - 1)
    high, low = jnp.right_shift(column, 6).astype(jnp.float32), (column & 63).astype(jnp.float32)
    lefts, rights = [], []
    for k in range(CHUNKS):
        one = slice(k, k + 1)
        hit = ones_where((depth[one] == iota((DEPTH, LANES), 0)) & (owner[one] == here))
        lefts.append(jnp.concatenate([hit * high[one], hit * low[one]], 0))
        rights.append(ones_where(middle[one] == iota((CHUNKS, LANES), 0)))
    found = bdot(jnp.concatenate(lefts, 1), jnp.concatenate(rights, 1), ((1,), (1,)))
    columns = (found[:DEPTH] * 64.0 + found[DEPTH:]).astype(jnp.int32)
    span = amp_ref.shape[1]
    lane = iota((DEPTH, span), 1)
    order = [j for hop in range(len(HOPS)) for j in range(hop, CHUNKS, len(HOPS))]
    chosen = jnp.concatenate(
        [ones_where(lane == columns[:, j : j + 1]).astype(jnp.bfloat16) for j in order], 0
    )
    fetch.wait()
    got = bdot(chosen, amp_ref[...], ((1,), (1,))).astype(jnp.bfloat16)
    for hop, sent_ref in enumerate(sent_refs):
        sent_ref[...] = got[hop * 4 * DEPTH : (hop + 1) * 4 * DEPTH]


def route_kernel(shift, here_ref, index_ref, rank_ref, kept_ref, *refs):
    forward_ref, settle_ref, stay_ref = refs
    stay_ref[...] = kept_ref[...]
    index, rank, here = widen(index_ref), rank_ref[...], here_ref[0]
    owner = jnp.right_shift(index, shift)
    last, depth = rank & 15, jnp.right_shift(rank, 4)
    hop = rank & 3
    x, y = jnp.right_shift(owner, 2), owner & 3
    for k, (dx, dy) in enumerate(HOPS):
        x, y = jnp.where(hop == k, x + dx, x), jnp.where(hop == k, y + dy, y)
    middle = (x & 3) * 4 + (y & 3)
    member, within = count_before(middle)
    place = pick(member, within)
    source = (hop * (4 * DEPTH) + jnp.right_shift(last, 2) * DEPTH + depth).astype(jnp.float32)
    lane = iota((ROOM, CHUNKS * DEPTH), 1)
    for k in range(CHUNKS):
        one = slice(k, k + 1)
        hit = (place[one] == iota((ROOM, LANES), 0)) & (middle[one] == here)
        row = jnp.sum(jnp.where(hit, source[one], 0.0), axis=1, keepdims=True).astype(jnp.int32)
        forward_ref[k * ROOM : (k + 1) * ROOM, :] = ones_where(lane == row).astype(jnp.bfloat16)
    arrived = (middle * ROOM + place).astype(jnp.float32)
    own = iota((CHUNKS, LANES), 0) == here
    wanted = jnp.sum(jnp.where(own, arrived, 0.0), axis=0, keepdims=True).astype(jnp.int32)
    settle_ref[...] = ones_where(iota((CHUNKS * ROOM, LANES), 0) == wanted).astype(jnp.bfloat16)


def forward_kernel(forward_ref, *refs):
    *come_refs, moved_ref = refs
    arrived = jnp.concatenate([ref[...] for ref in come_refs], 0)
    moved = bdot(forward_ref[...], arrived).astype(jnp.bfloat16)
    moved_ref[...] = moved.reshape(moved_ref.shape)


def settle_kernel(second_ref, settle_ref, after_ref, own_ref):
    del after_ref
    arrived = second_ref[...].reshape(CHUNKS * ROOM, second_ref.shape[2])
    own_ref[...] = bdot(arrived, settle_ref[...], ((0,), (0,))).astype(jnp.bfloat16)


def ladder_kernel(amp_ref, int_ref, after_ref, coded_ref, held_ref, stage_ref, in_sems, out_sems):
    del after_ref
    count = CHUNKS // PER
    height = amp_ref.shape[0]
    width = PER * LANES
    ins, outs = [], []
    for b in range(count):
        ins.append(
            pltpu.make_async_copy(
                int_ref.at[:, pl.ds(b * width, width)], held_ref.at[b], in_sems.at[b]
            )
        )
        ins[b].start()
    for b in range(count):
        ins[b].wait()
        slab = jnp.dot(amp_ref[...], held_ref[b], preferred_element_type=jnp.float32)
        for j in range(PER):
            part = slab[:, j * LANES : (j + 1) * LANES]
            largest = jnp.max(jnp.abs(part), axis=0, keepdims=True)
            code = jnp.ceil(jnp.log2(jnp.maximum(largest, 2.0**-120)) * STEPS) + 1.0
            shrunk = part * jnp.exp2(code * (-1.0 / STEPS)) * TOP
            k = b * PER + j
            stage_ref[k, :height, :] = jnp.round(shrunk).astype(jnp.int32).astype(jnp.int16)
            stage_ref[k, height:, :] = jnp.broadcast_to(
                code.astype(jnp.int32), (CODE_ROWS, LANES)
            ).astype(jnp.int16)
        outs.append(
            pltpu.make_async_copy(
                stage_ref.at[pl.ds(b * PER, PER)],
                coded_ref.at[pl.ds(b * PER, PER)],
                out_sems.at[b],
            )
        )
        outs[b].start()
    for out in outs:
        out.wait()


def either_kernel(core_ref, zero_ref, one_ref, out_ref):
    @pl.when(core_ref[0] == 0)
    def _():
        out_ref[...] = zero_ref[...]

    @pl.when(core_ref[0] != 0)
    def _():
        out_ref[...] = one_ref[...]


def finish_kernel(place_ref, pair_ref, far_coded_ref, occ_ref, virt_ref, *refs):
    *groups, out_ref, coded_ref, ordered_ref, coded_sems, block_sems = refs
    z, core = place_ref[0], place_ref[1]
    rows = out_ref.shape[0]
    chips = (0, 1, -1, 2, -2, 3, -3, 4)
    blocks = []
    for group_ref in groups:
        for k in range(group_ref.shape[0] // rows):
            slot = len(blocks)
            which = core if slot < len(chips) else 1 - core
            n = jnp.bitwise_and(z - chips[slot % len(chips)] + 8, 7) * 2 + which
            held = pl.ds(pl.multiple_of(n * rows, rows), rows)
            blocks.append(
                pltpu.make_async_copy(
                    group_ref.at[pl.ds(k * rows, rows)], ordered_ref.at[held], block_sems.at[slot]
                )
            )
    piece = CHUNKS // PIECES
    shares = []
    for k in range(PIECES):
        some = pl.ds(k * piece, piece)
        shares.append(
            pltpu.make_async_copy(far_coded_ref.at[some], coded_ref.at[some], coded_sems.at[k])
        )
    for copy in blocks + shares:
        copy.start()
    for copy in blocks:
        copy.wait()
    hole = jnp.dot(pair_ref[...], ordered_ref[...], preferred_element_type=jnp.float32)
    total = jnp.zeros(out_ref.shape, jnp.float32)
    for k in range(CHUNKS):
        if k % piece == 0:
            shares[k // piece].wait()
        code = coded_ref[k, rows:, :].astype(jnp.int32).astype(jnp.float32)[:1, :]
        values = coded_ref[k, :rows, :].astype(jnp.int32).astype(jnp.float32)
        total = total + values * jnp.exp2(code * (1.0 / STEPS))
    out_ref[...] = (total * (1.0 / TOP) + hole) / (virt_ref[...] - occ_ref[...])


def on_device(amplitudes, integrals, pair_integrals, slab_index, occupied_energy, virtual_energy):
    wide_index = lax.axis_index("wide")
    narrow_index = lax.axis_index("narrow")
    height, span = amplitudes.shape
    shift = span.bit_length() - 1
    here = wide_index.astype(jnp.int32).reshape(1)
    index = slab_index.reshape(2 * CHUNKS, LANES // 2)
    core = narrow_index & 1

    def step(value, dz, dc=0, turn=1):
        ring = [
            (z * 2 + c, (z + (turn if c else 1) * dz) % 8 * 2 + (c + dc) % 2)
            for z in range(8)
            for c in range(2)
        ]
        return lax.ppermute(value, "narrow", ring)

    *sent, rank = pl.pallas_call(
        lambda *refs: select_kernel(shift, *refs),
        out_shape=(
            *[jax.ShapeDtypeStruct((4 * DEPTH, height), jnp.bfloat16) for _ in HOPS],
            jax.ShapeDtypeStruct((CHUNKS, LANES), jnp.int32),
        ),
        in_specs=[SMEM, VMEM, HBM],
        out_specs=(VMEM,) * (len(HOPS) + 1),
        scratch_shapes=[pltpu.VMEM((height, span), jnp.bfloat16), pltpu.SemaphoreType.DMA(())],
        compiler_params=pltpu.CompilerParams(vmem_limit_bytes=59 << 20),
        cost_estimate=pl.CostEstimate(flops=2**30, bytes_accessed=2**21, transcendentals=0),
        name="select",
    )(here, index, amplitudes)
    came = [
        lax.ppermute(
            sent[k],
            "wide",
            [(x * 4 + y, (x + dx) % 4 * 4 + (y + dy) % 4) for x in range(4) for y in range(4)],
        )
        for k, (dx, dy) in enumerate(HOPS)
        if k
    ]

    forward, settle, stay = pl.pallas_call(
        lambda *refs: route_kernel(shift, *refs),
        out_shape=(
            jax.ShapeDtypeStruct((CHUNKS * ROOM, CHUNKS * DEPTH), jnp.bfloat16),
            jax.ShapeDtypeStruct((CHUNKS * ROOM, LANES), jnp.bfloat16),
            jax.ShapeDtypeStruct(sent[0].shape, jnp.bfloat16),
        ),
        in_specs=[SMEM, VMEM, VMEM, VMEM],
        out_specs=(VMEM, VMEM, VMEM),
        compiler_params=pltpu.CompilerParams(vmem_limit_bytes=16 << 20),
        cost_estimate=pl.CostEstimate(flops=2**28, bytes_accessed=2**20, transcendentals=0),
        name="route",
    )(here, index, rank, sent[0])

    moved = pl.pallas_call(
        forward_kernel,
        out_shape=jax.ShapeDtypeStruct((CHUNKS, ROOM, height), jnp.bfloat16),
        in_specs=[VMEM] * (len(HOPS) + 1),
        out_specs=VMEM,
        compiler_params=pltpu.CompilerParams(vmem_limit_bytes=8 << 20),
        cost_estimate=pl.CostEstimate(flops=2**28, bytes_accessed=2**20, transcendentals=0),
        name="forward",
    )(forward, stay, *came)
    second = lax.all_to_all(moved, "wide", 0, 0, tiled=True)

    slabs = CHUNKS // PER
    coded = pl.pallas_call(
        ladder_kernel,
        out_shape=jax.ShapeDtypeStruct((CHUNKS, height + CODE_ROWS, LANES), jnp.int16),
        in_specs=[VMEM, HBM, HBM],
        out_specs=HBM,
        scratch_shapes=[
            pltpu.VMEM((slabs, span, PER * LANES), jnp.bfloat16),
            pltpu.VMEM((CHUNKS, height + CODE_ROWS, LANES), jnp.int16),
            pltpu.SemaphoreType.DMA((slabs,)),
            pltpu.SemaphoreType.DMA((slabs,)),
        ],
        compiler_params=pltpu.CompilerParams(vmem_limit_bytes=50 << 20),
        cost_estimate=pl.CostEstimate(
            flops=2 * height * span * CHUNKS * LANES, bytes_accessed=18 * 2**20, transcendentals=0
        ),
        name="ladder",
    )(amplitudes, integrals, moved)
    shares = lax.all_to_all(coded, "wide", 0, 0, tiled=True)

    own = pl.pallas_call(
        settle_kernel,
        out_shape=jax.ShapeDtypeStruct((height, LANES), jnp.bfloat16),
        in_specs=[VMEM, VMEM, HBM],
        out_specs=VMEM,
        compiler_params=pltpu.CompilerParams(vmem_limit_bytes=8 << 20),
        cost_estimate=pl.CostEstimate(flops=2**26, bytes_accessed=2**20, transcendentals=0),
        name="settle",
    )(second, settle, coded)

    up, down, up2, down2 = step(own, 1), step(own, -1), step(own, 2), step(own, -2)
    up3, down3 = step(up2, 1), step(down2, -1)
    two = pl.pallas_call(
        either_kernel,
        out_shape=jax.ShapeDtypeStruct(up2.shape, jnp.bfloat16),
        in_specs=[SMEM, VMEM, VMEM],
        out_specs=VMEM,
        compiler_params=pltpu.CompilerParams(vmem_limit_bytes=4 << 20),
        cost_estimate=pl.CostEstimate(flops=0, bytes_accessed=2**18, transcendentals=0),
        name="either",
    )(core.astype(jnp.int32).reshape(1), up2, down2)
    four = step(two, 2, turn=-1)
    near = jnp.concatenate([own, up, down, up2, down2], 0)
    near_sibling = step(near, 0, 1)
    far = jnp.concatenate([up3, down3, four], 0)
    far_sibling = step(far, 0, 1)

    where = jnp.stack([narrow_index >> 1, core]).astype(jnp.int32)
    return pl.pallas_call(
        finish_kernel,
        out_shape=jax.ShapeDtypeStruct((height, LANES), jnp.float32),
        in_specs=[SMEM, VMEM, HBM, VMEM, VMEM] + [HBM] * 4,
        out_specs=VMEM,
        scratch_shapes=[
            pltpu.VMEM(shares.shape, jnp.int16),
            pltpu.VMEM((CHUNKS * height, LANES), jnp.bfloat16),
            pltpu.SemaphoreType.DMA((PIECES,)),
            pltpu.SemaphoreType.DMA((CHUNKS,)),
        ],
        compiler_params=pltpu.CompilerParams(vmem_limit_bytes=48 << 20),
        cost_estimate=pl.CostEstimate(flops=2**30, bytes_accessed=2**23, transcendentals=0),
        name="finish",
    )(
        where,
        pair_integrals,
        shares,
        occupied_energy.reshape(height, 1),
        virtual_energy.reshape(1, LANES),
        near,
        far,
        near_sibling,
        far_sibling,
    )


def solution(mesh):
    placed = (P("narrow", "wide"), P("wide", None), P("narrow", None), P(), P("narrow"), P("wide"))
    return jax.shard_map(
        on_device, mesh=mesh, in_specs=placed, out_specs=P("narrow", "wide"), check_vma=False
    )
```

```python
import jax
import jax.numpy as jnp
from jax import lax
from jax.experimental import pallas as pl
from jax.experimental.pallas import tpu as pltpu
from jax.sharding import PartitionSpec as P

CHUNKS = 16
DEPTH = 32
HOPS = ((0, 0), (1, 0), (3, 0), (0, 1))
ROOM = 80
LANES = 256
CODE_ROWS = 16
STEPS = 256.0
TOP = 32760.0
PIECES = 2
PER = 2
VMEM = pl.BlockSpec(memory_space=pltpu.VMEM)
HBM = pl.BlockSpec(memory_space=pltpu.HBM)
SMEM = pl.BlockSpec(memory_space=pltpu.SMEM)


def iota(shape, dim):
    return lax.broadcasted_iota(jnp.int32, shape, dim)


def ones_where(mask):
    return jnp.where(mask, 1.0, 0.0)


def bdot(left, right, dims=((1,), (0,))):
    return lax.dot_general(
        left.astype(jnp.bfloat16),
        right.astype(jnp.bfloat16),
        (dims, ((), ())),
        preferred_element_type=jnp.float32,
    )


def count_before(classes):
    member = jnp.concatenate(
        [ones_where(classes[c : c + 1, :] == iota((CHUNKS, LANES), 0)) for c in range(CHUNKS)], 0
    )
    earlier = ones_where(iota((LANES, LANES), 0) < iota((LANES, LANES), 1))
    return member, bdot(member, earlier)


def pick(member, table):
    return jnp.sum((member * table).reshape(CHUNKS, CHUNKS, LANES), axis=1).astype(jnp.int32)


def widen(ref):
    halves = [ref[pl.ds(k, CHUNKS, stride=2), :] for k in range(2)]
    return jnp.concatenate(halves, 1)


def select_kernel(shift, here_ref, index_ref, far_amp_ref, *refs):
    *sent_refs, rank_ref, amp_ref, amp_sem = refs
    fetch = pltpu.make_async_copy(far_amp_ref, amp_ref, amp_sem)
    fetch.start()
    index = widen(index_ref)
    here = here_ref[0]
    owner = jnp.right_shift(index, shift)
    member, within = count_before(owner)
    r, c = iota((LANES, LANES), 0), iota((LANES, LANES), 1)
    ahead = ones_where(((r & 15) == (c & 15)) & (jnp.right_shift(c, 4) < jnp.right_shift(r, 4)))
    base = jnp.sum(bdot(ahead, member), axis=1, keepdims=True)
    rank = pick(member, within + base)
    rank_ref[...] = rank
    middle, depth = rank & 15, jnp.right_shift(rank, 4)
    column = index & ((1 << shift) - 1)
    high, low = jnp.right_shift(column, 6).astype(jnp.float32), (column & 63).astype(jnp.float32)
    lefts, rights = [], []
    for k in range(CHUNKS):
        one = slice(k, k + 1)
        hit = ones_where((depth[one] == iota((DEPTH, LANES), 0)) & (owner[one] == here))
        lefts.append(jnp.concatenate([hit * high[one], hit * low[one]], 0))
        rights.append(ones_where(middle[one] == iota((CHUNKS, LANES), 0)))
    found = bdot(jnp.concatenate(lefts, 1), jnp.concatenate(rights, 1), ((1,), (1,)))
    columns = (found[:DEPTH] * 64.0 + found[DEPTH:]).astype(jnp.int32)
    span = amp_ref.shape[1]
    lane = iota((DEPTH, span), 1)
    order = [j for hop in range(len(HOPS)) for j in range(hop, CHUNKS, len(HOPS))]
    chosen = jnp.concatenate(
        [ones_where(lane == columns[:, j : j + 1]).astype(jnp.bfloat16) for j in order], 0
    )
    fetch.wait()
    got = bdot(chosen, amp_ref[...], ((1,), (1,))).astype(jnp.bfloat16)
    for hop, sent_ref in enumerate(sent_refs):
        sent_ref[...] = got[hop * 4 * DEPTH : (hop + 1) * 4 * DEPTH]


def route_kernel(shift, here_ref, index_ref, rank_ref, kept_ref, *refs):
    forward_ref, settle_ref, stay_ref = refs
    stay_ref[...] = kept_ref[...]
    index, rank, here = widen(index_ref), rank_ref[...], here_ref[0]
    owner = jnp.right_shift(index, shift)
    last, depth = rank & 15, jnp.right_shift(rank, 4)
    hop = rank & 3
    x, y = jnp.right_shift(owner, 2), owner & 3
    for k, (dx, dy) in enumerate(HOPS):
        x, y = jnp.where(hop == k, x + dx, x), jnp.where(hop == k, y + dy, y)
    middle = (x & 3) * 4 + (y & 3)
    member, within = count_before(middle)
    place = pick(member, within)
    source = (hop * (4 * DEPTH) + jnp.right_shift(last, 2) * DEPTH + depth).astype(jnp.float32)
    lane = iota((ROOM, CHUNKS * DEPTH), 1)
    for k in range(CHUNKS):
        one = slice(k, k + 1)
        hit = (place[one] == iota((ROOM, LANES), 0)) & (middle[one] == here)
        row = jnp.sum(jnp.where(hit, source[one], 0.0), axis=1, keepdims=True).astype(jnp.int32)
        forward_ref[k * ROOM : (k + 1) * ROOM, :] = ones_where(lane == row).astype(jnp.bfloat16)
    arrived = (middle * ROOM + place).astype(jnp.float32)
    own = iota((CHUNKS, LANES), 0) == here
    wanted = jnp.sum(jnp.where(own, arrived, 0.0), axis=0, keepdims=True).astype(jnp.int32)
    settle_ref[...] = ones_where(iota((CHUNKS * ROOM, LANES), 0) == wanted).astype(jnp.bfloat16)


def forward_kernel(forward_ref, *refs):
    *come_refs, moved_ref = refs
    arrived = jnp.concatenate([ref[...] for ref in come_refs], 0)
    moved = bdot(forward_ref[...], arrived).astype(jnp.bfloat16)
    moved_ref[...] = moved.reshape(moved_ref.shape)


def settle_kernel(second_ref, settle_ref, after_ref, own_ref):
    del after_ref
    arrived = second_ref[...].reshape(CHUNKS * ROOM, second_ref.shape[2])
    own_ref[...] = bdot(arrived, settle_ref[...], ((0,), (0,))).astype(jnp.bfloat16)


def ladder_kernel(amp_ref, int_ref, after_ref, coded_ref, held_ref, stage_ref, in_sems, out_sems):
    del after_ref
    count = CHUNKS // PER
    height = amp_ref.shape[0]
    width = PER * LANES
    ins, outs = [], []
    for b in range(count):
        ins.append(
            pltpu.make_async_copy(
                int_ref.at[:, pl.ds(b * width, width)], held_ref.at[b], in_sems.at[b]
            )
        )
        ins[b].start()
    for b in range(count):
        ins[b].wait()
        slab = jnp.dot(amp_ref[...], held_ref[b], preferred_element_type=jnp.float32)
        for j in range(PER):
            part = slab[:, j * LANES : (j + 1) * LANES]
            largest = jnp.max(jnp.abs(part), axis=0, keepdims=True)
            code = jnp.ceil(jnp.log2(jnp.maximum(largest, 2.0**-120)) * STEPS) + 1.0
            shrunk = part * jnp.exp2(code * (-1.0 / STEPS)) * TOP
            k = b * PER + j
            stage_ref[k, :height, :] = jnp.round(shrunk).astype(jnp.int32).astype(jnp.int16)
            stage_ref[k, height:, :] = jnp.broadcast_to(
                code.astype(jnp.int32), (CODE_ROWS, LANES)
            ).astype(jnp.int16)
        outs.append(
            pltpu.make_async_copy(
                stage_ref.at[pl.ds(b * PER, PER)],
                coded_ref.at[pl.ds(b * PER, PER)],
                out_sems.at[b],
            )
        )
        outs[b].start()
    for out in outs:
        out.wait()


def either_kernel(core_ref, zero_ref, one_ref, out_ref):
    @pl.when(core_ref[0] == 0)
    def _():
        out_ref[...] = zero_ref[...]

    @pl.when(core_ref[0] != 0)
    def _():
        out_ref[...] = one_ref[...]


def finish_kernel(
    place_ref, pair_ref, far_coded_ref, occ_ref, virt_ref, near_ref, far_ref, *refs
):
    *away_refs, out_ref, coded_ref, near_sibling_ref, far_sibling_ref, ordered_ref, sems = refs
    piece = CHUNKS // PIECES
    siblings = [
        pltpu.make_async_copy(away_refs[0], near_sibling_ref, sems.at[PIECES]),
        pltpu.make_async_copy(away_refs[1], far_sibling_ref, sems.at[PIECES + 1]),
    ]
    shares = []
    for k in range(PIECES):
        some = pl.ds(k * piece, piece)
        shares.append(
            pltpu.make_async_copy(far_coded_ref.at[some], coded_ref.at[some], sems.at[k])
        )
    for copy in siblings + shares:
        copy.start()
    z, core = place_ref[0], place_ref[1]
    rows = out_ref.shape[0]
    chips = (0, 1, -1, 2, -2, 3, -3, 4)
    slot = 0
    for group_ref in (near_ref, far_ref, near_sibling_ref, far_sibling_ref):
        if group_ref is near_sibling_ref:
            for copy in siblings:
                copy.wait()
        for k in range(group_ref.shape[0] // rows):
            which = core if slot < len(chips) else 1 - core
            n = jnp.bitwise_and(z - chips[slot % len(chips)] + 8, 7) * 2 + which
            held = pl.ds(pl.multiple_of(n * rows, rows), rows)
            ordered_ref[held, :] = group_ref[k * rows : (k + 1) * rows, :]
            slot += 1
    hole = jnp.dot(pair_ref[...], ordered_ref[...], preferred_element_type=jnp.float32)
    total = jnp.zeros(out_ref.shape, jnp.float32)
    for k in range(CHUNKS):
        if k % piece == 0:
            shares[k // piece].wait()
        code = coded_ref[k, rows:, :].astype(jnp.int32).astype(jnp.float32)[:1, :]
        values = coded_ref[k, :rows, :].astype(jnp.int32).astype(jnp.float32)
        total = total + values * jnp.exp2(code * (1.0 / STEPS))
    out_ref[...] = (total * (1.0 / TOP) + hole) / (virt_ref[...] - occ_ref[...])


def on_device(amplitudes, integrals, pair_integrals, slab_index, occupied_energy, virtual_energy):
    wide_index = lax.axis_index("wide")
    narrow_index = lax.axis_index("narrow")
    height, span = amplitudes.shape
    shift = span.bit_length() - 1
    here = wide_index.astype(jnp.int32).reshape(1)
    index = slab_index.reshape(2 * CHUNKS, LANES // 2)
    core = narrow_index & 1

    def step(value, dz, dc=0, turn=1):
        ring = [
            (z * 2 + c, (z + (turn if c else 1) * dz) % 8 * 2 + (c + dc) % 2)
            for z in range(8)
            for c in range(2)
        ]
        return lax.ppermute(value, "narrow", ring)

    *sent, rank = pl.pallas_call(
        lambda *refs: select_kernel(shift, *refs),
        out_shape=(
            *[jax.ShapeDtypeStruct((4 * DEPTH, height), jnp.bfloat16) for _ in HOPS],
            jax.ShapeDtypeStruct((CHUNKS, LANES), jnp.int32),
        ),
        in_specs=[SMEM, VMEM, HBM],
        out_specs=(VMEM,) * (len(HOPS) + 1),
        scratch_shapes=[pltpu.VMEM((height, span), jnp.bfloat16), pltpu.SemaphoreType.DMA(())],
        compiler_params=pltpu.CompilerParams(vmem_limit_bytes=59 << 20),
        cost_estimate=pl.CostEstimate(flops=2**30, bytes_accessed=2**21, transcendentals=0),
        name="select",
    )(here, index, amplitudes)
    came = [
        lax.ppermute(
            sent[k],
            "wide",
            [(x * 4 + y, (x + dx) % 4 * 4 + (y + dy) % 4) for x in range(4) for y in range(4)],
        )
        for k, (dx, dy) in enumerate(HOPS)
        if k
    ]

    forward, settle, stay = pl.pallas_call(
        lambda *refs: route_kernel(shift, *refs),
        out_shape=(
            jax.ShapeDtypeStruct((CHUNKS * ROOM, CHUNKS * DEPTH), jnp.bfloat16),
            jax.ShapeDtypeStruct((CHUNKS * ROOM, LANES), jnp.bfloat16),
            jax.ShapeDtypeStruct(sent[0].shape, jnp.bfloat16),
        ),
        in_specs=[SMEM, VMEM, VMEM, VMEM],
        out_specs=(VMEM, VMEM, VMEM),
        compiler_params=pltpu.CompilerParams(vmem_limit_bytes=16 << 20),
        cost_estimate=pl.CostEstimate(flops=2**28, bytes_accessed=2**20, transcendentals=0),
        name="route",
    )(here, index, rank, sent[0])

    moved = pl.pallas_call(
        forward_kernel,
        out_shape=jax.ShapeDtypeStruct((CHUNKS, ROOM, height), jnp.bfloat16),
        in_specs=[VMEM] * (len(HOPS) + 1),
        out_specs=VMEM,
        compiler_params=pltpu.CompilerParams(vmem_limit_bytes=8 << 20),
        cost_estimate=pl.CostEstimate(flops=2**28, bytes_accessed=2**20, transcendentals=0),
        name="forward",
    )(forward, stay, *came)
    second = lax.all_to_all(moved, "wide", 0, 0, tiled=True)

    slabs = CHUNKS // PER
    coded = pl.pallas_call(
        ladder_kernel,
        out_shape=jax.ShapeDtypeStruct((CHUNKS, height + CODE_ROWS, LANES), jnp.int16),
        in_specs=[VMEM, HBM, HBM],
        out_specs=HBM,
        scratch_shapes=[
            pltpu.VMEM((slabs, span, PER * LANES), jnp.bfloat16),
            pltpu.VMEM((CHUNKS, height + CODE_ROWS, LANES), jnp.int16),
            pltpu.SemaphoreType.DMA((slabs,)),
            pltpu.SemaphoreType.DMA((slabs,)),
        ],
        compiler_params=pltpu.CompilerParams(vmem_limit_bytes=50 << 20),
        cost_estimate=pl.CostEstimate(
            flops=2 * height * span * CHUNKS * LANES, bytes_accessed=18 * 2**20, transcendentals=0
        ),
        name="ladder",
    )(amplitudes, integrals, moved)
    shares = lax.all_to_all(coded, "wide", 0, 0, tiled=True)

    own = pl.pallas_call(
        settle_kernel,
        out_shape=jax.ShapeDtypeStruct((height, LANES), jnp.bfloat16),
        in_specs=[VMEM, VMEM, HBM],
        out_specs=VMEM,
        compiler_params=pltpu.CompilerParams(vmem_limit_bytes=8 << 20),
        cost_estimate=pl.CostEstimate(flops=2**26, bytes_accessed=2**20, transcendentals=0),
        name="settle",
    )(second, settle, coded)

    up, down, up2, down2 = step(own, 1), step(own, -1), step(own, 2), step(own, -2)
    up3, down3 = step(up2, 1), step(down2, -1)
    two = pl.pallas_call(
        either_kernel,
        out_shape=jax.ShapeDtypeStruct(up2.shape, jnp.bfloat16),
        in_specs=[SMEM, VMEM, VMEM],
        out_specs=VMEM,
        compiler_params=pltpu.CompilerParams(vmem_limit_bytes=4 << 20),
        cost_estimate=pl.CostEstimate(flops=0, bytes_accessed=2**18, transcendentals=0),
        name="either",
    )(core.astype(jnp.int32).reshape(1), up2, down2)
    four = step(two, 2, turn=-1)
    near = jnp.concatenate([own, up, down, up2, down2], 0)
    near_sibling = step(near, 0, 1)
    far = jnp.concatenate([up3, down3, four], 0)
    far_sibling = step(far, 0, 1)

    where = jnp.stack([narrow_index >> 1, core]).astype(jnp.int32)
    return pl.pallas_call(
        finish_kernel,
        out_shape=jax.ShapeDtypeStruct((height, LANES), jnp.float32),
        in_specs=[SMEM, VMEM, HBM, VMEM, VMEM, VMEM, VMEM, HBM, HBM],
        out_specs=VMEM,
        scratch_shapes=[
            pltpu.VMEM(shares.shape, jnp.int16),
            pltpu.VMEM(near.shape, jnp.bfloat16),
            pltpu.VMEM(far.shape, jnp.bfloat16),
            pltpu.VMEM((CHUNKS * height, LANES), jnp.bfloat16),
            pltpu.SemaphoreType.DMA((PIECES + 2,)),
        ],
        compiler_params=pltpu.CompilerParams(vmem_limit_bytes=48 << 20),
        cost_estimate=pl.CostEstimate(flops=2**30, bytes_accessed=2**23, transcendentals=0),
        name="finish",
    )(
        where,
        pair_integrals,
        shares,
        occupied_energy.reshape(height, 1),
        virtual_energy.reshape(1, LANES),
        near,
        far,
        near_sibling,
        far_sibling,
    )


def solution(mesh):
    placed = (P("narrow", "wide"), P("wide", None), P("narrow", None), P(), P("narrow"), P("wide"))
    return jax.shard_map(
        on_device, mesh=mesh, in_specs=placed, out_specs=P("narrow", "wide"), check_vma=False
    )
```

```python
import jax
import jax.numpy as jnp
from jax import lax
from jax.experimental import pallas as pl
from jax.experimental.pallas import tpu as pltpu
from jax.sharding import PartitionSpec as P

CHUNKS = 16
DEPTH = 32
HOPS = ((0, 0), (1, 0), (3, 0), (0, 1))
ROOM = 80
LANES = 256
CODE_ROWS = 16
STEPS = 256.0
TOP = 32760.0
PIECES = 2
PER = 2
VMEM = pl.BlockSpec(memory_space=pltpu.VMEM)
HBM = pl.BlockSpec(memory_space=pltpu.HBM)
SMEM = pl.BlockSpec(memory_space=pltpu.SMEM)


def iota(shape, dim):
    return lax.broadcasted_iota(jnp.int32, shape, dim)


def ones_where(mask):
    return jnp.where(mask, 1.0, 0.0)


def bdot(left, right, dims=((1,), (0,))):
    return lax.dot_general(
        left.astype(jnp.bfloat16),
        right.astype(jnp.bfloat16),
        (dims, ((), ())),
        preferred_element_type=jnp.float32,
    )


def count_before(classes):
    member = jnp.concatenate(
        [ones_where(classes[c : c + 1, :] == iota((CHUNKS, LANES), 0)) for c in range(CHUNKS)], 0
    )
    earlier = ones_where(iota((LANES, LANES), 0) < iota((LANES, LANES), 1))
    return member, bdot(member, earlier)


def pick(member, table):
    return jnp.sum((member * table).reshape(CHUNKS, CHUNKS, LANES), axis=1).astype(jnp.int32)


def rank_in_owner(owner):
    member, within = count_before(owner)
    r, c = iota((LANES, LANES), 0), iota((LANES, LANES), 1)
    ahead = ones_where(((r & 15) == (c & 15)) & (jnp.right_shift(c, 4) < jnp.right_shift(r, 4)))
    base = jnp.sum(bdot(ahead, member), axis=1, keepdims=True)
    return pick(member, within + base)


def widen(ref):
    halves = [ref[pl.ds(k, CHUNKS, stride=2), :] for k in range(2)]
    return jnp.concatenate(halves, 1)


def select_kernel(shift, here_ref, index_ref, far_amp_ref, *refs):
    *sent_refs, amp_ref, amp_sem = refs
    fetch = pltpu.make_async_copy(far_amp_ref, amp_ref, amp_sem)
    fetch.start()
    index = widen(index_ref)
    here = here_ref[0]
    owner = jnp.right_shift(index, shift)
    rank = rank_in_owner(owner)
    middle, depth = rank & 15, jnp.right_shift(rank, 4)
    column = index & ((1 << shift) - 1)
    high, low = jnp.right_shift(column, 6).astype(jnp.float32), (column & 63).astype(jnp.float32)
    lefts, rights = [], []
    for k in range(CHUNKS):
        one = slice(k, k + 1)
        hit = ones_where((depth[one] == iota((DEPTH, LANES), 0)) & (owner[one] == here))
        lefts.append(jnp.concatenate([hit * high[one], hit * low[one]], 0))
        rights.append(ones_where(middle[one] == iota((CHUNKS, LANES), 0)))
    found = bdot(jnp.concatenate(lefts, 1), jnp.concatenate(rights, 1), ((1,), (1,)))
    columns = (found[:DEPTH] * 64.0 + found[DEPTH:]).astype(jnp.int32)
    span = amp_ref.shape[1]
    lane = iota((DEPTH, span), 1)
    order = [j for hop in range(len(HOPS)) for j in range(hop, CHUNKS, len(HOPS))]
    chosen = jnp.concatenate(
        [ones_where(lane == columns[:, j : j + 1]).astype(jnp.bfloat16) for j in order], 0
    )
    fetch.wait()
    got = bdot(chosen, amp_ref[...], ((1,), (1,))).astype(jnp.bfloat16)
    for hop, sent_ref in enumerate(sent_refs):
        sent_ref[...] = got[hop * 4 * DEPTH : (hop + 1) * 4 * DEPTH]


def route_kernel(shift, here_ref, index_ref, kept_ref, *refs):
    forward_ref, settle_ref, stay_ref = refs
    stay_ref[...] = kept_ref[...]
    index, here = widen(index_ref), here_ref[0]
    owner = jnp.right_shift(index, shift)
    rank = rank_in_owner(owner)
    last, depth = rank & 15, jnp.right_shift(rank, 4)
    hop = rank & 3
    x, y = jnp.right_shift(owner, 2), owner & 3
    for k, (dx, dy) in enumerate(HOPS):
        x, y = jnp.where(hop == k, x + dx, x), jnp.where(hop == k, y + dy, y)
    middle = (x & 3) * 4 + (y & 3)
    member, within = count_before(middle)
    place = pick(member, within)
    source = (hop * (4 * DEPTH) + jnp.right_shift(last, 2) * DEPTH + depth).astype(jnp.float32)
    lane = iota((ROOM, CHUNKS * DEPTH), 1)
    for k in range(CHUNKS):
        one = slice(k, k + 1)
        hit = (place[one] == iota((ROOM, LANES), 0)) & (middle[one] == here)
        row = jnp.sum(jnp.where(hit, source[one], 0.0), axis=1, keepdims=True).astype(jnp.int32)
        forward_ref[k * ROOM : (k + 1) * ROOM, :] = ones_where(lane == row).astype(jnp.bfloat16)
    arrived = (middle * ROOM + place).astype(jnp.float32)
    own = iota((CHUNKS, LANES), 0) == here
    wanted = jnp.sum(jnp.where(own, arrived, 0.0), axis=0, keepdims=True).astype(jnp.int32)
    settle_ref[...] = ones_where(iota((CHUNKS * ROOM, LANES), 0) == wanted).astype(jnp.bfloat16)


def forward_kernel(forward_ref, *refs):
    *come_refs, moved_ref = refs
    arrived = jnp.concatenate([ref[...] for ref in come_refs], 0)
    moved = bdot(forward_ref[...], arrived).astype(jnp.bfloat16)
    moved_ref[...] = moved.reshape(moved_ref.shape)


def settle_kernel(second_ref, settle_ref, after_ref, own_ref):
    del after_ref
    arrived = second_ref[...].reshape(CHUNKS * ROOM, second_ref.shape[2])
    own_ref[...] = bdot(arrived, settle_ref[...], ((0,), (0,))).astype(jnp.bfloat16)


def ladder_kernel(amp_ref, int_ref, after_ref, coded_ref, held_ref, stage_ref, in_sems, out_sems):
    del after_ref
    count = CHUNKS // PER
    height = amp_ref.shape[0]
    width = PER * LANES
    ins, outs = [], []
    for b in range(count):
        ins.append(
            pltpu.make_async_copy(
                int_ref.at[:, pl.ds(b * width, width)], held_ref.at[b], in_sems.at[b]
            )
        )
        ins[b].start()
    for b in range(count):
        ins[b].wait()
        slab = jnp.dot(amp_ref[...], held_ref[b], preferred_element_type=jnp.float32)
        for j in range(PER):
            part = slab[:, j * LANES : (j + 1) * LANES]
            largest = jnp.max(jnp.abs(part), axis=0, keepdims=True)
            code = jnp.ceil(jnp.log2(jnp.maximum(largest, 2.0**-120)) * STEPS) + 1.0
            shrunk = part * jnp.exp2(code * (-1.0 / STEPS)) * TOP
            k = b * PER + j
            stage_ref[k, :height, :] = jnp.round(shrunk).astype(jnp.int32).astype(jnp.int16)
            stage_ref[k, height:, :] = jnp.broadcast_to(
                code.astype(jnp.int32), (CODE_ROWS, LANES)
            ).astype(jnp.int16)
        outs.append(
            pltpu.make_async_copy(
                stage_ref.at[pl.ds(b * PER, PER)],
                coded_ref.at[pl.ds(b * PER, PER)],
                out_sems.at[b],
            )
        )
        outs[b].start()
    for out in outs:
        out.wait()


def either_kernel(core_ref, zero_ref, one_ref, out_ref):
    @pl.when(core_ref[0] == 0)
    def _():
        out_ref[...] = zero_ref[...]

    @pl.when(core_ref[0] != 0)
    def _():
        out_ref[...] = one_ref[...]


def finish_kernel(
    place_ref, pair_ref, far_coded_ref, occ_ref, virt_ref, near_ref, far_ref, *refs
):
    *away_refs, out_ref, coded_ref, near_sibling_ref, far_sibling_ref, ordered_ref, sems = refs
    piece = CHUNKS // PIECES
    siblings = [
        pltpu.make_async_copy(away_refs[0], near_sibling_ref, sems.at[PIECES]),
        pltpu.make_async_copy(away_refs[1], far_sibling_ref, sems.at[PIECES + 1]),
    ]
    shares = []
    for k in range(PIECES):
        some = pl.ds(k * piece, piece)
        shares.append(
            pltpu.make_async_copy(far_coded_ref.at[some], coded_ref.at[some], sems.at[k])
        )
    for copy in siblings + shares:
        copy.start()
    z, core = place_ref[0], place_ref[1]
    rows = out_ref.shape[0]
    chips = (0, 1, -1, 2, -2, 3, -3, 4)
    slot = 0
    for group_ref in (near_ref, far_ref, near_sibling_ref, far_sibling_ref):
        if group_ref is near_sibling_ref:
            for copy in siblings:
                copy.wait()
        for k in range(group_ref.shape[0] // rows):
            which = core if slot < len(chips) else 1 - core
            n = jnp.bitwise_and(z - chips[slot % len(chips)] + 8, 7) * 2 + which
            held = pl.ds(pl.multiple_of(n * rows, rows), rows)
            ordered_ref[held, :] = group_ref[k * rows : (k + 1) * rows, :]
            slot += 1
    hole = jnp.dot(pair_ref[...], ordered_ref[...], preferred_element_type=jnp.float32)
    total = jnp.zeros(out_ref.shape, jnp.float32)
    for k in range(CHUNKS):
        if k % piece == 0:
            shares[k // piece].wait()
        code = coded_ref[k, rows:, :].astype(jnp.int32).astype(jnp.float32)[:1, :]
        values = coded_ref[k, :rows, :].astype(jnp.int32).astype(jnp.float32)
        total = total + values * jnp.exp2(code * (1.0 / STEPS))
    out_ref[...] = (total * (1.0 / TOP) + hole) / (virt_ref[...] - occ_ref[...])


def on_device(amplitudes, integrals, pair_integrals, slab_index, occupied_energy, virtual_energy):
    wide_index = lax.axis_index("wide")
    narrow_index = lax.axis_index("narrow")
    height, span = amplitudes.shape
    shift = span.bit_length() - 1
    here = wide_index.astype(jnp.int32).reshape(1)
    index = slab_index.reshape(2 * CHUNKS, LANES // 2)
    core = narrow_index & 1

    def step(value, dz, dc=0, turn=1):
        ring = [
            (z * 2 + c, (z + (turn if c else 1) * dz) % 8 * 2 + (c + dc) % 2)
            for z in range(8)
            for c in range(2)
        ]
        return lax.ppermute(value, "narrow", ring)

    sent = pl.pallas_call(
        lambda *refs: select_kernel(shift, *refs),
        out_shape=(
            *[jax.ShapeDtypeStruct((4 * DEPTH, height), jnp.bfloat16) for _ in HOPS],
        ),
        in_specs=[SMEM, VMEM, HBM],
        out_specs=(VMEM,) * len(HOPS),
        scratch_shapes=[pltpu.VMEM((height, span), jnp.bfloat16), pltpu.SemaphoreType.DMA(())],
        compiler_params=pltpu.CompilerParams(vmem_limit_bytes=59 << 20),
        cost_estimate=pl.CostEstimate(flops=2**30, bytes_accessed=2**21, transcendentals=0),
        name="select",
    )(here, index, amplitudes)
    came = [
        lax.ppermute(
            sent[k],
            "wide",
            [(x * 4 + y, (x + dx) % 4 * 4 + (y + dy) % 4) for x in range(4) for y in range(4)],
        )
        for k, (dx, dy) in enumerate(HOPS)
        if k
    ]

    forward, settle, stay = pl.pallas_call(
        lambda *refs: route_kernel(shift, *refs),
        out_shape=(
            jax.ShapeDtypeStruct((CHUNKS * ROOM, CHUNKS * DEPTH), jnp.bfloat16),
            jax.ShapeDtypeStruct((CHUNKS * ROOM, LANES), jnp.bfloat16),
            jax.ShapeDtypeStruct(sent[0].shape, jnp.bfloat16),
        ),
        in_specs=[SMEM, VMEM, VMEM],
        out_specs=(VMEM, VMEM, VMEM),
        compiler_params=pltpu.CompilerParams(vmem_limit_bytes=16 << 20),
        cost_estimate=pl.CostEstimate(flops=2**28, bytes_accessed=2**20, transcendentals=0),
        name="route",
    )(here, index, sent[0])

    moved = pl.pallas_call(
        forward_kernel,
        out_shape=jax.ShapeDtypeStruct((CHUNKS, ROOM, height), jnp.bfloat16),
        in_specs=[VMEM] * (len(HOPS) + 1),
        out_specs=VMEM,
        compiler_params=pltpu.CompilerParams(vmem_limit_bytes=8 << 20),
        cost_estimate=pl.CostEstimate(flops=2**28, bytes_accessed=2**20, transcendentals=0),
        name="forward",
    )(forward, stay, *came)
    second = lax.all_to_all(moved, "wide", 0, 0, tiled=True)

    slabs = CHUNKS // PER
    coded = pl.pallas_call(
        ladder_kernel,
        out_shape=jax.ShapeDtypeStruct((CHUNKS, height + CODE_ROWS, LANES), jnp.int16),
        in_specs=[VMEM, HBM, HBM],
        out_specs=HBM,
        scratch_shapes=[
            pltpu.VMEM((slabs, span, PER * LANES), jnp.bfloat16),
            pltpu.VMEM((CHUNKS, height + CODE_ROWS, LANES), jnp.int16),
            pltpu.SemaphoreType.DMA((slabs,)),
            pltpu.SemaphoreType.DMA((slabs,)),
        ],
        compiler_params=pltpu.CompilerParams(vmem_limit_bytes=50 << 20),
        cost_estimate=pl.CostEstimate(
            flops=2 * height * span * CHUNKS * LANES, bytes_accessed=18 * 2**20, transcendentals=0
        ),
        name="ladder",
    )(amplitudes, integrals, moved)
    shares = lax.all_to_all(coded, "wide", 0, 0, tiled=True)

    own = pl.pallas_call(
        settle_kernel,
        out_shape=jax.ShapeDtypeStruct((height, LANES), jnp.bfloat16),
        in_specs=[VMEM, VMEM, HBM],
        out_specs=VMEM,
        compiler_params=pltpu.CompilerParams(vmem_limit_bytes=8 << 20),
        cost_estimate=pl.CostEstimate(flops=2**26, bytes_accessed=2**20, transcendentals=0),
        name="settle",
    )(second, settle, coded)

    up, down, up2, down2 = step(own, 1), step(own, -1), step(own, 2), step(own, -2)
    up3, down3 = step(up2, 1), step(down2, -1)
    two = pl.pallas_call(
        either_kernel,
        out_shape=jax.ShapeDtypeStruct(up2.shape, jnp.bfloat16),
        in_specs=[SMEM, VMEM, VMEM],
        out_specs=VMEM,
        compiler_params=pltpu.CompilerParams(vmem_limit_bytes=4 << 20),
        cost_estimate=pl.CostEstimate(flops=0, bytes_accessed=2**18, transcendentals=0),
        name="either",
    )(core.astype(jnp.int32).reshape(1), up2, down2)
    four = step(two, 2, turn=-1)
    near = jnp.concatenate([own, up, down, up2, down2], 0)
    near_sibling = step(near, 0, 1)
    far = jnp.concatenate([up3, down3, four], 0)
    far_sibling = step(far, 0, 1)

    where = jnp.stack([narrow_index >> 1, core]).astype(jnp.int32)
    return pl.pallas_call(
        finish_kernel,
        out_shape=jax.ShapeDtypeStruct((height, LANES), jnp.float32),
        in_specs=[SMEM, VMEM, HBM, VMEM, VMEM, VMEM, VMEM, HBM, HBM],
        out_specs=VMEM,
        scratch_shapes=[
            pltpu.VMEM(shares.shape, jnp.int16),
            pltpu.VMEM(near.shape, jnp.bfloat16),
            pltpu.VMEM(far.shape, jnp.bfloat16),
            pltpu.VMEM((CHUNKS * height, LANES), jnp.bfloat16),
            pltpu.SemaphoreType.DMA((PIECES + 2,)),
        ],
        compiler_params=pltpu.CompilerParams(vmem_limit_bytes=48 << 20),
        cost_estimate=pl.CostEstimate(flops=2**30, bytes_accessed=2**23, transcendentals=0),
        name="finish",
    )(
        where,
        pair_integrals,
        shares,
        occupied_energy.reshape(height, 1),
        virtual_energy.reshape(1, LANES),
        near,
        far,
        near_sibling,
        far_sibling,
    )


def solution(mesh):
    placed = (P("narrow", "wide"), P("wide", None), P("narrow", None), P(), P("narrow"), P("wide"))
    return jax.shard_map(
        on_device, mesh=mesh, in_specs=placed, out_specs=P("narrow", "wide"), check_vma=False
    )
```

```python
import jax
import jax.numpy as jnp
from jax import lax
from jax.experimental import pallas as pl
from jax.experimental.pallas import tpu as pltpu
from jax.sharding import PartitionSpec as P

CHUNKS = 16
DEPTH = 32
HOPS = ((0, 0), (1, 0), (3, 0), (0, 1))
ROOM = 80
LANES = 256
CODE_ROWS = 16
STEPS = 256.0
TOP = 32760.0
PIECES = 4
PER = 2
VMEM = pl.BlockSpec(memory_space=pltpu.VMEM)
HBM = pl.BlockSpec(memory_space=pltpu.HBM)
SMEM = pl.BlockSpec(memory_space=pltpu.SMEM)


def iota(shape, dim):
    return lax.broadcasted_iota(jnp.int32, shape, dim)


def ones_where(mask):
    return jnp.where(mask, 1.0, 0.0)


def bdot(left, right, dims=((1,), (0,))):
    return lax.dot_general(
        left.astype(jnp.bfloat16),
        right.astype(jnp.bfloat16),
        (dims, ((), ())),
        preferred_element_type=jnp.float32,
    )


def count_before(classes):
    member = jnp.concatenate(
        [ones_where(classes[c : c + 1, :] == iota((CHUNKS, LANES), 0)) for c in range(CHUNKS)], 0
    )
    earlier = ones_where(iota((LANES, LANES), 0) < iota((LANES, LANES), 1))
    return member, bdot(member, earlier)


def pick(member, table):
    return jnp.sum((member * table).reshape(CHUNKS, CHUNKS, LANES), axis=1).astype(jnp.int32)


def rank_in_owner(owner):
    member, within = count_before(owner)
    r, c = iota((LANES, LANES), 0), iota((LANES, LANES), 1)
    ahead = ones_where(((r & 15) == (c & 15)) & (jnp.right_shift(c, 4) < jnp.right_shift(r, 4)))
    base = jnp.sum(bdot(ahead, member), axis=1, keepdims=True)
    return pick(member, within + base)


def widen(ref):
    halves = [ref[pl.ds(k, CHUNKS, stride=2), :] for k in range(2)]
    return jnp.concatenate(halves, 1)


def select_kernel(shift, here_ref, index_ref, far_amp_ref, *refs):
    *sent_refs, amp_ref, amp_sem = refs
    fetch = pltpu.make_async_copy(far_amp_ref, amp_ref, amp_sem)
    fetch.start()
    index = widen(index_ref)
    here = here_ref[0]
    owner = jnp.right_shift(index, shift)
    rank = rank_in_owner(owner)
    middle, depth = rank & 15, jnp.right_shift(rank, 4)
    column = index & ((1 << shift) - 1)
    high, low = jnp.right_shift(column, 6).astype(jnp.float32), (column & 63).astype(jnp.float32)
    lefts, rights = [], []
    for k in range(CHUNKS):
        one = slice(k, k + 1)
        hit = ones_where((depth[one] == iota((DEPTH, LANES), 0)) & (owner[one] == here))
        lefts.append(jnp.concatenate([hit * high[one], hit * low[one]], 0))
        rights.append(ones_where(middle[one] == iota((CHUNKS, LANES), 0)))
    found = bdot(jnp.concatenate(lefts, 1), jnp.concatenate(rights, 1), ((1,), (1,)))
    columns = (found[:DEPTH] * 64.0 + found[DEPTH:]).astype(jnp.int32)
    span = amp_ref.shape[1]
    lane = iota((DEPTH, span), 1)
    order = [j for hop in range(len(HOPS)) for j in range(hop, CHUNKS, len(HOPS))]
    chosen = jnp.concatenate(
        [ones_where(lane == columns[:, j : j + 1]).astype(jnp.bfloat16) for j in order], 0
    )
    fetch.wait()
    got = bdot(chosen, amp_ref[...], ((1,), (1,))).astype(jnp.bfloat16)
    for hop, sent_ref in enumerate(sent_refs):
        sent_ref[...] = got[hop * 4 * DEPTH : (hop + 1) * 4 * DEPTH]


def route_kernel(shift, here_ref, index_ref, kept_ref, *refs):
    forward_ref, settle_ref, stay_ref = refs
    stay_ref[...] = kept_ref[...]
    index, here = widen(index_ref), here_ref[0]
    owner = jnp.right_shift(index, shift)
    rank = rank_in_owner(owner)
    last, depth = rank & 15, jnp.right_shift(rank, 4)
    hop = rank & 3
    x, y = jnp.right_shift(owner, 2), owner & 3
    for k, (dx, dy) in enumerate(HOPS):
        x, y = jnp.where(hop == k, x + dx, x), jnp.where(hop == k, y + dy, y)
    middle = (x & 3) * 4 + (y & 3)
    member, within = count_before(middle)
    place = pick(member, within)
    source = (hop * (4 * DEPTH) + jnp.right_shift(last, 2) * DEPTH + depth).astype(jnp.float32)
    lane = iota((ROOM, CHUNKS * DEPTH), 1)
    for k in range(CHUNKS):
        one = slice(k, k + 1)
        hit = (place[one] == iota((ROOM, LANES), 0)) & (middle[one] == here)
        row = jnp.sum(jnp.where(hit, source[one], 0.0), axis=1, keepdims=True).astype(jnp.int32)
        forward_ref[k * ROOM : (k + 1) * ROOM, :] = ones_where(lane == row).astype(jnp.bfloat16)
    arrived = (middle * ROOM + place).astype(jnp.float32)
    own = iota((CHUNKS, LANES), 0) == here
    wanted = jnp.sum(jnp.where(own, arrived, 0.0), axis=0, keepdims=True).astype(jnp.int32)
    settle_ref[...] = ones_where(iota((CHUNKS * ROOM, LANES), 0) == wanted).astype(jnp.bfloat16)


def forward_kernel(forward_ref, *refs):
    *come_refs, moved_ref = refs
    arrived = jnp.concatenate([ref[...] for ref in come_refs], 0)
    moved = bdot(forward_ref[...], arrived).astype(jnp.bfloat16)
    moved_ref[...] = moved.reshape(moved_ref.shape)


def settle_kernel(second_ref, settle_ref, after_ref, own_ref):
    del after_ref
    arrived = second_ref[...].reshape(CHUNKS * ROOM, second_ref.shape[2])
    own_ref[...] = bdot(arrived, settle_ref[...], ((0,), (0,))).astype(jnp.bfloat16)


def ladder_kernel(amp_ref, int_ref, after_ref, coded_ref, held_ref, stage_ref, in_sems, out_sems):
    del after_ref
    count = CHUNKS // PER
    height = amp_ref.shape[0]
    width = PER * LANES
    ins, outs = [], []
    for b in range(count):
        ins.append(
            pltpu.make_async_copy(
                int_ref.at[:, pl.ds(b * width, width)], held_ref.at[b], in_sems.at[b]
            )
        )
        ins[b].start()
    for b in range(count):
        ins[b].wait()
        slab = jnp.dot(amp_ref[...], held_ref[b], preferred_element_type=jnp.float32)
        for j in range(PER):
            part = slab[:, j * LANES : (j + 1) * LANES]
            largest = jnp.max(jnp.abs(part), axis=0, keepdims=True)
            code = jnp.ceil(jnp.log2(jnp.maximum(largest, 2.0**-120)) * STEPS) + 1.0
            shrunk = part * jnp.exp2(code * (-1.0 / STEPS)) * TOP
            k = b * PER + j
            stage_ref[k, :height, :] = jnp.round(shrunk).astype(jnp.int32).astype(jnp.int16)
            stage_ref[k, height:, :] = jnp.broadcast_to(
                code.astype(jnp.int32), (CODE_ROWS, LANES)
            ).astype(jnp.int16)
        outs.append(
            pltpu.make_async_copy(
                stage_ref.at[pl.ds(b * PER, PER)],
                coded_ref.at[pl.ds(b * PER, PER)],
                out_sems.at[b],
            )
        )
        outs[b].start()
    for out in outs:
        out.wait()


def either_kernel(core_ref, zero_ref, one_ref, out_ref):
    @pl.when(core_ref[0] == 0)
    def _():
        out_ref[...] = zero_ref[...]

    @pl.when(core_ref[0] != 0)
    def _():
        out_ref[...] = one_ref[...]


def finish_kernel(
    place_ref, pair_ref, far_coded_ref, occ_ref, virt_ref, near_ref, far_ref, *refs
):
    *away_refs, out_ref, coded_ref, near_sibling_ref, far_sibling_ref, ordered_ref, sems = refs
    piece = CHUNKS // PIECES
    siblings = [
        pltpu.make_async_copy(away_refs[0], near_sibling_ref, sems.at[PIECES]),
        pltpu.make_async_copy(away_refs[1], far_sibling_ref, sems.at[PIECES + 1]),
    ]
    shares = []
    for k in range(PIECES):
        some = pl.ds(k * piece, piece)
        shares.append(
            pltpu.make_async_copy(far_coded_ref.at[some], coded_ref.at[some], sems.at[k])
        )
    for copy in siblings + shares:
        copy.start()
    z, core = place_ref[0], place_ref[1]
    rows = out_ref.shape[0]
    chips = (0, 1, -1, 2, -2, 3, -3, 4)
    slot = 0
    for group_ref in (near_ref, far_ref, near_sibling_ref, far_sibling_ref):
        if group_ref is near_sibling_ref:
            for copy in siblings:
                copy.wait()
        for k in range(group_ref.shape[0] // rows):
            which = core if slot < len(chips) else 1 - core
            n = jnp.bitwise_and(z - chips[slot % len(chips)] + 8, 7) * 2 + which
            held = pl.ds(pl.multiple_of(n * rows, rows), rows)
            ordered_ref[held, :] = group_ref[k * rows : (k + 1) * rows, :]
            slot += 1
    hole = jnp.dot(pair_ref[...], ordered_ref[...], preferred_element_type=jnp.float32)
    total = jnp.zeros(out_ref.shape, jnp.float32)
    for k in range(CHUNKS):
        if k % piece == 0:
            shares[k // piece].wait()
        code = coded_ref[k, rows:, :].astype(jnp.int32).astype(jnp.float32)[:1, :]
        values = coded_ref[k, :rows, :].astype(jnp.int32).astype(jnp.float32)
        total = total + values * jnp.exp2(code * (1.0 / STEPS))
    out_ref[...] = (total * (1.0 / TOP) + hole) / (virt_ref[...] - occ_ref[...])


def on_device(amplitudes, integrals, pair_integrals, slab_index, occupied_energy, virtual_energy):
    wide_index = lax.axis_index("wide")
    narrow_index = lax.axis_index("narrow")
    height, span = amplitudes.shape
    shift = span.bit_length() - 1
    here = wide_index.astype(jnp.int32).reshape(1)
    index = slab_index.reshape(2 * CHUNKS, LANES // 2)
    core = narrow_index & 1

    def step(value, dz, dc=0, turn=1):
        ring = [
            (z * 2 + c, (z + (turn if c else 1) * dz) % 8 * 2 + (c + dc) % 2)
            for z in range(8)
            for c in range(2)
        ]
        return lax.ppermute(value, "narrow", ring)

    sent = pl.pallas_call(
        lambda *refs: select_kernel(shift, *refs),
        out_shape=(
            *[jax.ShapeDtypeStruct((4 * DEPTH, height), jnp.bfloat16) for _ in HOPS],
        ),
        in_specs=[SMEM, VMEM, HBM],
        out_specs=(VMEM,) * len(HOPS),
        scratch_shapes=[pltpu.VMEM((height, span), jnp.bfloat16), pltpu.SemaphoreType.DMA(())],
        compiler_params=pltpu.CompilerParams(vmem_limit_bytes=59 << 20),
        cost_estimate=pl.CostEstimate(flops=2**30, bytes_accessed=2**21, transcendentals=0),
        name="select",
    )(here, index, amplitudes)
    came = [
        lax.ppermute(
            sent[k],
            "wide",
            [(x * 4 + y, (x + dx) % 4 * 4 + (y + dy) % 4) for x in range(4) for y in range(4)],
        )
        for k, (dx, dy) in enumerate(HOPS)
        if k
    ]

    forward, settle, stay = pl.pallas_call(
        lambda *refs: route_kernel(shift, *refs),
        out_shape=(
            jax.ShapeDtypeStruct((CHUNKS * ROOM, CHUNKS * DEPTH), jnp.bfloat16),
            jax.ShapeDtypeStruct((CHUNKS * ROOM, LANES), jnp.bfloat16),
            jax.ShapeDtypeStruct(sent[0].shape, jnp.bfloat16),
        ),
        in_specs=[SMEM, VMEM, VMEM],
        out_specs=(VMEM, VMEM, VMEM),
        compiler_params=pltpu.CompilerParams(vmem_limit_bytes=16 << 20),
        cost_estimate=pl.CostEstimate(flops=2**28, bytes_accessed=2**20, transcendentals=0),
        name="route",
    )(here, index, sent[0])

    moved = pl.pallas_call(
        forward_kernel,
        out_shape=jax.ShapeDtypeStruct((CHUNKS, ROOM, height), jnp.bfloat16),
        in_specs=[VMEM] * (len(HOPS) + 1),
        out_specs=VMEM,
        compiler_params=pltpu.CompilerParams(vmem_limit_bytes=8 << 20),
        cost_estimate=pl.CostEstimate(flops=2**28, bytes_accessed=2**20, transcendentals=0),
        name="forward",
    )(forward, stay, *came)
    second = lax.all_to_all(moved, "wide", 0, 0, tiled=True)

    slabs = CHUNKS // PER
    coded = pl.pallas_call(
        ladder_kernel,
        out_shape=jax.ShapeDtypeStruct((CHUNKS, height + CODE_ROWS, LANES), jnp.int16),
        in_specs=[VMEM, HBM, HBM],
        out_specs=HBM,
        scratch_shapes=[
            pltpu.VMEM((slabs, span, PER * LANES), jnp.bfloat16),
            pltpu.VMEM((CHUNKS, height + CODE_ROWS, LANES), jnp.int16),
            pltpu.SemaphoreType.DMA((slabs,)),
            pltpu.SemaphoreType.DMA((slabs,)),
        ],
        compiler_params=pltpu.CompilerParams(vmem_limit_bytes=50 << 20),
        cost_estimate=pl.CostEstimate(
            flops=2 * height * span * CHUNKS * LANES, bytes_accessed=18 * 2**20, transcendentals=0
        ),
        name="ladder",
    )(amplitudes, integrals, moved)
    shares = lax.all_to_all(coded, "wide", 0, 0, tiled=True)

    own = pl.pallas_call(
        settle_kernel,
        out_shape=jax.ShapeDtypeStruct((height, LANES), jnp.bfloat16),
        in_specs=[VMEM, VMEM, HBM],
        out_specs=VMEM,
        compiler_params=pltpu.CompilerParams(vmem_limit_bytes=8 << 20),
        cost_estimate=pl.CostEstimate(flops=2**26, bytes_accessed=2**20, transcendentals=0),
        name="settle",
    )(second, settle, coded)

    up, down, up2, down2 = step(own, 1), step(own, -1), step(own, 2), step(own, -2)
    up3, down3 = step(up2, 1), step(down2, -1)
    two = pl.pallas_call(
        either_kernel,
        out_shape=jax.ShapeDtypeStruct(up2.shape, jnp.bfloat16),
        in_specs=[SMEM, VMEM, VMEM],
        out_specs=VMEM,
        compiler_params=pltpu.CompilerParams(vmem_limit_bytes=4 << 20),
        cost_estimate=pl.CostEstimate(flops=0, bytes_accessed=2**18, transcendentals=0),
        name="either",
    )(core.astype(jnp.int32).reshape(1), up2, down2)
    four = step(two, 2, turn=-1)
    near = jnp.concatenate([own, up, down, up2, down2], 0)
    near_sibling = step(near, 0, 1)
    far = jnp.concatenate([up3, down3, four], 0)
    far_sibling = step(far, 0, 1)

    where = jnp.stack([narrow_index >> 1, core]).astype(jnp.int32)
    return pl.pallas_call(
        finish_kernel,
        out_shape=jax.ShapeDtypeStruct((height, LANES), jnp.float32),
        in_specs=[SMEM, VMEM, HBM, VMEM, VMEM, VMEM, VMEM, HBM, HBM],
        out_specs=VMEM,
        scratch_shapes=[
            pltpu.VMEM(shares.shape, jnp.int16),
            pltpu.VMEM(near.shape, jnp.bfloat16),
            pltpu.VMEM(far.shape, jnp.bfloat16),
            pltpu.VMEM((CHUNKS * height, LANES), jnp.bfloat16),
            pltpu.SemaphoreType.DMA((PIECES + 2,)),
        ],
        compiler_params=pltpu.CompilerParams(vmem_limit_bytes=48 << 20),
        cost_estimate=pl.CostEstimate(flops=2**30, bytes_accessed=2**23, transcendentals=0),
        name="finish",
    )(
        where,
        pair_integrals,
        shares,
        occupied_energy.reshape(height, 1),
        virtual_energy.reshape(1, LANES),
        near,
        far,
        near_sibling,
        far_sibling,
    )


def solution(mesh):
    placed = (P("narrow", "wide"), P("wide", None), P("narrow", None), P(), P("narrow"), P("wide"))
    return jax.shard_map(
        on_device, mesh=mesh, in_specs=placed, out_specs=P("narrow", "wide"), check_vma=False
    )
```

```python
import jax
import jax.numpy as jnp
from jax import lax
from jax.experimental import pallas as pl
from jax.experimental.pallas import tpu as pltpu
from jax.sharding import PartitionSpec as P

CHUNKS = 16
DEPTH = 32
HOPS = ((0, 0), (1, 0), (3, 0), (0, 1))
ROOM = 80
LANES = 256
CODE_ROWS = 16
STEPS = 256.0
TOP = 32760.0
PIECES = 2
PER = 2
VMEM = pl.BlockSpec(memory_space=pltpu.VMEM)
HBM = pl.BlockSpec(memory_space=pltpu.HBM)
SMEM = pl.BlockSpec(memory_space=pltpu.SMEM)


def iota(shape, dim):
    return lax.broadcasted_iota(jnp.int32, shape, dim)


def ones_where(mask):
    return jnp.where(mask, 1.0, 0.0)


def bdot(left, right, dims=((1,), (0,))):
    return lax.dot_general(
        left.astype(jnp.bfloat16),
        right.astype(jnp.bfloat16),
        (dims, ((), ())),
        preferred_element_type=jnp.float32,
    )


def count_before(classes):
    member = jnp.concatenate(
        [ones_where(classes[c : c + 1, :] == iota((CHUNKS, LANES), 0)) for c in range(CHUNKS)], 0
    )
    earlier = ones_where(iota((LANES, LANES), 0) < iota((LANES, LANES), 1))
    return member, bdot(member, earlier)


def pick(member, table):
    return jnp.sum((member * table).reshape(CHUNKS, CHUNKS, LANES), axis=1).astype(jnp.int32)


def rank_in_owner(owner):
    member, within = count_before(owner)
    r, c = iota((LANES, LANES), 0), iota((LANES, LANES), 1)
    ahead = ones_where(((r & 15) == (c & 15)) & (jnp.right_shift(c, 4) < jnp.right_shift(r, 4)))
    base = jnp.sum(bdot(ahead, member), axis=1, keepdims=True)
    return pick(member, within + base)


def widen(ref):
    halves = [ref[pl.ds(k, CHUNKS, stride=2), :] for k in range(2)]
    return jnp.concatenate(halves, 1)


def select_kernel(shift, here_ref, index_ref, far_amp_ref, *refs):
    *sent_refs, amp_ref, amp_sem = refs
    fetch = pltpu.make_async_copy(far_amp_ref, amp_ref, amp_sem)
    fetch.start()
    index = widen(index_ref)
    here = here_ref[0]
    owner = jnp.right_shift(index, shift)
    rank = rank_in_owner(owner)
    middle, depth = rank & 15, jnp.right_shift(rank, 4)
    column = index & ((1 << shift) - 1)
    high, low = jnp.right_shift(column, 6).astype(jnp.float32), (column & 63).astype(jnp.float32)
    lefts, rights = [], []
    for k in range(CHUNKS):
        one = slice(k, k + 1)
        hit = ones_where((depth[one] == iota((DEPTH, LANES), 0)) & (owner[one] == here))
        lefts.append(jnp.concatenate([hit * high[one], hit * low[one]], 0))
        rights.append(ones_where(middle[one] == iota((CHUNKS, LANES), 0)))
    found = bdot(jnp.concatenate(lefts, 1), jnp.concatenate(rights, 1), ((1,), (1,)))
    columns = (found[:DEPTH] * 64.0 + found[DEPTH:]).astype(jnp.int32)
    span = amp_ref.shape[1]
    lane = iota((DEPTH, span), 1)
    order = [j for hop in range(len(HOPS)) for j in range(hop, CHUNKS, len(HOPS))]
    chosen = jnp.concatenate(
        [ones_where(lane == columns[:, j : j + 1]).astype(jnp.bfloat16) for j in order], 0
    )
    fetch.wait()
    got = bdot(chosen, amp_ref[...], ((1,), (1,))).astype(jnp.bfloat16)
    for hop, sent_ref in enumerate(sent_refs):
        sent_ref[...] = got[hop * 4 * DEPTH : (hop + 1) * 4 * DEPTH]


def route_kernel(shift, here_ref, index_ref, kept_ref, *refs):
    forward_ref, settle_ref, stay_ref = refs
    stay_ref[...] = kept_ref[...]
    index, here = widen(index_ref), here_ref[0]
    owner = jnp.right_shift(index, shift)
    rank = rank_in_owner(owner)
    last, depth = rank & 15, jnp.right_shift(rank, 4)
    hop = rank & 3
    x, y = jnp.right_shift(owner, 2), owner & 3
    for k, (dx, dy) in enumerate(HOPS):
        x, y = jnp.where(hop == k, x + dx, x), jnp.where(hop == k, y + dy, y)
    middle = (x & 3) * 4 + (y & 3)
    member, within = count_before(middle)
    place = pick(member, within)
    source = (hop * (4 * DEPTH) + jnp.right_shift(last, 2) * DEPTH + depth).astype(jnp.float32)
    lane = iota((ROOM, CHUNKS * DEPTH), 1)
    for k in range(CHUNKS):
        one = slice(k, k + 1)
        hit = (place[one] == iota((ROOM, LANES), 0)) & (middle[one] == here)
        row = jnp.sum(jnp.where(hit, source[one], 0.0), axis=1, keepdims=True).astype(jnp.int32)
        forward_ref[k * ROOM : (k + 1) * ROOM, :] = ones_where(lane == row).astype(jnp.bfloat16)
    arrived = (middle * ROOM + place).astype(jnp.float32)
    own = iota((CHUNKS, LANES), 0) == here
    wanted = jnp.sum(jnp.where(own, arrived, 0.0), axis=0, keepdims=True).astype(jnp.int32)
    settle_ref[...] = ones_where(iota((CHUNKS * ROOM, LANES), 0) == wanted).astype(jnp.bfloat16)


def forward_kernel(forward_ref, *refs):
    *come_refs, far_moved_ref, moved_ref, sems = refs
    arrived = jnp.concatenate([ref[...] for ref in come_refs], 0)
    half = CHUNKS // 2
    copies = []
    for k in range(2):
        moved = bdot(forward_ref[k * half * ROOM : (k + 1) * half * ROOM, :], arrived)
        some = pl.ds(k * half, half)
        moved_ref[some] = moved.astype(jnp.bfloat16).reshape(half, ROOM, moved.shape[1])
        copies.append(
            pltpu.make_async_copy(moved_ref.at[some], far_moved_ref.at[some], sems.at[k])
        )
        copies[k].start()
    for copy in copies:
        copy.wait()


def settle_kernel(second_ref, settle_ref, after_ref, own_ref):
    del after_ref
    arrived = second_ref[...].reshape(CHUNKS * ROOM, second_ref.shape[2])
    own_ref[...] = bdot(arrived, settle_ref[...], ((0,), (0,))).astype(jnp.bfloat16)


def ladder_kernel(amp_ref, int_ref, after_ref, coded_ref, held_ref, stage_ref, in_sems, out_sems):
    del after_ref
    count = CHUNKS // PER
    height = amp_ref.shape[0]
    width = PER * LANES
    ins, outs = [], []
    for b in range(count):
        ins.append(
            pltpu.make_async_copy(
                int_ref.at[:, pl.ds(b * width, width)], held_ref.at[b], in_sems.at[b]
            )
        )
        ins[b].start()
    for b in range(count):
        ins[b].wait()
        slab = jnp.dot(amp_ref[...], held_ref[b], preferred_element_type=jnp.float32)
        for j in range(PER):
            part = slab[:, j * LANES : (j + 1) * LANES]
            largest = jnp.max(jnp.abs(part), axis=0, keepdims=True)
            code = jnp.ceil(jnp.log2(jnp.maximum(largest, 2.0**-120)) * STEPS) + 1.0
            shrunk = part * jnp.exp2(code * (-1.0 / STEPS)) * TOP
            k = b * PER + j
            stage_ref[k, :height, :] = jnp.round(shrunk).astype(jnp.int32).astype(jnp.int16)
            stage_ref[k, height:, :] = jnp.broadcast_to(
                code.astype(jnp.int32), (CODE_ROWS, LANES)
            ).astype(jnp.int16)
        outs.append(
            pltpu.make_async_copy(
                stage_ref.at[pl.ds(b * PER, PER)],
                coded_ref.at[pl.ds(b * PER, PER)],
                out_sems.at[b],
            )
        )
        outs[b].start()
    for out in outs:
        out.wait()


def either_kernel(core_ref, zero_ref, one_ref, out_ref):
    @pl.when(core_ref[0] == 0)
    def _():
        out_ref[...] = zero_ref[...]

    @pl.when(core_ref[0] != 0)
    def _():
        out_ref[...] = one_ref[...]


def finish_kernel(
    place_ref, pair_ref, far_coded_ref, occ_ref, virt_ref, near_ref, far_ref, *refs
):
    *away_refs, out_ref, coded_ref, near_sibling_ref, far_sibling_ref, ordered_ref, sems = refs
    piece = CHUNKS // PIECES
    siblings = [
        pltpu.make_async_copy(away_refs[0], near_sibling_ref, sems.at[PIECES]),
        pltpu.make_async_copy(away_refs[1], far_sibling_ref, sems.at[PIECES + 1]),
    ]
    shares = []
    for k in range(PIECES):
        some = pl.ds(k * piece, piece)
        shares.append(
            pltpu.make_async_copy(far_coded_ref.at[some], coded_ref.at[some], sems.at[k])
        )
    for copy in siblings + shares:
        copy.start()
    z, core = place_ref[0], place_ref[1]
    rows = out_ref.shape[0]
    chips = (0, 1, -1, 2, -2, 3, -3, 4)
    slot = 0
    for group_ref in (near_ref, far_ref, near_sibling_ref, far_sibling_ref):
        if group_ref is near_sibling_ref:
            for copy in siblings:
                copy.wait()
        for k in range(group_ref.shape[0] // rows):
            which = core if slot < len(chips) else 1 - core
            n = jnp.bitwise_and(z - chips[slot % len(chips)] + 8, 7) * 2 + which
            held = pl.ds(pl.multiple_of(n * rows, rows), rows)
            ordered_ref[held, :] = group_ref[k * rows : (k + 1) * rows, :]
            slot += 1
    hole = jnp.dot(pair_ref[...], ordered_ref[...], preferred_element_type=jnp.float32)
    total = jnp.zeros(out_ref.shape, jnp.float32)
    for k in range(CHUNKS):
        if k % piece == 0:
            shares[k // piece].wait()
        code = coded_ref[k, rows:, :].astype(jnp.int32).astype(jnp.float32)[:1, :]
        values = coded_ref[k, :rows, :].astype(jnp.int32).astype(jnp.float32)
        total = total + values * jnp.exp2(code * (1.0 / STEPS))
    out_ref[...] = (total * (1.0 / TOP) + hole) / (virt_ref[...] - occ_ref[...])


def on_device(amplitudes, integrals, pair_integrals, slab_index, occupied_energy, virtual_energy):
    wide_index = lax.axis_index("wide")
    narrow_index = lax.axis_index("narrow")
    height, span = amplitudes.shape
    shift = span.bit_length() - 1
    here = wide_index.astype(jnp.int32).reshape(1)
    index = slab_index.reshape(2 * CHUNKS, LANES // 2)
    core = narrow_index & 1

    def step(value, dz, dc=0, turn=1):
        ring = [
            (z * 2 + c, (z + (turn if c else 1) * dz) % 8 * 2 + (c + dc) % 2)
            for z in range(8)
            for c in range(2)
        ]
        return lax.ppermute(value, "narrow", ring)

    sent = pl.pallas_call(
        lambda *refs: select_kernel(shift, *refs),
        out_shape=(
            *[jax.ShapeDtypeStruct((4 * DEPTH, height), jnp.bfloat16) for _ in HOPS],
        ),
        in_specs=[SMEM, VMEM, HBM],
        out_specs=(VMEM,) * len(HOPS),
        scratch_shapes=[pltpu.VMEM((height, span), jnp.bfloat16), pltpu.SemaphoreType.DMA(())],
        compiler_params=pltpu.CompilerParams(vmem_limit_bytes=59 << 20),
        cost_estimate=pl.CostEstimate(flops=2**30, bytes_accessed=2**21, transcendentals=0),
        name="select",
    )(here, index, amplitudes)
    came = [
        lax.ppermute(
            sent[k],
            "wide",
            [(x * 4 + y, (x + dx) % 4 * 4 + (y + dy) % 4) for x in range(4) for y in range(4)],
        )
        for k, (dx, dy) in enumerate(HOPS)
        if k
    ]

    forward, settle, stay = pl.pallas_call(
        lambda *refs: route_kernel(shift, *refs),
        out_shape=(
            jax.ShapeDtypeStruct((CHUNKS * ROOM, CHUNKS * DEPTH), jnp.bfloat16),
            jax.ShapeDtypeStruct((CHUNKS * ROOM, LANES), jnp.bfloat16),
            jax.ShapeDtypeStruct(sent[0].shape, jnp.bfloat16),
        ),
        in_specs=[SMEM, VMEM, VMEM],
        out_specs=(VMEM, VMEM, VMEM),
        compiler_params=pltpu.CompilerParams(vmem_limit_bytes=16 << 20),
        cost_estimate=pl.CostEstimate(flops=2**28, bytes_accessed=2**20, transcendentals=0),
        name="route",
    )(here, index, sent[0])

    moved = pl.pallas_call(
        forward_kernel,
        out_shape=jax.ShapeDtypeStruct((CHUNKS, ROOM, height), jnp.bfloat16),
        in_specs=[VMEM] * (len(HOPS) + 1),
        out_specs=HBM,
        scratch_shapes=[
            pltpu.VMEM((CHUNKS, ROOM, height), jnp.bfloat16),
            pltpu.SemaphoreType.DMA((2,)),
        ],
        compiler_params=pltpu.CompilerParams(vmem_limit_bytes=8 << 20),
        cost_estimate=pl.CostEstimate(flops=2**28, bytes_accessed=2**20, transcendentals=0),
        name="forward",
    )(forward, stay, *came)
    second = lax.all_to_all(moved, "wide", 0, 0, tiled=True)

    slabs = CHUNKS // PER
    coded = pl.pallas_call(
        ladder_kernel,
        out_shape=jax.ShapeDtypeStruct((CHUNKS, height + CODE_ROWS, LANES), jnp.int16),
        in_specs=[VMEM, HBM, HBM],
        out_specs=HBM,
        scratch_shapes=[
            pltpu.VMEM((slabs, span, PER * LANES), jnp.bfloat16),
            pltpu.VMEM((CHUNKS, height + CODE_ROWS, LANES), jnp.int16),
            pltpu.SemaphoreType.DMA((slabs,)),
            pltpu.SemaphoreType.DMA((slabs,)),
        ],
        compiler_params=pltpu.CompilerParams(vmem_limit_bytes=50 << 20),
        cost_estimate=pl.CostEstimate(
            flops=2 * height * span * CHUNKS * LANES, bytes_accessed=18 * 2**20, transcendentals=0
        ),
        name="ladder",
    )(amplitudes, integrals, moved)
    shares = lax.all_to_all(coded, "wide", 0, 0, tiled=True)

    own = pl.pallas_call(
        settle_kernel,
        out_shape=jax.ShapeDtypeStruct((height, LANES), jnp.bfloat16),
        in_specs=[VMEM, VMEM, HBM],
        out_specs=VMEM,
        compiler_params=pltpu.CompilerParams(vmem_limit_bytes=8 << 20),
        cost_estimate=pl.CostEstimate(flops=2**26, bytes_accessed=2**20, transcendentals=0),
        name="settle",
    )(second, settle, coded)

    up, down, up2, down2 = step(own, 1), step(own, -1), step(own, 2), step(own, -2)
    up3, down3 = step(up2, 1), step(down2, -1)
    two = pl.pallas_call(
        either_kernel,
        out_shape=jax.ShapeDtypeStruct(up2.shape, jnp.bfloat16),
        in_specs=[SMEM, VMEM, VMEM],
        out_specs=VMEM,
        compiler_params=pltpu.CompilerParams(vmem_limit_bytes=4 << 20),
        cost_estimate=pl.CostEstimate(flops=0, bytes_accessed=2**18, transcendentals=0),
        name="either",
    )(core.astype(jnp.int32).reshape(1), up2, down2)
    four = step(two, 2, turn=-1)
    near = jnp.concatenate([own, up, down, up2, down2], 0)
    near_sibling = step(near, 0, 1)
    far = jnp.concatenate([up3, down3, four], 0)
    far_sibling = step(far, 0, 1)

    where = jnp.stack([narrow_index >> 1, core]).astype(jnp.int32)
    return pl.pallas_call(
        finish_kernel,
        out_shape=jax.ShapeDtypeStruct((height, LANES), jnp.float32),
        in_specs=[SMEM, VMEM, HBM, VMEM, VMEM, VMEM, VMEM, HBM, HBM],
        out_specs=VMEM,
        scratch_shapes=[
            pltpu.VMEM(shares.shape, jnp.int16),
            pltpu.VMEM(near.shape, jnp.bfloat16),
            pltpu.VMEM(far.shape, jnp.bfloat16),
            pltpu.VMEM((CHUNKS * height, LANES), jnp.bfloat16),
            pltpu.SemaphoreType.DMA((PIECES + 2,)),
        ],
        compiler_params=pltpu.CompilerParams(vmem_limit_bytes=48 << 20),
        cost_estimate=pl.CostEstimate(flops=2**30, bytes_accessed=2**23, transcendentals=0),
        name="finish",
    )(
        where,
        pair_integrals,
        shares,
        occupied_energy.reshape(height, 1),
        virtual_energy.reshape(1, LANES),
        near,
        far,
        near_sibling,
        far_sibling,
    )


def solution(mesh):
    placed = (P("narrow", "wide"), P("wide", None), P("narrow", None), P(), P("narrow"), P("wide"))
    return jax.shard_map(
        on_device, mesh=mesh, in_specs=placed, out_specs=P("narrow", "wide"), check_vma=False
    )
```
